1024 devices in a mesh: depth: 64 (over y, x), lat: 16 (over z, core).
Axes of the slice: x: 8, y: 8, z: 8, core: 2. Of those that a mesh axis runs over, the one named last changes fastest.
Arguments:
- thermal_values: float32 [4096, 128, 128], P('depth', 'lat'), may hold values from 0 to 1
- reactant_fraction: float32 [4096, 128, 128], P('depth', 'lat'), may hold values from 0 to 1
- active_sheet_number: int32 [64], P('depth'), may hold values from 1 to 64, 2048 in all
- colour_lookup_library: bfloat16 [8, 4, 128], replicated, may hold values from 0 to 1
- colour_lookup_choice: int32 [4], replicated, may hold values from 0 to 7
- camera_direction: int32 [4], replicated, may hold values from 0 to 1
Outputs:
- temperature_next: float32 [4096, 128, 128], P('depth', 'lat')
- fuel_next: float32 [4096, 128, 128], P('depth', 'lat')
- image: float32 [4, 4, 16, 1024], P(None, None, 'lat', 'depth')
The draws below stay inside these ranges and needn't reach their ends.
Inputs may be any that keep to these rules, and one draw needn't show every extreme that they name: `active_sheet_number`: the live layers of all blocks sum to 2048; some block has exactly 64.
All inputs are finite; a program needn't handle non-finite values.
Results may differ from the reference program's by a relative error of at most 0.0003.
Values sent between devices are 32-bit elements; how exact they have to be, the bound alone decides.
No kernel may reach another device: no remote copies, remote signals or barrier semaphores. Data moves between devices by JAX's collectives and lax.ppermute only.
A program may use at most 32 MiB of HBM per device.

```python
import math
import jax
import jax.numpy as jnp
import numpy as np
from jax import lax

LX = 8
MEAN_DEPTH = 32
SHEET_PLACES = 64
STEPS = 2
NTF = 4
NBINS = 128
NTAB = 8
MESH_HEIGHT = 128
MESH_WIDTH = 128
ALL_SHEET_PLACES = 4096
N_DEPTH = 64
N_LAT = 16


def set_ends(values, stream_key, smallest, high):
    shape = values.shape
    spot = [jax.random.randint(jax.random.fold_in(stream_key, axis), (), 0, shape[axis]) for axis in range(len(shape))]
    values = values.at[tuple(spot)].set(smallest)
    longest = shape.index(max(shape))
    spot[longest] = (spot[longest] + 1) % shape[longest]
    return values.at[tuple(spot)].set(high)


def levels(key, dims, split, least, top_value):
    level = 1.0
    for axis_at, shards_of in split:
        draws = jax.random.uniform(jax.random.fold_in(jax.random.fold_in(key, 6), axis_at), (shards_of,), jnp.float32, least / len(split), top_value / len(split))
        level = level * jnp.repeat(jnp.exp(draws), dims[axis_at] // shards_of).reshape((-1,) + (1,) * (len(dims) - 1 - axis_at))
    return level


def split_up(count, total, most, lean):
    loads = [(1 << 20) // math.isqrt(standing ** lean) + 1 for standing in range(2, count + 1)]
    spare, given = total - most - (count - 1), [1] * (count - 1)
    while spare > 0:
        free = [i for i in range(count - 1) if given[i] < most]
        whole, remaining = sum([loads[i] for i in free]), spare
        for i in free:
            extra = min(most - given[i], max(1, remaining * loads[i] // whole), spare)
            given[i] = given[i] + extra
            spare = spare - extra
    return np.array([most] + given)


def ragged_sizes(key, number_of, total, limit, skew):
    if number_of == 2:
        one = jax.random.randint(key, (), max(1, total - limit), min(limit, total - 1) + 1)
        return jnp.stack([one, total - one])
    tallies = jnp.asarray(split_up(number_of, total, limit, skew), jnp.int32)
    pairs = (number_of - 1) // 2
    source_of, sink = tallies[1:1 + 2 * pairs:2], tallies[2:2 + 2 * pairs:2]
    room = jnp.minimum(source_of - 1, limit - sink)
    moved = jax.random.randint(jax.random.fold_in(key, 1), (pairs,), 0, 1 << 20) % (room + 1)
    tallies = tallies.at[1:1 + 2 * pairs:2].set(source_of - moved).at[2:2 + 2 * pairs:2].set(sink + moved)
    return tallies[jax.random.permutation(jax.random.fold_in(key, 2), number_of)]


def setup_inputs(seed: int = 0) -> dict:
    arg_keys = jax.random.split(jax.random.key(seed), 7)
    return {
        "thermal_values": jnp.clip(1.0 * jax.random.uniform(arg_keys[0], (ALL_SHEET_PLACES, MESH_HEIGHT, MESH_WIDTH), jnp.float32) ** levels(arg_keys[0], (ALL_SHEET_PLACES, MESH_HEIGHT, MESH_WIDTH), ((0, 64), (1, 16)), -0.2, 0.2), 0.0, 1.0),
        "reactant_fraction": jnp.clip(1.0 * jax.random.uniform(arg_keys[1], (ALL_SHEET_PLACES, MESH_HEIGHT, MESH_WIDTH), jnp.float32) ** levels(arg_keys[1], (ALL_SHEET_PLACES, MESH_HEIGHT, MESH_WIDTH), ((0, 64), (1, 16)), -0.2, 0.2), 0.0, 1.0),
        "active_sheet_number": ragged_sizes(arg_keys[2], N_DEPTH, MEAN_DEPTH * N_DEPTH, SHEET_PLACES, 2).astype(jnp.int32),
        "colour_lookup_library": jnp.clip(jax.random.uniform(arg_keys[3], (NTAB, 4, NBINS), jnp.float32, 0.0, 1.0), 0.0, 1.0).astype(jnp.bfloat16),
        "colour_lookup_choice": set_ends(jax.random.randint(arg_keys[4], (NTF,), 0, NTAB), jax.random.fold_in(arg_keys[4], 1), 0, NTAB - 1).astype(jnp.int32),
        "camera_direction": set_ends(jax.random.randint(arg_keys[5], (NTF,), 0, 2), jax.random.fold_in(arg_keys[5], 1), 0, 1).astype(jnp.int32),
    }


time_step = 0.03
heat_release = 2.0
zeldovich = 8.0
expansion = 0.8


def update_fields(solution_snapshot, neighbours, active_flags):
    heat_field = solution_snapshot[0]
    fuel_field = solution_snapshot[1]
    local_coef = 1.0 + 3.0 * heat_field
    heat_flux = jnp.zeros_like(heat_field)
    fuel_flux = jnp.zeros_like(fuel_field)
    for neighbour in neighbours:
        face_coef = 0.5 * (local_coef + 1.0 + 3.0 * neighbour[0])
        heat_flux = heat_flux + face_coef * (neighbour[0] - heat_field)
        fuel_flux = fuel_flux + 0.5 * face_coef * (neighbour[1] - fuel_field)
    shifted = heat_field - 1.0
    reaction = fuel_field * jnp.exp(zeldovich * shifted / (1.0 + expansion * shifted))
    new_heat = heat_field + time_step * (heat_flux + heat_release * reaction)
    new_fuel = fuel_field + time_step * (fuel_flux - reaction)
    return jnp.where(active_flags, jnp.stack([new_heat, new_fuel]), 0.0)


def advance_block(heat_block, fuel_block, below_rim, above_rim, depth_count):
    solution_snapshot = jnp.stack([heat_block, fuel_block])
    active_flags = (jnp.arange(SHEET_PLACES) < depth_count)[None, :, None, None]
    zero_index = jnp.zeros((), jnp.int32)
    extended = jnp.concatenate([below_rim[:, None], solution_snapshot, jnp.zeros_like(below_rim)[:, None]], axis=1)
    extended = lax.dynamic_update_slice(extended, above_rim[:, None], (zero_index, (depth_count + 1).astype(jnp.int32), zero_index, zero_index))
    row_padded = jnp.pad(solution_snapshot, ((0, 0), (0, 0), (1, 1), (0, 0)))
    column_padded = jnp.pad(solution_snapshot, ((0, 0), (0, 0), (0, 0), (1, 1)))
    neighbours = [extended[:, :-2], extended[:, 2:], row_padded[:, :, :-2], row_padded[:, :, 2:],
                  column_padded[..., :-2], column_padded[..., 2:]]
    result = update_fields(solution_snapshot, neighbours, active_flags)
    return result[0], result[1]


def composite_over(front_image, back_image, channel_axis):
    opacity = lax.slice_in_dim(front_image, 3, 4, axis=channel_axis)
    return front_image + (1.0 - opacity) * back_image


def interpolate(one_table, scalar):
    position = jnp.clip(scalar, 0.0, 1.0) * (NBINS - 1)
    lower_bin = jnp.minimum(jnp.floor(position), NBINS - 2)
    fraction = position - lower_bin
    bin_index = lower_bin.astype(jnp.int32)
    low_value = one_table[:, bin_index]
    high_value = one_table[:, bin_index + 1]
    return low_value + fraction[None] * (high_value - low_value)


def reference(thermal_values, reactant_fraction, active_sheet_number, colour_lookup_library, colour_lookup_choice, camera_direction):
    thermal_piece_pile = thermal_values.reshape(N_DEPTH, SHEET_PLACES, MESH_HEIGHT, MESH_WIDTH)
    fuel_blocks = reactant_fraction.reshape(N_DEPTH, SHEET_PLACES, MESH_HEIGHT, MESH_WIDTH)
    active_flags = (jnp.arange(SHEET_PLACES)[None, :] < active_sheet_number[:, None])[:, :, None, None]
    thermal_piece_pile = jnp.where(active_flags, thermal_piece_pile, 0.0)
    fuel_blocks = jnp.where(active_flags, fuel_blocks, 0.0)
    last_index = (active_sheet_number - 1).astype(jnp.int32)[:, None, None, None]
    for repeat in range(STEPS):
        last_heat = jnp.take_along_axis(thermal_piece_pile, last_index, axis=1)[:, 0]
        last_fuel = jnp.take_along_axis(fuel_blocks, last_index, axis=1)[:, 0]
        last_layer = jnp.stack([last_heat, last_fuel], axis=1)
        first_layer = jnp.stack([thermal_piece_pile[:, 0], fuel_blocks[:, 0]], axis=1)
        zeros_rim = jnp.zeros_like(first_layer[:1])
        below_rims = jnp.concatenate([zeros_rim, last_layer[:-1]], axis=0)
        above_rims = jnp.concatenate([first_layer[1:], zeros_rim], axis=0)
        thermal_piece_pile, fuel_blocks = lax.map(lambda block_item: advance_block(*block_item),
                                           (thermal_piece_pile, fuel_blocks, below_rims, above_rims, active_sheet_number))
    tables = colour_lookup_library[colour_lookup_choice].astype(jnp.float32)
    per_cell = 3.0 / (MEAN_DEPTH * N_DEPTH)
    backward = (camera_direction == 1)

    def render_block(accumulated, block_item):
        heat_block, fuel_block, depth_count = block_item
        block_alive = (jnp.arange(SHEET_PLACES) < depth_count)[None, :, None, None]
        values = jnp.stack([interpolate(tables[tf_number], heat_block if tf_number < 2 else fuel_block)
                            for tf_number in range(NTF)])
        optical = jnp.where(block_alive, values[:, 3] * per_cell, 0.0)
        inclusive = jnp.cumsum(optical, axis=1)
        column_sum = inclusive[:, -1]
        preceding = jnp.where(backward[:, None, None, None], column_sum[:, None] - inclusive, inclusive - optical)
        weight = jnp.exp(-preceding) * (1.0 - jnp.exp(-optical))
        colour_sum = jnp.sum(weight[:, None] * values[:, :3], axis=2)
        opacity = 1.0 - jnp.exp(-column_sum)
        new_image = jnp.concatenate([colour_sum, opacity[:, None]], axis=1)
        merged = jnp.where(backward[:, None, None, None], composite_over(new_image, accumulated, 1),
                           composite_over(accumulated, new_image, 1))
        return merged, None

    start_image = jnp.zeros((NTF, 4, MESH_HEIGHT, MESH_WIDTH), jnp.float32)
    image, unused = lax.scan(render_block, start_image, (thermal_piece_pile, fuel_blocks, active_sheet_number))
    image = image.reshape(NTF, 4, N_LAT, LX * MESH_WIDTH)
    return (thermal_piece_pile.reshape(N_DEPTH * SHEET_PLACES, MESH_HEIGHT, MESH_WIDTH), fuel_blocks.reshape(N_DEPTH * SHEET_PLACES, MESH_HEIGHT, MESH_WIDTH), image)
```

```python
import functools

import jax
import jax.numpy as jnp
from jax import lax
from jax.experimental import pallas as pl
from jax.experimental.pallas import tpu as pltpu
from jax.sharding import PartitionSpec as P

MEAN_DEPTH = 32
STEPS = 2

time_step = 0.03
heat_release = 2.0
zeldovich = 8.0
expansion = 0.8

VMEM = pltpu.VMEM
SMEM = pltpu.SMEM
F32 = jnp.float32


def in_vmem():
    return pl.BlockSpec(memory_space=VMEM)


def in_smem():
    return pl.BlockSpec(memory_space=SMEM)


def pack_rows(meta, theta, fuel, low_rows, high_rows, last_layer, first_layer):
    depth_count = meta[0]
    for number, field in enumerate((theta, fuel)):
        for row in range(2):
            low_rows[2 * number + row] = field[:, row, :]
            high_rows[2 * number + row] = field[:, 6 + row, :]
        last_layer[number] = field[depth_count - 1]
        first_layer[number] = field[0]


def pack_rims(
    meta, theta, fuel, rows_below, rows_above, upward, downward
):
    depth_count = meta[0]
    last = depth_count - 1
    second_last = jnp.maximum(depth_count - 2, 0)
    second = jnp.minimum(1, last)
    size = jnp.full((1, 128), depth_count.astype(F32))
    for number, field in enumerate((theta, fuel)):
        upward[number, 0] = field[last]
        upward[number, 1] = field[second_last]
        upward[number, 2, 0:1] = rows_below[2 * number + 1, pl.ds(last, 1), :]
        upward[number, 2, 1:2] = rows_above[2 * number, pl.ds(last, 1), :]
        upward[number, 2, 2:3] = size
        upward[number, 2, 3:8] = jnp.zeros((5, 128), F32)
        downward[number, 0] = field[0]
        downward[number, 1] = field[second]
        downward[number, 2, 0:1] = rows_below[2 * number + 1, 0:1, :]
        downward[number, 2, 1:2] = rows_above[2 * number, 0:1, :]
        downward[number, 2, 2:3] = size
        downward[number, 2, 3:8] = jnp.zeros((5, 128), F32)


def lanes():
    return lax.broadcasted_iota(jnp.int32, (8, 128), 1)


def sublanes():
    return lax.broadcasted_iota(jnp.int32, (8, 128), 0)


def left_of(x):
    return jnp.where(lanes() == 0, 0.0, pltpu.roll(x, 1, 1))


def right_of(x):
    return jnp.where(lanes() == 127, 0.0, pltpu.roll(x, 127, 1))


def row_below(x, halo_row):
    return jnp.where(sublanes() == 0, jnp.broadcast_to(halo_row, (8, 128)), pltpu.roll(x, 1, 0))


def row_above(x, halo_row):
    return jnp.where(sublanes() == 7, jnp.broadcast_to(halo_row, (8, 128)), pltpu.roll(x, 7, 0))


def stepped(heat, fuel, neighbours):
    heat_sum = neighbours[0][0]
    fuel_sum = neighbours[0][1]
    product_sum = neighbours[0][0] * neighbours[0][1]
    square_sum = neighbours[0][0] * neighbours[0][0]
    for heat_n, fuel_n in neighbours[1:]:
        heat_sum = heat_sum + heat_n
        fuel_sum = fuel_sum + fuel_n
        product_sum = product_sum + heat_n * fuel_n
        square_sum = square_sum + heat_n * heat_n
    heat_flux = (heat_sum - 6.0 * heat) + 1.5 * (square_sum - 6.0 * (heat * heat))
    fuel_flux = 0.5 * (
        (1.0 + 1.5 * heat) * (fuel_sum - 6.0 * fuel) + 1.5 * (product_sum - fuel * heat_sum)
    )
    ratio = zeldovich / expansion
    reaction = fuel * jnp.exp(ratio - ratio / ((1.0 - expansion) + expansion * heat))
    return (
        heat + time_step * (heat_flux + heat_release * reaction),
        fuel + time_step * (fuel_flux - reaction),
    )


def advance_and_render(
    places,
    functions,
    meta,
    choice,
    camera,
    theta,
    fuel,
    library,
    own_low,
    own_high,
    rows_below,
    rows_above,
    from_below,
    from_above,
    from_below_2,
    from_above_2,
    theta_next,
    fuel_next,
    image,
    field0,
    field1,
    edge0,
    edge1,
    tables,
    low_table,
    rise_table,
    copies,
):
    depth_count = meta[0]
    lat_index = meta[1]
    lat_count = meta[2]
    bins = library.shape[2]
    fetch = [
        pltpu.make_async_copy(source, field0.at[number, pl.ds(2, places)], copies.at[number])
        for number, source in enumerate((theta, fuel))
    ]
    for copy in fetch:
        copy.start()

    tables[...] = library[...].astype(F32)
    per_cell = 3.0 / meta[3].astype(F32)
    for f in range(functions):
        sign = jnp.where(camera[f] == 0, -per_cell, per_cell)
        for c in range(4):
            low = jnp.broadcast_to(tables[choice[f], c : c + 1, :], (8, bins))
            rise = pltpu.roll(low, bins - 1, 1) - low
            if c == 3:
                low = low * sign
                rise = rise * sign
            low_table[4 * f + c] = low
            rise_table[4 * f + c] = rise

    lead = 8
    for number in range(2):
        for row in range(2):
            edge0[number, row, lead : lead + places] = rows_below[2 * number + row]
            edge0[number, 2 + row, lead : lead + places] = rows_above[2 * number + row]
        edge0[number, 1, lead - 1 : lead] = from_below[number, 2, 0:1]
        edge0[number, 2, lead - 1 : lead] = from_below[number, 2, 1:2]
        edge0[number, 1, pl.ds(lead + depth_count, 1)] = from_above[number, 2, 0:1]
        edge0[number, 2, pl.ds(lead + depth_count, 1)] = from_above[number, 2, 1:2]

    for copy in fetch:
        copy.wait()
    below_size = jnp.broadcast_to(from_below[0, 2, 2:3], (8, 128))
    above_size = jnp.broadcast_to(from_above[0, 2, 2:3], (8, 128))
    for number in range(2):
        field0[number, 0] = jnp.where(below_size == 1.0, from_below_2[number], from_below[number, 1])
        field0[number, 1] = from_below[number, 0]
        field0[number, depth_count + 2] = from_above[number, 0]
        field0[number, depth_count + 3] = jnp.where(
            above_size == 1.0, from_above_2[number], from_above[number, 1]
        )

    for block in range(places // 8):
        at = lead + 8 * block
        for side in range(2):
            edge_row = 1 + side
            outer_row = 3 * side
            inner = (own_low, own_high)[side]
            heat = edge0[0, edge_row, at : at + 8]
            burn = edge0[1, edge_row, at : at + 8]
            around = []
            for shift in (-1, 1):
                around.append(
                    tuple(edge0[n, edge_row, at + shift : at + shift + 8] for n in range(2))
                )
            around.append(tuple(edge0[n, outer_row, at : at + 8] for n in range(2)))
            around.append(
                tuple(inner[2 * n + side, 8 * block : 8 * block + 8] for n in range(2))
            )
            around.append((left_of(heat), left_of(burn)))
            around.append((right_of(heat), right_of(burn)))
            new_heat, new_burn = stepped(heat, burn, around)
            outside = (lat_index == 0) if side == 0 else (lat_index == lat_count - 1)
            edge1[0, side, 8 * block : 8 * block + 8] = jnp.where(outside, 0.0, new_heat)
            edge1[1, side, 8 * block : 8 * block + 8] = jnp.where(outside, 0.0, new_burn)

    def block_step(field, at, count, edge_rows):
        heat = [field[0, at - 1 + j] for j in range(count + 2)]
        burn = [field[1, at - 1 + j] for j in range(count + 2)]
        results = []
        for j in range(1, count + 1):
            h, b = heat[j], burn[j]
            (h_low, b_low), (h_high, b_high) = edge_rows(j - 1)
            around = [
                (heat[j - 1], burn[j - 1]),
                (heat[j + 1], burn[j + 1]),
                (row_below(h, h_low), row_below(b, b_low)),
                (row_above(h, h_high), row_above(b, b_high)),
                (left_of(h), left_of(b)),
                (right_of(h), right_of(b)),
            ]
            results.append(stepped(h, b, around))
        return results

    unroll = 6

    def first_step(block, carry):
        start = block * unroll

        def edge_rows(j):
            place = lead - 1 + start + j
            return [
                tuple(edge0[n, 1 + side, pl.ds(place, 1), :] for n in range(2)) for side in range(2)
            ]

        for j, (h, b) in enumerate(block_step(field0, start + 1, unroll, edge_rows)):
            field1[0, start + j] = h
            field1[1, start + j] = b
        return carry

    lax.fori_loop(0, (places + 2) // unroll, first_step, 0)
    for number in range(2):
        field1[number, 0] = jnp.where(below_size > 0.0, field1[number, 0], 0.0)
        field1[number, depth_count + 1] = jnp.where(
            above_size > 0.0, field1[number, depth_count + 1], 0.0
        )

    unroll_2 = 4

    def second_step(block, carry):
        start = block * unroll_2

        def edge_rows(j):
            return [
                tuple(edge1[n, side, pl.ds(start + j, 1), :] for n in range(2)) for side in range(2)
            ]

        carry = list(carry)
        for j, new in enumerate(block_step(field1, start + 1, unroll_2, edge_rows)):
            alive = start + j < depth_count
            for number, out in enumerate((theta_next, fuel_next)):
                value = jnp.where(alive, new[number], 0.0)
                out[start + j] = value
                position = jnp.clip(value, 0.0, 1.0) * (bins - 1)
                lower = jnp.minimum(position.astype(jnp.int32), bins - 2)
                fraction = position - lower.astype(F32)

                def look_up(entry):
                    low = jnp.take_along_axis(low_table[entry], lower, axis=1)
                    rise = jnp.take_along_axis(rise_table[entry], lower, axis=1)
                    return low + fraction * rise

                for f in range(2 * number, 2 * number + 2):
                    gone, red, green, blue = carry[4 * f : 4 * f + 4]
                    depth = jnp.where(alive, look_up(4 * f + 3), 0.0)
                    gain = depth * (1.0 + depth * (0.5 + depth * (1.0 / 6.0)))
                    gain = gain + gone * gain
                    carry[4 * f] = gone + gain
                    carry[4 * f + 1] = red + gain * look_up(4 * f)
                    carry[4 * f + 2] = green + gain * look_up(4 * f + 1)
                    carry[4 * f + 3] = blue + gain * look_up(4 * f + 2)
        return tuple(carry)

    zero = jnp.zeros((8, 128), F32)
    sums = lax.fori_loop(0, places // unroll_2, second_step, (zero,) * (4 * functions))

    channels = []
    for f in range(functions):
        gone, red, green, blue = sums[4 * f : 4 * f + 4]
        scale = jnp.where(camera[f] == 0, -1.0, 1.0 / (1.0 + gone))
        channels += [red * scale, green * scale, blue * scale, gone * scale]

    group = lanes() // 16
    for half in range(2):
        regs = channels[8 * half : 8 * half + 8]
        for bit in (1, 2, 4):
            upper = (group & bit) != 0
            fresh = list(regs)
            for i in range(8):
                if i & bit:
                    continue
                a, b = regs[i], regs[i | bit]
                fresh[i] = jnp.where(upper, pltpu.roll(b, 16 * bit, 1), a)
                fresh[i | bit] = jnp.where(upper, b, pltpu.roll(a, 128 - 16 * bit, 1))
            regs = fresh
        for g in range(8):
            image[pl.ds(2 * g + half, 8, stride=16), :] = regs[g]


def composite(camera, pieces, image):
    sources = pieces.shape[0] // 2
    lane = lanes()
    row = sublanes()
    opacity_lane = lane // 64 * 64 + 48 + lane % 16
    for half in range(2):
        forward = jnp.where(
            lane < 64,
            (camera[2 * half] == 0).astype(jnp.int32),
            (camera[2 * half + 1] == 0).astype(jnp.int32),
        ) == 1
        values, clear, through = [], [], []
        carry = jnp.ones((8, 128), F32)
        for block in range(sources // 8):
            value = pieces[pl.ds(16 * block + half, 8, stride=2), :]
            passing = 1.0 - jnp.take_along_axis(value, opacity_lane, axis=1)
            product = passing
            for shift in (1, 2, 4):
                product = product * jnp.where(row >= shift, pltpu.roll(product, shift, 0), 1.0)
            product = product * carry
            carry = jnp.broadcast_to(product[7:8], (8, 128))
            values.append(value)
            clear.append(passing)
            through.append(product)
        total = jnp.zeros((8, 128), F32)
        for value, passing, product in zip(values, clear, through):
            top = jnp.where(forward, product, carry)
            bottom = jnp.where(forward, passing, product)
            total = total + value * (top / bottom)
        line = jnp.sum(total, axis=0, keepdims=True)
        for clo in range(8):
            channel = 8 * half + clo
            image[channel // 4, channel % 4] = line[:, 16 * clo : 16 * clo + 16]


def shifted(array, axis, by):
    count = lax.axis_size(axis)
    pairs = [(i, i + by) for i in range(count) if 0 <= i + by < count]
    return lax.ppermute(array, axis, pairs)


def on_device(
    thermal_values,
    reactant_fraction,
    active_sheet_number,
    colour_lookup_library,
    colour_lookup_choice,
    camera_direction,
):
    places = thermal_values.shape[0]
    functions = colour_lookup_choice.shape[0]
    devices = lax.axis_size("depth")
    meta = jnp.stack(
        [
            active_sheet_number[0],
            lax.axis_index("lat").astype(jnp.int32),
            jnp.int32(lax.axis_size("lat")),
            jnp.int32(MEAN_DEPTH * devices),
        ]
    )
    rows = jax.ShapeDtypeStruct((4, places, 128), F32)
    layers = jax.ShapeDtypeStruct((2, 8, 128), F32)
    rim = jax.ShapeDtypeStruct((2, 3, 8, 128), F32)
    low_rows, high_rows, last_layer, first_layer = pl.pallas_call(
        pack_rows,
        out_shape=(rows, rows, layers, layers),
        in_specs=[in_smem(), in_vmem(), in_vmem()],
        out_specs=(in_vmem(),) * 4,
        name="pack_rows",
    )(meta, thermal_values, reactant_fraction)
    rows_below = shifted(high_rows, "lat", 1)
    rows_above = shifted(low_rows, "lat", -1)
    from_below_2 = shifted(last_layer, "depth", 2)
    from_above_2 = shifted(first_layer, "depth", -2)
    upward, downward = pl.pallas_call(
        pack_rims,
        out_shape=(rim, rim),
        in_specs=[in_smem()] + [in_vmem()] * 4,
        out_specs=(in_vmem(),) * 2,
        name="pack_rims",
    )(meta, thermal_values, reactant_fraction, rows_below, rows_above)
    from_below = shifted(upward, "depth", 1)
    from_above = shifted(downward, "depth", -1)
    field = jax.ShapeDtypeStruct(thermal_values.shape, F32)
    bins = colour_lookup_library.shape[2]
    theta_next, fuel_next, pieces = pl.pallas_call(
        functools.partial(advance_and_render, places, functions),
        out_shape=(field, field, jax.ShapeDtypeStruct((2 * devices, 128), F32)),
        in_specs=[in_smem()] * 3 + [pl.BlockSpec(memory_space=pl.ANY)] * 2 + [in_vmem()] * 9,
        out_specs=(in_vmem(),) * 3,
        scratch_shapes=[
            VMEM((2, places + 4, 8, 128), F32),
            VMEM((2, places + 2, 8, 128), F32),
            VMEM((2, 4, places + 16, 128), F32),
            VMEM((2, 2, places, 128), F32),
            VMEM(colour_lookup_library.shape, F32),
            VMEM((4 * functions, 8, bins), F32),
            VMEM((4 * functions, 8, bins), F32),
            pltpu.SemaphoreType.DMA((2,)),
        ],
        name="advance_and_render",
    )(
        meta,
        colour_lookup_choice,
        camera_direction,
        thermal_values,
        reactant_fraction,
        colour_lookup_library,
        low_rows,
        high_rows,
        rows_below,
        rows_above,
        from_below,
        from_above,
        from_below_2,
        from_above_2,
    )
    pieces = lax.all_to_all(pieces, "depth", 0, 0, tiled=True)
    image = pl.pallas_call(
        composite,
        out_shape=jax.ShapeDtypeStruct((functions, 4, 1, 16), F32),
        in_specs=[in_smem(), in_vmem()],
        out_specs=in_vmem(),
        name="composite",
    )(camera_direction, pieces)
    return (theta_next, fuel_next, image)


def solution(mesh):
    placed = (P("depth", "lat", None), P("depth", "lat", None), P("depth"), P(), P(), P())
    return jax.shard_map(
        on_device,
        mesh=mesh,
        in_specs=placed,
        out_specs=(P("depth", "lat", None), P("depth", "lat", None), P(None, None, "lat", "depth")),
        check_vma=False,
    )
```

```python
import functools

import jax
import jax.numpy as jnp
from jax import lax
from jax.experimental import pallas as pl
from jax.experimental.pallas import tpu as pltpu
from jax.sharding import PartitionSpec as P

MEAN_DEPTH = 32
STEPS = 2

time_step = 0.03
heat_release = 2.0
zeldovich = 8.0
expansion = 0.8

VMEM = pltpu.VMEM
SMEM = pltpu.SMEM
F32 = jnp.float32


def in_vmem():
    return pl.BlockSpec(memory_space=VMEM)


def in_smem():
    return pl.BlockSpec(memory_space=SMEM)


UNROLL_1 = 16
UNROLL_2 = 16


def pack_rows(
    counts, theta, fuel, field0, low_rows, high_rows, last_layer, first_layer, upward, downward, copies
):
    places = theta.shape[0]
    fetch = [
        pltpu.make_async_copy(source, field0.at[number, pl.ds(2, places)], copies.at[number])
        for number, source in enumerate((theta, fuel))
    ]
    for copy in fetch:
        copy.start()
    depth_count = counts[0]
    last = depth_count + 1
    second_last = jnp.maximum(depth_count, 2)
    second = jnp.minimum(3, last)
    size = jnp.broadcast_to(depth_count.astype(F32), (8, 128))
    for number in range(2):
        fetch[number].wait()
        for row in range(2):
            low_rows[2 * number + row] = field0[number, 2 : places + 2, row, :]
            high_rows[2 * number + row] = field0[number, 2 : places + 2, 6 + row, :]
        top = field0[number, last]
        bottom = field0[number, 2]
        last_layer[number] = top
        first_layer[number] = bottom
        upward[number, 0] = top
        upward[number, 1] = field0[number, second_last]
        upward[number, 2] = size
        downward[number, 0] = bottom
        downward[number, 1] = field0[number, second]
        downward[number, 2] = size


def pack_rims(
    counts, upward_in, downward_in, rows_below, rows_above, below_2, above_2, upward, downward
):
    last = counts[0] - 1
    for number in range(2):
        upward[number] = upward_in[number]
        downward[number] = downward_in[number]
        upward[number, 2, 0:1] = rows_below[2 * number + 1, pl.ds(last, 1), :]
        upward[number, 2, 1:2] = rows_above[2 * number, pl.ds(last, 1), :]
        downward[number, 2, 0:1] = rows_below[2 * number + 1, 0:1, :]
        downward[number, 2, 1:2] = rows_above[2 * number, 0:1, :]


def lanes():
    return lax.broadcasted_iota(jnp.int32, (8, 128), 1)


def sublanes():
    return lax.broadcasted_iota(jnp.int32, (8, 128), 0)


def left_of(x):
    return jnp.where(lanes() == 0, 0.0, pltpu.roll(x, 1, 1))


def right_of(x):
    return jnp.where(lanes() == 127, 0.0, pltpu.roll(x, 127, 1))


def row_below(x, halo_row):
    return jnp.where(sublanes() == 0, jnp.broadcast_to(halo_row, (8, 128)), pltpu.roll(x, 1, 0))


def row_above(x, halo_row):
    return jnp.where(sublanes() == 7, jnp.broadcast_to(halo_row, (8, 128)), pltpu.roll(x, 7, 0))


def stepped(heat, fuel, neighbours):
    heat_sum = neighbours[0][0]
    fuel_sum = neighbours[0][1]
    product_sum = neighbours[0][0] * neighbours[0][1]
    square_sum = neighbours[0][0] * neighbours[0][0]
    for heat_n, fuel_n in neighbours[1:]:
        heat_sum = heat_sum + heat_n
        fuel_sum = fuel_sum + fuel_n
        product_sum = product_sum + heat_n * fuel_n
        square_sum = square_sum + heat_n * heat_n
    heat_flux = (heat_sum - 6.0 * heat) + 1.5 * (square_sum - 6.0 * (heat * heat))
    fuel_flux = 0.5 * (
        (1.0 + 1.5 * heat) * (fuel_sum - 6.0 * fuel) + 1.5 * (product_sum - fuel * heat_sum)
    )
    ratio = zeldovich / expansion
    reaction = fuel * jnp.exp(ratio - ratio / ((1.0 - expansion) + expansion * heat))
    return (
        heat + time_step * (heat_flux + heat_release * reaction),
        fuel + time_step * (fuel_flux - reaction),
    )


LEAD = 8


def block_step(field, at, count, edge_rows):
    heat = [field[0, at - 1 + j] for j in range(count + 2)]
    burn = [field[1, at - 1 + j] for j in range(count + 2)]
    results = []
    for j in range(1, count + 1):
        h, b = heat[j], burn[j]
        (h_low, b_low), (h_high, b_high) = edge_rows(j - 1)
        around = [
            (heat[j - 1], burn[j - 1]),
            (heat[j + 1], burn[j + 1]),
            (row_below(h, h_low), row_below(b, b_low)),
            (row_above(h, h_high), row_above(b, b_high)),
            (left_of(h), left_of(b)),
            (right_of(h), right_of(b)),
        ]
        results.append(stepped(h, b, around))
    return results


def rows_beside(edge, sides, place):
    return [tuple(edge[n, side, pl.ds(place, 1), :] for n in range(2)) for side in sides]


def step_edges(edge0, inner, side, at, inner_at, count):
    edge_row = 1 + side
    outer_row = 3 * side

    def rows(ref, row, place):
        found = tuple(ref(n)[row(n), pl.ds(place, count), :] for n in range(2))
        return tuple(jnp.broadcast_to(x, (8, 128)) for x in found)

    def edge(row, shift):
        return rows(lambda n: edge0.at[n], lambda n: row, at + shift)

    heat, burn = edge(edge_row, 0)
    around = [
        edge(edge_row, -1),
        edge(edge_row, 1),
        edge(outer_row, 0),
        rows(lambda n: inner, lambda n: 2 * n + side, inner_at),
        (left_of(heat), left_of(burn)),
        (right_of(heat), right_of(burn)),
    ]
    outside = lax.axis_index("lat") == (0 if side == 0 else lax.axis_size("lat") - 1)
    return [jnp.where(outside, 0.0, x) for x in stepped(heat, burn, around)]


def inner_step(
    places,
    functions,
    all_layers,
    choice,
    camera,
    field0,
    library,
    own_low,
    own_high,
    rows_below,
    rows_above,
    field1,
    edge0,
    edge1,
    low_table,
    rise_table,
    tables,
):
    bins = library.shape[2]
    tables[...] = library[...].astype(F32)
    per_cell = 3.0 / all_layers
    for f in range(functions):
        sign = jnp.where(camera[f] == 0, -per_cell, per_cell)
        for c in range(4):
            low = jnp.broadcast_to(tables[choice[f], c : c + 1, :], (8, bins))
            rise = pltpu.roll(low, bins - 1, 1) - low
            if c == 3:
                low = low * sign
                rise = rise * sign
            low_table[4 * f + c] = low
            rise_table[4 * f + c] = rise

    for number in range(2):
        for row in range(2):
            edge0[number, row, LEAD : LEAD + places] = rows_below[2 * number + row]
            edge0[number, 2 + row, LEAD : LEAD + places] = rows_above[2 * number + row]

    for block in range(places // 8):
        for side in range(2):
            inner = (own_low, own_high)[side]
            fresh = step_edges(edge0, inner, side, LEAD + 8 * block, 8 * block, 8)
            for number in range(2):
                edge1[number, side, 8 * block : 8 * block + 8] = fresh[number]

    unroll = UNROLL_1

    def first_step(block, carry):
        start = block * unroll

        def edge_rows(j):
            return rows_beside(edge0, (1, 2), LEAD + start + j)

        for j, new in enumerate(block_step(field0, start + 2, unroll, edge_rows)):
            for number in range(2):
                field1[number, start + 1 + j] = new[number]
        return carry

    lax.fori_loop(0, places // unroll, first_step, 0)


def outer_step(
    places,
    functions,
    counts,
    camera,
    field0_in,
    field1_in,
    edge0_in,
    edge1_in,
    low_table,
    rise_table,
    own_low,
    own_high,
    from_below,
    from_above,
    from_below_2,
    from_above_2,
    theta_next,
    fuel_next,
    image,
    field0,
    field1,
    edge0,
    edge1,
    result,
    copies,
):
    depth_count = counts[0]
    bins = low_table.shape[2]
    below_size = jnp.broadcast_to(from_below[0, 2, 2:3], (8, 128))
    above_size = jnp.broadcast_to(from_above[0, 2, 2:3], (8, 128))
    for number in range(2):
        field0[number, 0] = jnp.where(below_size == 1.0, from_below_2[number], from_below[number, 1])
        field0[number, 1] = from_below[number, 0]
        field0[number, depth_count + 2] = from_above[number, 0]
        field0[number, depth_count + 3] = jnp.where(
            above_size == 1.0, from_above_2[number], from_above[number, 1]
        )
        for side in range(2):
            edge0[number, 1 + side, LEAD - 1 : LEAD] = from_below[number, 2, side : side + 1]
            edge0[number, 1 + side, pl.ds(LEAD + depth_count, 1)] = from_above[
                number, 2, side : side + 1
            ]
    for place in (0, depth_count - 1):
        for side in range(2):
            fresh = step_edges(edge0, (own_low, own_high)[side], side, LEAD + place, place, 1)
            for number in range(2):
                edge1[number, side, pl.ds(place, 1)] = fresh[number][0:1]
    for place, size in (
        (-1, below_size),
        (0, None),
        (depth_count - 1, None),
        (depth_count, above_size),
    ):

        def edge_rows(j, place=place):
            return rows_beside(edge0, (1, 2), LEAD + place)

        (fresh,) = block_step(field0, place + 2, 1, edge_rows)
        for number in range(2):
            value = fresh[number]
            field1[number, place + 1] = (
                value if size is None else jnp.where(size > 0.0, value, 0.0)
            )

    unroll = UNROLL_2

    def leave(number, first, count):
        return pltpu.make_async_copy(
            result.at[number, pl.ds(first, count)],
            (theta_next, fuel_next)[number].at[pl.ds(first, count)],
            copies.at[number],
        )

    def second_step(block, carry):
        start = block * unroll

        def edge_rows(j):
            return rows_beside(edge1, (0, 1), start + j)

        carry = list(carry)
        for j, new in enumerate(block_step(field1, start + 1, unroll, edge_rows)):
            alive = start + j < depth_count
            for number in range(2):
                value = jnp.where(alive, new[number], 0.0)
                result[number, start + j] = value
                position = jnp.clip(value, 0.0, 1.0) * (bins - 1)
                lower = jnp.minimum(position.astype(jnp.int32), bins - 2)
                fraction = position - lower.astype(F32)

                def look_up(entry):
                    low = jnp.take_along_axis(low_table[entry], lower, axis=1)
                    rise = jnp.take_along_axis(rise_table[entry], lower, axis=1)
                    return low + fraction * rise

                for f in range(2 * number, 2 * number + 2):
                    gone, red, green, blue = carry[4 * f : 4 * f + 4]
                    depth = jnp.where(alive, look_up(4 * f + 3), 0.0)
                    gain = depth * (1.0 + depth * (0.5 + depth * (1.0 / 6.0)))
                    gain = gain + gone * gain
                    carry[4 * f] = gone + gain
                    carry[4 * f + 1] = red + gain * look_up(4 * f)
                    carry[4 * f + 2] = green + gain * look_up(4 * f + 1)
                    carry[4 * f + 3] = blue + gain * look_up(4 * f + 2)
        for number in range(2):
            leave(number, start, unroll).start()
        return tuple(carry)

    zero = jnp.zeros((8, 128), F32)
    sums = lax.fori_loop(0, places // unroll, second_step, (zero,) * (4 * functions))

    channels = []
    for f in range(functions):
        gone, red, green, blue = sums[4 * f : 4 * f + 4]
        scale = jnp.where(camera[f] == 0, -1.0, 1.0 / (1.0 + gone))
        channels += [red * scale, green * scale, blue * scale, gone * scale]

    group = lanes() // 16
    for half in range(2):
        regs = channels[8 * half : 8 * half + 8]
        for bit in (1, 2, 4):
            upper = (group & bit) != 0
            fresh = list(regs)
            for i in range(8):
                if i & bit:
                    continue
                a, b = regs[i], regs[i | bit]
                fresh[i] = jnp.where(upper, pltpu.roll(b, 16 * bit, 1), a)
                fresh[i | bit] = jnp.where(upper, b, pltpu.roll(a, 128 - 16 * bit, 1))
            regs = fresh
        for g in range(8):
            image[pl.ds(2 * g + half, 8, stride=16), :] = regs[g]
    for number in range(2):
        leave(number, 0, places).wait()


def composite(camera, pieces, image):
    sources = pieces.shape[0] // 2
    lane = lanes()
    row = sublanes()
    opacity_lane = lane // 64 * 64 + 48 + lane % 16
    for half in range(2):
        forward = jnp.where(
            lane < 64,
            (camera[2 * half] == 0).astype(jnp.int32),
            (camera[2 * half + 1] == 0).astype(jnp.int32),
        ) == 1
        values, clear, through = [], [], []
        carry = jnp.ones((8, 128), F32)
        for block in range(sources // 8):
            value = pieces[pl.ds(16 * block + half, 8, stride=2), :]
            passing = 1.0 - jnp.take_along_axis(value, opacity_lane, axis=1)
            product = passing
            for shift in (1, 2, 4):
                product = product * jnp.where(row >= shift, pltpu.roll(product, shift, 0), 1.0)
            product = product * carry
            carry = jnp.broadcast_to(product[7:8], (8, 128))
            values.append(value)
            clear.append(passing)
            through.append(product)
        total = jnp.zeros((8, 128), F32)
        for value, passing, product in zip(values, clear, through):
            top = jnp.where(forward, product, carry)
            bottom = jnp.where(forward, passing, product)
            total = total + value * (top / bottom)
        line = jnp.sum(total, axis=0, keepdims=True)
        for clo in range(8):
            channel = 8 * half + clo
            image[channel // 4, channel % 4] = line[:, 16 * clo : 16 * clo + 16]


def shifted(array, axis, by):
    count = lax.axis_size(axis)
    pairs = [(i, i + by) for i in range(count) if 0 <= i + by < count]
    return lax.ppermute(array, axis, pairs)


def held(array):
    return pltpu.with_memory_space_constraint(array, VMEM)


def in_hbm(array):
    return pltpu.with_memory_space_constraint(array, pltpu.HBM)


def params():
    return pltpu.CompilerParams(vmem_limit_bytes=16 * 1024 * 1024)


def anywhere():
    return pl.BlockSpec(memory_space=pl.ANY)


def first_kernel(active_sheet_number, thermal_values, reactant_fraction):
    places = thermal_values.shape[0]
    rows = VMEM((4, places, 128), F32)
    layers = VMEM((2, 8, 128), F32)
    rim = VMEM((2, 3, 8, 128), F32)
    return pl.pallas_call(
        pack_rows,
        out_shape=(VMEM((2, places + 4, 8, 128), F32), rows, rows, layers, layers, rim, rim),
        in_specs=[in_smem()] + [anywhere()] * 2,
        out_specs=(in_vmem(),) * 7,
        scratch_shapes=[pltpu.SemaphoreType.DMA((2,))],
        compiler_params=params(),
        name="pack_rows",
    )(active_sheet_number, *map(in_hbm, (thermal_values, reactant_fraction)))


def rim_kernel(counts, upward, downward, *received):
    rim = VMEM((2, 3, 8, 128), F32)
    return pl.pallas_call(
        pack_rims,
        out_shape=(rim, rim),
        in_specs=[in_smem()] + [in_vmem()] * 6,
        out_specs=(in_vmem(),) * 2,
        compiler_params=params(),
        name="pack_rims",
    )(counts, *map(held, (upward, downward, *received)))


def inner_kernel(devices, choice, camera, field0, library, *rows):
    places = field0.shape[1] - 4
    functions = choice.shape[0]
    bins = library.shape[2]
    table = VMEM((4 * functions, 8, bins), F32)
    return pl.pallas_call(
        functools.partial(inner_step, places, functions, float(MEAN_DEPTH * devices)),
        out_shape=(
            VMEM((2, places + 2, 8, 128), F32),
            VMEM((2, 4, places + 16, 128), F32),
            VMEM((2, 2, places, 128), F32),
            table,
            table,
        ),
        in_specs=[in_smem()] * 2 + [in_vmem()] * 6,
        out_specs=(in_vmem(),) * 5,
        scratch_shapes=[VMEM(library.shape, F32)],
        compiler_params=params(),
        cost_estimate=pl.CostEstimate(flops=10**7, bytes_accessed=10**6, transcendentals=10**5),
        name="inner_step",
    )(choice, camera, held(field0), library, *map(held, rows))


def outer_kernel(devices, counts, camera, *arrays):
    field0, field1, edge0, edge1 = arrays[:4]
    places = field0.shape[1] - 4
    functions = camera.shape[0]
    field = jax.ShapeDtypeStruct((places, 8, 128), F32)
    return pl.pallas_call(
        functools.partial(outer_step, places, functions),
        out_shape=(field, field, VMEM((2 * devices, 128), F32))
        + tuple(VMEM(x.shape, F32) for x in (field0, field1, edge0, edge1)),
        in_specs=[in_smem()] * 2 + [in_vmem()] * len(arrays),
        out_specs=(anywhere(),) * 2 + (in_vmem(),) * 5,
        scratch_shapes=[
            VMEM((2, places, 8, 128), F32),
            pltpu.SemaphoreType.DMA((2,)),
        ],
        input_output_aliases={2 + i: 3 + i for i in range(4)},
        compiler_params=params(),
        cost_estimate=pl.CostEstimate(flops=2 * 10**7, bytes_accessed=10**6, transcendentals=10**5),
        name="outer_step",
    )(counts, camera, *map(held, arrays))[:3]


def last_kernel(functions, camera, pieces):
    return pl.pallas_call(
        composite,
        out_shape=jax.ShapeDtypeStruct((functions, 4, 1, 16), F32),
        in_specs=[in_smem(), in_vmem()],
        out_specs=in_vmem(),
        compiler_params=params(),
        name="composite",
    )(camera, held(pieces))


def on_device(
    thermal_values,
    reactant_fraction,
    active_sheet_number,
    colour_lookup_library,
    colour_lookup_choice,
    camera_direction,
):
    devices = lax.axis_size("depth")
    field0, own_low, own_high, last_layer, first_layer, upward, downward = first_kernel(
        active_sheet_number, thermal_values, reactant_fraction
    )
    rows_below = shifted(own_high, "lat", 1)
    rows_above = shifted(own_low, "lat", -1)
    below_2 = shifted(last_layer, "depth", 2)
    above_2 = shifted(first_layer, "depth", -2)
    upward, downward = rim_kernel(
        active_sheet_number, upward, downward, rows_below, rows_above, below_2, above_2
    )
    from_below = shifted(upward, "depth", 1)
    from_above = shifted(downward, "depth", -1)
    field1, edge0, edge1, low_table, rise_table = inner_kernel(
        devices,
        colour_lookup_choice,
        camera_direction,
        field0,
        colour_lookup_library,
        own_low,
        own_high,
        rows_below,
        rows_above,
    )
    theta_next, fuel_next, pieces = outer_kernel(
        devices,
        active_sheet_number,
        camera_direction,
        field0,
        field1,
        edge0,
        edge1,
        low_table,
        rise_table,
        own_low,
        own_high,
        from_below,
        from_above,
        below_2,
        above_2,
    )
    pieces = lax.all_to_all(pieces, "depth", 0, 0, tiled=True)
    image = last_kernel(colour_lookup_choice.shape[0], camera_direction, pieces)
    return (theta_next, fuel_next, image)


def solution(mesh):
    placed = (P("depth", "lat", None), P("depth", "lat", None), P("depth"), P(), P(), P())
    return jax.shard_map(
        on_device,
        mesh=mesh,
        in_specs=placed,
        out_specs=(P("depth", "lat", None), P("depth", "lat", None), P(None, None, "lat", "depth")),
        check_vma=False,
    )
```

```python
import functools

import jax
import jax.numpy as jnp
from jax import lax
from jax.experimental import pallas as pl
from jax.experimental.pallas import tpu as pltpu
from jax.sharding import PartitionSpec as P

MEAN_DEPTH = 32
STEPS = 2

time_step = 0.03
heat_release = 2.0
zeldovich = 8.0
expansion = 0.8

VMEM = pltpu.VMEM
SMEM = pltpu.SMEM
F32 = jnp.float32


def in_vmem():
    return pl.BlockSpec(memory_space=VMEM)


def in_smem():
    return pl.BlockSpec(memory_space=SMEM)


UNROLL_1 = 16
UNROLL_2 = 16


def is_even(axis):
    return lax.rem(lax.axis_index(axis), 2) == 0


def select(which, first, second):
    return jnp.where(which, first, second)


def pack_rows(
    counts_in,
    choice_in,
    camera_in,
    theta,
    fuel,
    library_in,
    counts,
    choice,
    camera,
    library,
    field0,
    own_rows,
    rows_pair,
    rows_gap,
    rim_pair,
    rim_gap,
    copies,
):
    places = theta.shape[0]
    moves = [
        (counts_in, counts),
        (theta, field0.at[0, pl.ds(2, places)]),
        (fuel, field0.at[1, pl.ds(2, places)]),
        (choice_in, choice),
        (camera_in, camera),
        (library_in, library),
    ]
    fetch = [
        pltpu.make_async_copy(source, target, copies.at[number])
        for number, (source, target) in enumerate(moves)
    ]
    for copy in fetch:
        copy.start()
    lat_even, depth_even = is_even("lat"), is_even("depth")
    for number in range(2):
        fetch[1 + number].wait()
        for row in range(2):
            low = field0[number, 2 : places + 2, row, :]
            high = field0[number, 2 : places + 2, 6 + row, :]
            rows_pair[2 * number + row] = select(lat_even, high, low)
            rows_gap[2 * number + row] = select(lat_even, low, high)
            own_rows[2 * row + number] = (low, high)[row]
    fetch[0].wait()
    depth_count = counts[0]
    last = depth_count + 1
    second_last = jnp.maximum(depth_count, 2)
    second = jnp.minimum(3, last)
    size = jnp.broadcast_to(depth_count.astype(F32), (8, 128))
    for number in range(2):
        up = (field0[number, last], field0[number, second_last], size)
        down = (field0[number, 2], field0[number, second], size)
        for layer in range(3):
            rim_pair[number, layer] = select(depth_even, up[layer], down[layer])
            rim_gap[number, layer] = select(depth_even, down[layer], up[layer])
    for copy in fetch[3:]:
        copy.wait()


def pack_rims(counts, rows_pair, rows_gap, rim_pair, rim_gap, next_pair, next_gap):
    last = counts[0] - 1
    lat_even, depth_even = is_even("lat"), is_even("depth")
    for number in range(2):
        from_above = select(depth_even, rim_pair[number, 0], rim_gap[number, 0])
        from_below = select(depth_even, rim_gap[number, 0], rim_pair[number, 0])

        def beside(place):
            below = [ref[2 * number + 1, pl.ds(place, 1), :] for ref in (rows_gap, rows_pair)]
            above = [ref[2 * number, pl.ds(place, 1), :] for ref in (rows_pair, rows_gap)]
            rows = [select(lat_even, *below), select(lat_even, *above)]
            return jnp.where(sublanes() == 0, *(jnp.broadcast_to(x, (8, 128)) for x in rows))

        up = (from_below, beside(last))
        down = (from_above, beside(0))
        for layer in range(2):
            next_pair[number, layer] = select(depth_even, up[layer], down[layer])
            next_gap[number, layer] = select(depth_even, down[layer], up[layer])


def lanes():
    return lax.broadcasted_iota(jnp.int32, (8, 128), 1)


def sublanes():
    return lax.broadcasted_iota(jnp.int32, (8, 128), 0)


def left_of(x):
    return jnp.where(lanes() == 0, 0.0, pltpu.roll(x, 1, 1))


def right_of(x):
    return jnp.where(lanes() == 127, 0.0, pltpu.roll(x, 127, 1))


def row_below(x, halo_row):
    return jnp.where(sublanes() == 0, jnp.broadcast_to(halo_row, (8, 128)), pltpu.roll(x, 1, 0))


def row_above(x, halo_row):
    return jnp.where(sublanes() == 7, jnp.broadcast_to(halo_row, (8, 128)), pltpu.roll(x, 7, 0))


def stepped(heat, fuel, neighbours):
    heat_sum = neighbours[0][0]
    fuel_sum = neighbours[0][1]
    product_sum = neighbours[0][0] * neighbours[0][1]
    square_sum = neighbours[0][0] * neighbours[0][0]
    for heat_n, fuel_n in neighbours[1:]:
        heat_sum = heat_sum + heat_n
        fuel_sum = fuel_sum + fuel_n
        product_sum = product_sum + heat_n * fuel_n
        square_sum = square_sum + heat_n * heat_n
    heat_flux = (heat_sum - 6.0 * heat) + 1.5 * (square_sum - 6.0 * (heat * heat))
    fuel_flux = 0.5 * (
        (1.0 + 1.5 * heat) * (fuel_sum - 6.0 * fuel) + 1.5 * (product_sum - fuel * heat_sum)
    )
    ratio = zeldovich / expansion
    reaction = fuel * jnp.exp(ratio - ratio / ((1.0 - expansion) + expansion * heat))
    return (
        heat + time_step * (heat_flux + heat_release * reaction),
        fuel + time_step * (fuel_flux - reaction),
    )


LEAD = 8


def block_step(field, at, count, edge_rows):
    heat = [field[0, at - 1 + j] for j in range(count + 2)]
    burn = [field[1, at - 1 + j] for j in range(count + 2)]
    results = []
    for j in range(1, count + 1):
        h, b = heat[j], burn[j]
        (h_low, b_low), (h_high, b_high) = edge_rows(j - 1)
        around = [
            (heat[j - 1], burn[j - 1]),
            (heat[j + 1], burn[j + 1]),
            (row_below(h, h_low), row_below(b, b_low)),
            (row_above(h, h_high), row_above(b, b_high)),
            (left_of(h), left_of(b)),
            (right_of(h), right_of(b)),
        ]
        results.append(stepped(h, b, around))
    return results


def rows_beside(edge, sides, place):
    return [tuple(edge[n, side, pl.ds(place, 1), :] for n in range(2)) for side in sides]


def step_edges(edge0, inner, side, at, inner_at, count):
    edge_row = 1 + side
    outer_row = 3 * side

    def rows(ref, row, place):
        found = tuple(ref(n)[row(n), pl.ds(place, count), :] for n in range(2))
        return tuple(jnp.broadcast_to(x, (8, 128)) for x in found)

    def edge(row, shift):
        return rows(lambda n: edge0.at[n], lambda n: row, at + shift)

    heat, burn = edge(edge_row, 0)
    around = [
        edge(edge_row, -1),
        edge(edge_row, 1),
        edge(outer_row, 0),
        rows(lambda n: inner, lambda n: 2 * side + n, inner_at),
        (left_of(heat), left_of(burn)),
        (right_of(heat), right_of(burn)),
    ]
    outside = lax.axis_index("lat") == (0 if side == 0 else lax.axis_size("lat") - 1)
    return [jnp.where(outside, 0.0, x) for x in stepped(heat, burn, around)]


def inner_step(
    places,
    functions,
    all_layers,
    counts,
    choice,
    camera,
    field0_in,
    library,
    own_rows,
    rows_pair,
    rows_gap,
    rim_pair,
    rim_gap,
    field0,
    field1,
    edge0,
    edge1,
    low_table,
    rise_table,
    tables,
):
    lat_even, depth_even = is_even("lat"), is_even("depth")
    for number in range(2):
        above, below = rim_pair[number, 0], rim_gap[number, 0]
        field0[number, 1] = select(depth_even, below, above)
        field0[number, counts[0] + 2] = select(depth_even, above, below)
    bins = library.shape[2]
    tables[...] = library[...].astype(F32)
    per_cell = 3.0 / all_layers
    for f in range(functions):
        sign = jnp.where(camera[f] == 0, -per_cell, per_cell)
        for c in range(4):
            low = jnp.broadcast_to(tables[choice[f], c : c + 1, :], (8, bins))
            rise = pltpu.roll(low, bins - 1, 1) - low
            if c == 3:
                low = low * sign
                rise = rise * sign
            low_table[4 * f + c] = low
            rise_table[4 * f + c] = rise

    for number in range(2):
        for row in range(2):
            pair, gap = rows_pair[2 * number + row], rows_gap[2 * number + row]
            edge0[number, row, LEAD : LEAD + places] = select(lat_even, gap, pair)
            edge0[number, 2 + row, LEAD : LEAD + places] = select(lat_even, pair, gap)

    for block in range(places // 8):
        for side in range(2):
            fresh = step_edges(edge0, own_rows, side, LEAD + 8 * block, 8 * block, 8)
            for number in range(2):
                edge1[number, side, 8 * block : 8 * block + 8] = fresh[number]

    unroll = UNROLL_1

    def first_step(block, carry):
        start = block * unroll

        def edge_rows(j):
            return rows_beside(edge0, (1, 2), LEAD + start + j)

        for j, new in enumerate(block_step(field0, start + 2, unroll, edge_rows)):
            for number in range(2):
                field1[number, start + 1 + j] = new[number]
        return carry

    lax.fori_loop(0, places // unroll, first_step, 0)


def outer_step(
    places,
    functions,
    counts,
    camera,
    field0_in,
    field1_in,
    edge0_in,
    edge1_in,
    low_table,
    rise_table,
    own_rows,
    rim_pair,
    rim_gap,
    next_pair,
    next_gap,
    theta_next,
    fuel_next,
    image,
    field0,
    field1,
    edge0,
    edge1,
    result,
    copies,
):
    depth_count = counts[0]
    bins = low_table.shape[2]
    depth_even = is_even("depth")

    def from_below(pair, gap, *at):
        return select(depth_even, gap[at], pair[at])

    def from_above(pair, gap, *at):
        return select(depth_even, pair[at], gap[at])

    below_size = from_below(rim_pair, rim_gap, 0, 2)
    above_size = from_above(rim_pair, rim_gap, 0, 2)
    for number in range(2):
        field0[number, 0] = jnp.where(
            below_size == 1.0,
            from_below(next_pair, next_gap, number, 0),
            from_below(rim_pair, rim_gap, number, 1),
        )
        field0[number, depth_count + 3] = jnp.where(
            above_size == 1.0,
            from_above(next_pair, next_gap, number, 0),
            from_above(rim_pair, rim_gap, number, 1),
        )
        below_rows = from_below(next_pair, next_gap, number, 1)
        above_rows = from_above(next_pair, next_gap, number, 1)
        for side in range(2):
            edge0[number, 1 + side, LEAD - 1 : LEAD] = below_rows[side : side + 1]
            edge0[number, 1 + side, pl.ds(LEAD + depth_count, 1)] = above_rows[side : side + 1]
    for place in (0, depth_count - 1):
        for side in range(2):
            fresh = step_edges(edge0, own_rows, side, LEAD + place, place, 1)
            for number in range(2):
                edge1[number, side, pl.ds(place, 1)] = fresh[number][0:1]
    for place, size in ((-1, below_size), (depth_count, above_size)):

        def edge_rows(j, place=place):
            return rows_beside(edge0, (1, 2), LEAD + place)

        (fresh,) = block_step(field0, place + 2, 1, edge_rows)
        for number in range(2):
            field1[number, place + 1] = jnp.where(size > 0.0, fresh[number], 0.0)

    unroll = UNROLL_2

    def leave(number, first, count):
        return pltpu.make_async_copy(
            result.at[number, pl.ds(first, count)],
            (theta_next, fuel_next)[number].at[pl.ds(first, count)],
            copies.at[number],
        )

    def second_step(block, carry):
        start = block * unroll

        def edge_rows(j):
            return rows_beside(edge1, (0, 1), start + j)

        carry = list(carry)
        for j, new in enumerate(block_step(field1, start + 1, unroll, edge_rows)):
            alive = start + j < depth_count
            for number in range(2):
                value = jnp.where(alive, new[number], 0.0)
                result[number, start + j] = value
                position = jnp.clip(value, 0.0, 1.0) * (bins - 1)
                lower = jnp.minimum(position.astype(jnp.int32), bins - 2)
                fraction = position - lower.astype(F32)

                def look_up(entry):
                    low = jnp.take_along_axis(low_table[entry], lower, axis=1)
                    rise = jnp.take_along_axis(rise_table[entry], lower, axis=1)
                    return low + fraction * rise

                for f in range(2 * number, 2 * number + 2):
                    gone, red, green, blue = carry[4 * f : 4 * f + 4]
                    depth = jnp.where(alive, look_up(4 * f + 3), 0.0)
                    gain = depth * (1.0 + depth * (0.5 + depth * (1.0 / 6.0)))
                    gain = gain + gone * gain
                    carry[4 * f] = gone + gain
                    carry[4 * f + 1] = red + gain * look_up(4 * f)
                    carry[4 * f + 2] = green + gain * look_up(4 * f + 1)
                    carry[4 * f + 3] = blue + gain * look_up(4 * f + 2)
        for number in range(2):
            leave(number, start, unroll).start()
        return tuple(carry)

    zero = jnp.zeros((8, 128), F32)
    sums = lax.fori_loop(0, places // unroll, second_step, (zero,) * (4 * functions))

    channels = []
    for f in range(functions):
        gone, red, green, blue = sums[4 * f : 4 * f + 4]
        scale = jnp.where(camera[f] == 0, -1.0, 1.0 / (1.0 + gone))
        channels += [red * scale, green * scale, blue * scale, gone * scale]

    group = lanes() // 16
    for half in range(2):
        regs = channels[8 * half : 8 * half + 8]
        for bit in (1, 2, 4):
            upper = (group & bit) != 0
            fresh = list(regs)
            for i in range(8):
                if i & bit:
                    continue
                a, b = regs[i], regs[i | bit]
                fresh[i] = jnp.where(upper, pltpu.roll(b, 16 * bit, 1), a)
                fresh[i | bit] = jnp.where(upper, b, pltpu.roll(a, 128 - 16 * bit, 1))
            regs = fresh
        for g in range(8):
            image[pl.ds(2 * g + half, 8, stride=16), :] = regs[g]
    for number in range(2):
        leave(number, 0, places).wait()


def composite(camera, pieces, image):
    sources = pieces.shape[0] // 2
    lane = lanes()
    row = sublanes()
    opacity_lane = lane // 64 * 64 + 48 + lane % 16
    for half in range(2):
        forward = jnp.where(
            lane < 64,
            (camera[2 * half] == 0).astype(jnp.int32),
            (camera[2 * half + 1] == 0).astype(jnp.int32),
        ) == 1
        values, clear, through = [], [], []
        carry = jnp.ones((8, 128), F32)
        for block in range(sources // 8):
            value = pieces[pl.ds(16 * block + half, 8, stride=2), :]
            passing = 1.0 - jnp.take_along_axis(value, opacity_lane, axis=1)
            product = passing
            for shift in (1, 2, 4):
                product = product * jnp.where(row >= shift, pltpu.roll(product, shift, 0), 1.0)
            product = product * carry
            carry = jnp.broadcast_to(product[7:8], (8, 128))
            values.append(value)
            clear.append(passing)
            through.append(product)
        total = jnp.zeros((8, 128), F32)
        for value, passing, product in zip(values, clear, through):
            top = jnp.where(forward, product, carry)
            bottom = jnp.where(forward, passing, product)
            total = total + value * (top / bottom)
        line = jnp.sum(total, axis=0, keepdims=True)
        for clo in range(8):
            channel = 8 * half + clo
            image[channel // 4, channel % 4] = line[:, 16 * clo : 16 * clo + 16]


def swapped(array, axis, first):
    count = lax.axis_size(axis)
    pairs = []
    for i in range(first, count - 1, 2):
        pairs += [(i, i + 1), (i + 1, i)]
    return lax.ppermute(array, axis, pairs)


def held(array):
    return pltpu.with_memory_space_constraint(array, VMEM)


def in_hbm(array):
    return pltpu.with_memory_space_constraint(array, pltpu.HBM)


def params():
    return pltpu.CompilerParams(vmem_limit_bytes=16 * 1024 * 1024)


def anywhere():
    return pl.BlockSpec(memory_space=pl.ANY)


def in_scalars(array):
    return pltpu.with_memory_space_constraint(array, SMEM)


def first_kernel(counts, choice, camera, theta, fuel, library):
    places = theta.shape[0]
    rows = VMEM((4, places, 128), F32)
    rim = VMEM((2, 3, 8, 128), F32)
    return pl.pallas_call(
        pack_rows,
        out_shape=tuple(SMEM(x.shape, jnp.int32) for x in (counts, choice, camera))
        + (VMEM(library.shape, library.dtype), VMEM((2, places + 4, 8, 128), F32))
        + (rows, rows, rows, rim, rim),
        in_specs=[anywhere()] * 6,
        out_specs=(in_smem(),) * 3 + (in_vmem(),) * 7,
        scratch_shapes=[pltpu.SemaphoreType.DMA((6,))],
        compiler_params=params(),
        name="pack_rows",
    )(counts, *map(in_hbm, (choice, camera, theta, fuel, library)))


def rim_kernel(counts, *received):
    rim = VMEM((2, 2, 8, 128), F32)
    return pl.pallas_call(
        pack_rims,
        out_shape=(rim, rim),
        in_specs=[in_smem()] + [in_vmem()] * 4,
        out_specs=(in_vmem(),) * 2,
        compiler_params=params(),
        name="pack_rims",
    )(in_scalars(counts), *map(held, received))


def inner_kernel(devices, counts, choice, camera, field0, library, *rows):
    places = field0.shape[1] - 4
    functions = choice.shape[0]
    bins = library.shape[2]
    table = VMEM((4 * functions, 8, bins), F32)
    return pl.pallas_call(
        functools.partial(inner_step, places, functions, float(MEAN_DEPTH * devices)),
        out_shape=(
            VMEM(field0.shape, F32),
            VMEM((2, places + 2, 8, 128), F32),
            VMEM((2, 4, places + 16, 128), F32),
            VMEM((2, 2, places, 128), F32),
            table,
            table,
        ),
        in_specs=[in_smem()] * 3 + [in_vmem()] * 7,
        out_specs=(in_vmem(),) * 6,
        scratch_shapes=[VMEM(library.shape, F32)],
        input_output_aliases={3: 0},
        compiler_params=params(),
        cost_estimate=pl.CostEstimate(flops=10**7, bytes_accessed=10**6, transcendentals=10**5),
        name="inner_step",
    )(*map(in_scalars, (counts, choice, camera)), *map(held, (field0, library, *rows)))


def outer_kernel(devices, counts, camera, *arrays):
    field0, field1, edge0, edge1 = arrays[:4]
    places = field0.shape[1] - 4
    functions = camera.shape[0]
    field = jax.ShapeDtypeStruct((places, 8, 128), F32)
    return pl.pallas_call(
        functools.partial(outer_step, places, functions),
        out_shape=(field, field, VMEM((2 * devices, 128), F32))
        + tuple(VMEM(x.shape, F32) for x in (field0, field1, edge0, edge1)),
        in_specs=[in_smem()] * 2 + [in_vmem()] * len(arrays),
        out_specs=(anywhere(),) * 2 + (in_vmem(),) * 5,
        scratch_shapes=[
            VMEM((2, places, 8, 128), F32),
            pltpu.SemaphoreType.DMA((2,)),
        ],
        input_output_aliases={2 + i: 3 + i for i in range(4)},
        compiler_params=params(),
        cost_estimate=pl.CostEstimate(flops=2 * 10**7, bytes_accessed=10**6, transcendentals=10**5),
        name="outer_step",
    )(*map(in_scalars, (counts, camera)), *map(held, arrays))[:3]


def last_kernel(functions, camera, pieces):
    return pl.pallas_call(
        composite,
        out_shape=jax.ShapeDtypeStruct((functions, 4, 1, 16), F32),
        in_specs=[in_smem(), in_vmem()],
        out_specs=in_vmem(),
        compiler_params=params(),
        name="composite",
    )(in_scalars(camera), held(pieces))


def on_device(
    thermal_values,
    reactant_fraction,
    active_sheet_number,
    colour_lookup_library,
    colour_lookup_choice,
    camera_direction,
):
    devices = lax.axis_size("depth")
    counts, choice, camera, library, field0, own_rows, *messages = first_kernel(
        active_sheet_number,
        colour_lookup_choice,
        camera_direction,
        thermal_values,
        reactant_fraction,
        colour_lookup_library,
    )
    rows_gap = swapped(messages[1], "lat", 1)
    rows_pair = swapped(messages[0], "lat", 0)
    rim_gap = swapped(messages[3], "depth", 1)
    rim_pair = swapped(messages[2], "depth", 0)
    next_pair, next_gap = rim_kernel(counts, rows_pair, rows_gap, rim_pair, rim_gap)
    next_gap = swapped(next_gap, "depth", 1)
    next_pair = swapped(next_pair, "depth", 0)
    field0, field1, edge0, edge1, low_table, rise_table = inner_kernel(
        devices,
        counts,
        choice,
        camera,
        field0,
        library,
        own_rows,
        rows_pair,
        rows_gap,
        rim_pair,
        rim_gap,
    )
    theta_next, fuel_next, pieces = outer_kernel(
        devices,
        counts,
        camera,
        field0,
        field1,
        edge0,
        edge1,
        low_table,
        rise_table,
        own_rows,
        rim_pair,
        rim_gap,
        next_pair,
        next_gap,
    )
    pieces = lax.all_to_all(pieces, "depth", 0, 0, tiled=True)
    image = last_kernel(colour_lookup_choice.shape[0], camera, pieces)
    return (theta_next, fuel_next, image)


def solution(mesh):
    placed = (P("depth", "lat", None), P("depth", "lat", None), P("depth"), P(), P(), P())
    return jax.shard_map(
        on_device,
        mesh=mesh,
        in_specs=placed,
        out_specs=(P("depth", "lat", None), P("depth", "lat", None), P(None, None, "lat", "depth")),
        check_vma=False,
    )
```

```python
import functools

import jax
import jax.numpy as jnp
from jax import lax
from jax.experimental import pallas as pl
from jax.experimental.pallas import tpu as pltpu
from jax.sharding import PartitionSpec as P

MEAN_DEPTH = 32
STEPS = 2

time_step = 0.03
heat_release = 2.0
zeldovich = 8.0
expansion = 0.8

VMEM = pltpu.VMEM
SMEM = pltpu.SMEM
F32 = jnp.float32


def in_vmem():
    return pl.BlockSpec(memory_space=VMEM)


def in_smem():
    return pl.BlockSpec(memory_space=SMEM)


UNROLL_1 = 16
UNROLL_EARLY = 16
UNROLL_MIDDLE = 22
EARLY = 16


def is_even(axis):
    return lax.rem(lax.axis_index(axis), 2) == 0


def select(which, first, second):
    return jnp.where(which, first, second)


def pack_rows(
    counts_in,
    choice_in,
    camera_in,
    theta,
    fuel,
    library_in,
    counts,
    choice,
    camera,
    library,
    field0,
    own_rows,
    rows_pair,
    rows_gap,
    rim_pair,
    rim_gap,
    copies,
):
    places = theta.shape[0]
    moves = [
        (counts_in, counts),
        (theta, field0.at[0, pl.ds(2, places)]),
        (fuel, field0.at[1, pl.ds(2, places)]),
        (choice_in, choice),
        (camera_in, camera),
        (library_in, library),
    ]
    fetch = [
        pltpu.make_async_copy(source, target, copies.at[number])
        for number, (source, target) in enumerate(moves)
    ]
    for copy in fetch:
        copy.start()
    lat_even, depth_even = is_even("lat"), is_even("depth")
    for number in range(2):
        fetch[1 + number].wait()
        for row in range(2):
            low = field0[number, 2 : places + 2, row, :]
            high = field0[number, 2 : places + 2, 6 + row, :]
            rows_pair[2 * number + row] = select(lat_even, high, low)
            rows_gap[2 * number + row] = select(lat_even, low, high)
            own_rows[2 * row + number] = (low, high)[row]
    fetch[0].wait()
    depth_count = counts[0]
    last = depth_count + 1
    second_last = jnp.maximum(depth_count, 2)
    second = jnp.minimum(3, last)
    size = jnp.broadcast_to(depth_count.astype(F32), (8, 128))
    for number in range(2):
        up = (field0[number, last], field0[number, second_last], size)
        down = (field0[number, 2], field0[number, second], size)
        for layer in range(3):
            rim_pair[number, layer] = select(depth_even, up[layer], down[layer])
            rim_gap[number, layer] = select(depth_even, down[layer], up[layer])
    for copy in fetch[3:]:
        copy.wait()


def pack_rims(counts, rows_pair, rows_gap, rim_pair, rim_gap, order, next_pair, next_gap):
    last = counts[0] - 1
    lat_even, depth_even = is_even("lat"), is_even("depth")
    for number in range(2):
        from_above = select(depth_even, rim_pair[number, 0], rim_gap[number, 0])
        from_below = select(depth_even, rim_gap[number, 0], rim_pair[number, 0])

        def beside(place):
            below = [ref[2 * number + 1, pl.ds(place, 1), :] for ref in (rows_gap, rows_pair)]
            above = [ref[2 * number, pl.ds(place, 1), :] for ref in (rows_pair, rows_gap)]
            rows = [select(lat_even, *below), select(lat_even, *above)]
            return jnp.where(sublanes() == 0, *(jnp.broadcast_to(x, (8, 128)) for x in rows))

        up = (from_below, beside(last))
        down = (from_above, beside(0))
        for layer in range(2):
            next_pair[number, layer] = select(depth_even, up[layer], down[layer])
            next_gap[number, layer] = select(depth_even, down[layer], up[layer])


def lanes():
    return lax.broadcasted_iota(jnp.int32, (8, 128), 1)


def sublanes():
    return lax.broadcasted_iota(jnp.int32, (8, 128), 0)


def left_of(x):
    return jnp.where(lanes() == 0, 0.0, pltpu.roll(x, 1, 1))


def right_of(x):
    return jnp.where(lanes() == 127, 0.0, pltpu.roll(x, 127, 1))


def row_below(x, halo_row):
    return jnp.where(sublanes() == 0, jnp.broadcast_to(halo_row, (8, 128)), pltpu.roll(x, 1, 0))


def row_above(x, halo_row):
    return jnp.where(sublanes() == 7, jnp.broadcast_to(halo_row, (8, 128)), pltpu.roll(x, 7, 0))


def stepped(heat, fuel, neighbours):
    heat_sum = neighbours[0][0]
    fuel_sum = neighbours[0][1]
    product_sum = neighbours[0][0] * neighbours[0][1]
    square_sum = neighbours[0][0] * neighbours[0][0]
    for heat_n, fuel_n in neighbours[1:]:
        heat_sum = heat_sum + heat_n
        fuel_sum = fuel_sum + fuel_n
        product_sum = product_sum + heat_n * fuel_n
        square_sum = square_sum + heat_n * heat_n
    heat_flux = (heat_sum - 6.0 * heat) + 1.5 * (square_sum - 6.0 * (heat * heat))
    fuel_flux = 0.5 * (
        (1.0 + 1.5 * heat) * (fuel_sum - 6.0 * fuel) + 1.5 * (product_sum - fuel * heat_sum)
    )
    ratio = zeldovich / expansion
    reaction = fuel * jnp.exp(ratio - ratio / ((1.0 - expansion) + expansion * heat))
    return (
        heat + time_step * (heat_flux + heat_release * reaction),
        fuel + time_step * (fuel_flux - reaction),
    )


LEAD = 8


def block_step(field, at, count, edge_rows):
    heat = [field[0, at - 1 + j] for j in range(count + 2)]
    burn = [field[1, at - 1 + j] for j in range(count + 2)]
    results = []
    for j in range(1, count + 1):
        h, b = heat[j], burn[j]
        (h_low, b_low), (h_high, b_high) = edge_rows(j - 1)
        around = [
            (heat[j - 1], burn[j - 1]),
            (heat[j + 1], burn[j + 1]),
            (row_below(h, h_low), row_below(b, b_low)),
            (row_above(h, h_high), row_above(b, b_high)),
            (left_of(h), left_of(b)),
            (right_of(h), right_of(b)),
        ]
        results.append(stepped(h, b, around))
    return results


def rows_beside(edge, sides, place):
    return [tuple(edge[n, side, pl.ds(place, 1), :] for n in range(2)) for side in sides]


def step_edges(edge0, inner, side, at, inner_at, count):
    edge_row = 1 + side
    outer_row = 3 * side

    def rows(ref, row, place):
        found = tuple(ref(n)[row(n), pl.ds(place, count), :] for n in range(2))
        return tuple(jnp.broadcast_to(x, (8, 128)) for x in found)

    def edge(row, shift):
        return rows(lambda n: edge0.at[n], lambda n: row, at + shift)

    heat, burn = edge(edge_row, 0)
    around = [
        edge(edge_row, -1),
        edge(edge_row, 1),
        edge(outer_row, 0),
        rows(lambda n: inner, lambda n: 2 * side + n, inner_at),
        (left_of(heat), left_of(burn)),
        (right_of(heat), right_of(burn)),
    ]
    outside = lax.axis_index("lat") == (0 if side == 0 else lax.axis_size("lat") - 1)
    return [jnp.where(outside, 0.0, x) for x in stepped(heat, burn, around)]


def look_up(low_table, rise_table, value):
    bins = low_table.shape[2]
    position = jnp.clip(value, 0.0, 1.0) * (bins - 1)
    lower = jnp.minimum(position.astype(jnp.int32), bins - 2)
    fraction = position - lower.astype(F32)

    def at(entry):
        low = jnp.take_along_axis(low_table[entry], lower, axis=1)
        rise = jnp.take_along_axis(rise_table[entry], lower, axis=1)
        return low + fraction * rise

    return at


def add_layer(sums, number, at, alive):
    for f in range(2 * number, 2 * number + 2):
        gone, red, green, blue = sums[4 * f : 4 * f + 4]
        depth = jnp.where(alive, at(4 * f + 3), 0.0)
        gain = depth * (1.0 + depth * (0.5 + depth * (1.0 / 6.0)))
        gain = gain + gone * gain
        sums[4 * f] = gone + gain
        sums[4 * f + 1] = red + gain * at(4 * f)
        sums[4 * f + 2] = green + gain * at(4 * f + 1)
        sums[4 * f + 3] = blue + gain * at(4 * f + 2)


def inner_layers(
    first, count, unroll, depth_count, field1, edge1, tables, results, sums, after=None
):
    def body(block, carry):
        start = first + block * unroll

        def edge_rows(j):
            return rows_beside(edge1, (0, 1), start + j)

        carry = list(carry)
        for j, new in enumerate(block_step(field1, start + 1, unroll, edge_rows)):
            for number in range(2):
                value = jnp.where(start + j < depth_count, new[number], 0.0)
                results[number][start + j] = value
                add_layer(carry, number, look_up(*tables, value), start + j < depth_count - 2)
        if after is not None:
            after(start, unroll)
        return tuple(carry)

    return lax.fori_loop(0, count // unroll, body, tuple(sums))


def early_step(
    places,
    functions,
    all_layers,
    counts,
    choice,
    camera,
    field0,
    library,
    own_rows,
    rows_pair,
    rows_gap,
    field1,
    edge0,
    edge1,
    low_table,
    rise_table,
    theta_next,
    fuel_next,
    sums,
    tables,
):
    lat_even = is_even("lat")
    bins = library.shape[2]
    tables[...] = library[...].astype(F32)
    per_cell = 3.0 / all_layers
    for f in range(functions):
        sign = jnp.where(camera[f] == 0, -per_cell, per_cell)
        for c in range(4):
            low = jnp.broadcast_to(tables[choice[f], c : c + 1, :], (8, bins))
            rise = pltpu.roll(low, bins - 1, 1) - low
            if c == 3:
                low = low * sign
                rise = rise * sign
            low_table[4 * f + c] = low
            rise_table[4 * f + c] = rise

    for number in range(2):
        for row in range(2):
            pair, gap = rows_pair[2 * number + row], rows_gap[2 * number + row]
            edge0[number, row, LEAD : LEAD + places] = select(lat_even, gap, pair)
            edge0[number, 2 + row, LEAD : LEAD + places] = select(lat_even, pair, gap)

    for block in range(places // 8):
        for side in range(2):
            fresh = step_edges(edge0, own_rows, side, LEAD + 8 * block, 8 * block, 8)
            for number in range(2):
                edge1[number, side, 8 * block : 8 * block + 8] = fresh[number]

    def first_step(block, carry):
        start = block * UNROLL_1

        def edge_rows(j):
            return rows_beside(edge0, (1, 2), LEAD + start + j)

        for j, new in enumerate(block_step(field0, start + 2, UNROLL_1, edge_rows)):
            for number in range(2):
                field1[number, start + 1 + j] = new[number]
        return carry

    lax.fori_loop(0, places // UNROLL_1, first_step, 0)
    zero = jnp.zeros((8, 128), F32)
    for out in (theta_next, fuel_next):
        for place in (0, 1, places - 2, places - 1):
            out[place] = zero
    found = inner_layers(
        2,
        EARLY,
        UNROLL_EARLY,
        counts[0],
        field1,
        edge1,
        (low_table, rise_table),
        (theta_next, fuel_next),
        [zero] * (4 * functions),
    )
    for entry, value in enumerate(found):
        sums[entry] = value


def middle_step(
    places,
    counts,
    field1,
    edge1,
    low_table,
    rise_table,
    order,
    theta_in,
    fuel_in,
    sums_in,
    theta_out,
    fuel_out,
    theta_next,
    fuel_next,
    sums,
    copies,
):
    def leave(number, first, count):
        return pltpu.make_async_copy(
            (theta_next, fuel_next)[number].at[pl.ds(first, count)],
            (theta_out, fuel_out)[number].at[pl.ds(first, count)],
            copies.at[number],
        )

    def start_leaving(first, count):
        for number in range(2):
            leave(number, first, count).start()

    start_leaving(0, 2 + EARLY)
    start_leaving(places - 2, 2)
    found = inner_layers(
        2 + EARLY,
        places - 4 - EARLY,
        UNROLL_MIDDLE,
        counts[0],
        field1,
        edge1,
        (low_table, rise_table),
        (theta_next, fuel_next),
        [sums_in[entry] for entry in range(sums_in.shape[0])],
        start_leaving,
    )
    for entry, value in enumerate(found):
        sums[entry] = value
    for number in range(2):
        leave(number, 0, places).wait()


def late_step(
    functions,
    counts,
    camera,
    field0_in,
    field1_in,
    edge0_in,
    edge1_in,
    low_table,
    rise_table,
    sums,
    own_rows,
    rim_pair,
    rim_gap,
    next_pair,
    next_gap,
    image,
    ends,
    field0,
    field1,
    edge0,
    edge1,
):
    depth_count = counts[0]
    depth_even = is_even("depth")

    def from_below(pair, gap, *at):
        return select(depth_even, gap[at], pair[at])

    def from_above(pair, gap, *at):
        return select(depth_even, pair[at], gap[at])

    below_size = from_below(rim_pair, rim_gap, 0, 2)
    above_size = from_above(rim_pair, rim_gap, 0, 2)
    for number in range(2):
        field0[number, 0] = jnp.where(
            below_size == 1.0,
            from_below(next_pair, next_gap, number, 0),
            from_below(rim_pair, rim_gap, number, 1),
        )
        field0[number, 1] = from_below(rim_pair, rim_gap, number, 0)
        field0[number, depth_count + 2] = from_above(rim_pair, rim_gap, number, 0)
        field0[number, depth_count + 3] = jnp.where(
            above_size == 1.0,
            from_above(next_pair, next_gap, number, 0),
            from_above(rim_pair, rim_gap, number, 1),
        )
        below_rows = from_below(next_pair, next_gap, number, 1)
        above_rows = from_above(next_pair, next_gap, number, 1)
        for side in range(2):
            edge0[number, 1 + side, LEAD - 1 : LEAD] = below_rows[side : side + 1]
            edge0[number, 1 + side, pl.ds(LEAD + depth_count, 1)] = above_rows[side : side + 1]
    for place in (0, depth_count - 1):
        for side in range(2):
            fresh = step_edges(edge0, own_rows, side, LEAD + place, place, 1)
            for number in range(2):
                edge1[number, side, pl.ds(place, 1)] = fresh[number][0:1]
    for place, size in (
        (-1, below_size),
        (0, None),
        (depth_count - 1, None),
        (depth_count, above_size),
    ):

        def edge_rows(j, place=place):
            return rows_beside(edge0, (1, 2), LEAD + place)

        (fresh,) = block_step(field0, place + 2, 1, edge_rows)
        for number in range(2):
            value = fresh[number]
            field1[number, place + 1] = (
                value if size is None else jnp.where(size > 0.0, value, 0.0)
            )

    zero = jnp.zeros((8, 128), F32)
    segments = []
    for slot, start in ((0, 0), (2, jnp.maximum(depth_count - 2, 2))):

        def edge_rows(j, start=start):
            return rows_beside(edge1, (0, 1), start + j)

        segment = [zero] * (4 * functions)
        for j, new in enumerate(block_step(field1, start + 1, 2, edge_rows)):
            place = start + j
            alive = place < depth_count
            for number in range(2):
                value = jnp.where(alive, new[number], 0.0)
                ends[number, slot + j] = value
                at = look_up(low_table, rise_table, value)
                add_layer(segment, number, at, alive)
        segments.append(segment)

    head, tail = segments
    channels = []
    for f in range(functions):
        through_head = 1.0 + head[4 * f]
        through_body = 1.0 + sums[4 * f]
        gone, red, green, blue = [
            head[4 * f + c]
            + through_head * (sums[4 * f + c] + through_body * tail[4 * f + c])
            for c in range(4)
        ]
        scale = jnp.where(camera[f] == 0, -1.0, 1.0 / (1.0 + gone))
        channels += [red * scale, green * scale, blue * scale, gone * scale]

    group = lanes() // 16
    for half in range(2):
        regs = channels[8 * half : 8 * half + 8]
        for bit in (1, 2, 4):
            upper = (group & bit) != 0
            fresh = list(regs)
            for i in range(8):
                if i & bit:
                    continue
                a, b = regs[i], regs[i | bit]
                fresh[i] = jnp.where(upper, pltpu.roll(b, 16 * bit, 1), a)
                fresh[i | bit] = jnp.where(upper, b, pltpu.roll(a, 128 - 16 * bit, 1))
            regs = fresh
        for g in range(8):
            image[pl.ds(2 * g + half, 8, stride=16), :] = regs[g]


def place_ends(counts, ends, theta_in, fuel_in, theta_next, fuel_next, copies):
    leave = [
        pltpu.make_async_copy(
            ends.at[number, pl.ds(slot, 2)], out.at[pl.ds(place, 2)], copies.at[number, slot // 2]
        )
        for number, out in enumerate((theta_next, fuel_next))
        for slot, place in ((0, 0), (2, jnp.maximum(counts[0] - 2, 2)))
    ]
    for copy in leave:
        copy.start()
    for copy in leave:
        copy.wait()


def composite(camera, pieces, image):
    sources = pieces.shape[0] // 2
    lane = lanes()
    row = sublanes()
    opacity_lane = lane // 64 * 64 + 48 + lane % 16
    for half in range(2):
        forward = jnp.where(
            lane < 64,
            (camera[2 * half] == 0).astype(jnp.int32),
            (camera[2 * half + 1] == 0).astype(jnp.int32),
        ) == 1
        values, clear, through = [], [], []
        carry = jnp.ones((8, 128), F32)
        for block in range(sources // 8):
            value = pieces[pl.ds(16 * block + half, 8, stride=2), :]
            passing = 1.0 - jnp.take_along_axis(value, opacity_lane, axis=1)
            product = passing
            for shift in (1, 2, 4):
                product = product * jnp.where(row >= shift, pltpu.roll(product, shift, 0), 1.0)
            product = product * carry
            carry = jnp.broadcast_to(product[7:8], (8, 128))
            values.append(value)
            clear.append(passing)
            through.append(product)
        total = jnp.zeros((8, 128), F32)
        for value, passing, product in zip(values, clear, through):
            top = jnp.where(forward, product, carry)
            bottom = jnp.where(forward, passing, product)
            total = total + value * (top / bottom)
        line = jnp.sum(total, axis=0, keepdims=True)
        for clo in range(8):
            channel = 8 * half + clo
            image[channel // 4, channel % 4] = line[:, 16 * clo : 16 * clo + 16]


def swapped(array, axis, first):
    count = lax.axis_size(axis)
    pairs = []
    for i in range(first, count - 1, 2):
        pairs += [(i, i + 1), (i + 1, i)]
    return lax.ppermute(array, axis, pairs)


def held(array):
    return pltpu.with_memory_space_constraint(array, VMEM)


def in_hbm(array):
    return pltpu.with_memory_space_constraint(array, pltpu.HBM)


def params():
    return pltpu.CompilerParams(vmem_limit_bytes=16 * 1024 * 1024)


def anywhere():
    return pl.BlockSpec(memory_space=pl.ANY)


def in_scalars(array):
    return pltpu.with_memory_space_constraint(array, SMEM)


def first_kernel(counts, choice, camera, theta, fuel, library):
    places = theta.shape[0]
    rows = VMEM((4, places, 128), F32)
    rim = VMEM((2, 3, 8, 128), F32)
    return pl.pallas_call(
        pack_rows,
        out_shape=tuple(SMEM(x.shape, jnp.int32) for x in (counts, choice, camera))
        + (VMEM(library.shape, library.dtype), VMEM((2, places + 4, 8, 128), F32))
        + (rows, rows, rows, rim, rim),
        in_specs=[anywhere()] * 6,
        out_specs=(in_smem(),) * 3 + (in_vmem(),) * 7,
        scratch_shapes=[pltpu.SemaphoreType.DMA((6,))],
        compiler_params=params(),
        name="pack_rows",
    )(counts, *map(in_hbm, (choice, camera, theta, fuel, library)))


def rim_kernel(counts, *received):
    rim = VMEM((2, 2, 8, 128), F32)
    return pl.pallas_call(
        pack_rims,
        out_shape=(rim, rim),
        in_specs=[in_smem()] + [in_vmem()] * len(received),
        out_specs=(in_vmem(),) * 2,
        compiler_params=params(),
        name="pack_rims",
    )(in_scalars(counts), *map(held, received))


def cost(flops):
    return pl.CostEstimate(flops=flops, bytes_accessed=10**6, transcendentals=10**5)


def early_kernel(devices, counts, choice, camera, field0, library, *rows):
    places = field0.shape[1] - 4
    functions = choice.shape[0]
    bins = library.shape[2]
    table = VMEM((4 * functions, 8, bins), F32)
    field = VMEM((places, 8, 128), F32)
    return pl.pallas_call(
        functools.partial(early_step, places, functions, float(MEAN_DEPTH * devices)),
        out_shape=(
            VMEM((2, places + 2, 8, 128), F32),
            VMEM((2, 4, places + 16, 128), F32),
            VMEM((2, 2, places, 128), F32),
            table,
            table,
            field,
            field,
            VMEM((4 * functions, 8, 128), F32),
        ),
        in_specs=[in_smem()] * 3 + [in_vmem()] * 5,
        out_specs=(in_vmem(),) * 8,
        scratch_shapes=[VMEM(library.shape, F32)],
        compiler_params=params(),
        cost_estimate=cost(10**7),
        name="early_step",
    )(*map(in_scalars, (counts, choice, camera)), *map(held, (field0, library, *rows)))


def middle_kernel(counts, *arrays):
    theta_next, fuel_next, sums = arrays[-3:]
    field = jax.ShapeDtypeStruct(theta_next.shape, F32)
    return pl.pallas_call(
        functools.partial(middle_step, theta_next.shape[0]),
        out_shape=(field, field) + tuple(VMEM(x.shape, F32) for x in (theta_next, fuel_next, sums)),
        in_specs=[in_smem()] + [in_vmem()] * len(arrays),
        out_specs=(anywhere(),) * 2 + (in_vmem(),) * 3,
        scratch_shapes=[pltpu.SemaphoreType.DMA((2,))],
        input_output_aliases={len(arrays) - 2 + i: 2 + i for i in range(2)},
        compiler_params=params(),
        cost_estimate=cost(10**7),
        name="middle_step",
    )(in_scalars(counts), *map(held, arrays))


def late_kernel(devices, counts, camera, *arrays):
    functions = camera.shape[0]
    kept = arrays[:4]
    image, ends, *_ = pl.pallas_call(
        functools.partial(late_step, functions),
        out_shape=(VMEM((2 * devices, 128), F32), VMEM((2, 4, 8, 128), F32))
        + tuple(VMEM(x.shape, F32) for x in kept),
        in_specs=[in_smem()] * 2 + [in_vmem()] * len(arrays),
        out_specs=(in_vmem(),) * 6,
        input_output_aliases={2 + i: 2 + i for i in range(4)},
        compiler_params=params(),
        cost_estimate=cost(10**6),
        name="late_step",
    )(*map(in_scalars, (counts, camera)), *map(held, arrays))
    return image, ends


def end_kernel(counts, ends, *fields):
    field = jax.ShapeDtypeStruct(fields[0].shape, F32)
    return pl.pallas_call(
        place_ends,
        out_shape=(field, field),
        in_specs=[in_smem(), in_vmem()] + [anywhere()] * 2,
        out_specs=(anywhere(),) * 2,
        scratch_shapes=[pltpu.SemaphoreType.DMA((2, 2))],
        input_output_aliases={2: 0, 3: 1},
        compiler_params=params(),
        cost_estimate=cost(10**6),
        name="place_ends",
    )(in_scalars(counts), held(ends), *map(in_hbm, fields))


def last_kernel(functions, camera, pieces):
    return pl.pallas_call(
        composite,
        out_shape=jax.ShapeDtypeStruct((functions, 4, 1, 16), F32),
        in_specs=[in_smem(), in_vmem()],
        out_specs=in_vmem(),
        compiler_params=params(),
        name="composite",
    )(in_scalars(camera), held(pieces))


def on_device(
    thermal_values,
    reactant_fraction,
    active_sheet_number,
    colour_lookup_library,
    colour_lookup_choice,
    camera_direction,
):
    devices = lax.axis_size("depth")
    counts, choice, camera, library, field0, own_rows, *messages = first_kernel(
        active_sheet_number,
        colour_lookup_choice,
        camera_direction,
        thermal_values,
        reactant_fraction,
        colour_lookup_library,
    )
    rows_gap = swapped(messages[1], "lat", 1)
    rows_pair = swapped(messages[0], "lat", 0)
    rim_gap = swapped(messages[3], "depth", 1)
    rim_pair = swapped(messages[2], "depth", 0)
    field1, edge0, edge1, low_table, rise_table, theta_next, fuel_next, sums = early_kernel(
        devices, counts, choice, camera, field0, library, own_rows, rows_pair, rows_gap
    )
    next_pair, next_gap = rim_kernel(counts, rows_pair, rows_gap, rim_pair, rim_gap, sums)
    order = next_pair
    next_gap = swapped(next_gap, "depth", 1)
    next_pair = swapped(next_pair, "depth", 0)
    theta_next, fuel_next, _, _, sums = middle_kernel(
        counts, field1, edge1, low_table, rise_table, order, theta_next, fuel_next, sums
    )
    pieces, ends = late_kernel(
        devices,
        counts,
        camera,
        field0,
        field1,
        edge0,
        edge1,
        low_table,
        rise_table,
        sums,
        own_rows,
        rim_pair,
        rim_gap,
        next_pair,
        next_gap,
    )
    pieces = lax.all_to_all(pieces, "depth", 0, 0, tiled=True)
    theta_next, fuel_next = end_kernel(counts, ends, theta_next, fuel_next)
    image = last_kernel(choice.shape[0], camera, pieces)
    return (theta_next, fuel_next, image)


def solution(mesh):
    placed = (P("depth", "lat", None), P("depth", "lat", None), P("depth"), P(), P(), P())
    return jax.shard_map(
        on_device,
        mesh=mesh,
        in_specs=placed,
        out_specs=(P("depth", "lat", None), P("depth", "lat", None), P(None, None, "lat", "depth")),
        check_vma=False,
    )
```

```python
import functools

import jax
import jax.numpy as jnp
from jax import lax
from jax.experimental import pallas as pl
from jax.experimental.pallas import tpu as pltpu
from jax.sharding import PartitionSpec as P

MEAN_DEPTH = 32
STEPS = 2

time_step = 0.03
heat_release = 2.0
zeldovich = 8.0
expansion = 0.8

VMEM = pltpu.VMEM
SMEM = pltpu.SMEM
F32 = jnp.float32


def in_vmem():
    return pl.BlockSpec(memory_space=VMEM)


def in_smem():
    return pl.BlockSpec(memory_space=SMEM)


UNROLL_1 = 16
UNROLL_EARLY = 14
UNROLL_MIDDLE = 16
EARLY = 28


def is_even(axis):
    return lax.rem(lax.axis_index(axis), 2) == 0


def select(which, first, second):
    return jnp.where(which, first, second)


def pack_rows(
    counts_in,
    choice_in,
    camera_in,
    theta,
    fuel,
    library_in,
    counts,
    choice,
    camera,
    library,
    field0,
    own_rows,
    rows_pair,
    rows_gap,
    rim_pair,
    rim_gap,
    copies,
):
    places = theta.shape[0]
    moves = [
        (counts_in, counts),
        (theta, field0.at[0, pl.ds(2, places)]),
        (fuel, field0.at[1, pl.ds(2, places)]),
        (choice_in, choice),
        (camera_in, camera),
        (library_in, library),
    ]
    fetch = [
        pltpu.make_async_copy(source, target, copies.at[number])
        for number, (source, target) in enumerate(moves)
    ]
    for copy in fetch:
        copy.start()
    lat_even, depth_even = is_even("lat"), is_even("depth")
    for number in range(2):
        fetch[1 + number].wait()
        for row in range(2):
            low = field0[number, 2 : places + 2, row, :]
            high = field0[number, 2 : places + 2, 6 + row, :]
            rows_pair[2 * number + row] = select(lat_even, high, low)
            rows_gap[2 * number + row] = select(lat_even, low, high)
            own_rows[2 * row + number] = (low, high)[row]
    fetch[0].wait()
    depth_count = counts[0]
    last = depth_count + 1
    second_last = jnp.maximum(depth_count, 2)
    second = jnp.minimum(3, last)
    size = jnp.broadcast_to(depth_count.astype(F32), (8, 128))
    for number in range(2):
        up = (field0[number, last], field0[number, second_last], size)
        down = (field0[number, 2], field0[number, second], size)
        for layer in range(3):
            rim_pair[number, layer] = select(depth_even, up[layer], down[layer])
            rim_gap[number, layer] = select(depth_even, down[layer], up[layer])
    for copy in fetch[3:]:
        copy.wait()


def pack_rims(counts, rows_pair, rows_gap, rim_pair, rim_gap, order, next_pair, next_gap):
    last = counts[0] - 1
    lat_even, depth_even = is_even("lat"), is_even("depth")
    for number in range(2):
        from_above = select(depth_even, rim_pair[number, 0], rim_gap[number, 0])
        from_below = select(depth_even, rim_gap[number, 0], rim_pair[number, 0])

        def beside(place):
            below = [ref[2 * number + 1, pl.ds(place, 1), :] for ref in (rows_gap, rows_pair)]
            above = [ref[2 * number, pl.ds(place, 1), :] for ref in (rows_pair, rows_gap)]
            rows = [select(lat_even, *below), select(lat_even, *above)]
            return jnp.where(sublanes() == 0, *(jnp.broadcast_to(x, (8, 128)) for x in rows))

        up = (from_below, beside(last))
        down = (from_above, beside(0))
        for layer in range(2):
            next_pair[number, layer] = select(depth_even, up[layer], down[layer])
            next_gap[number, layer] = select(depth_even, down[layer], up[layer])


def lanes():
    return lax.broadcasted_iota(jnp.int32, (8, 128), 1)


def sublanes():
    return lax.broadcasted_iota(jnp.int32, (8, 128), 0)


def left_of(x):
    return jnp.where(lanes() == 0, 0.0, pltpu.roll(x, 1, 1))


def right_of(x):
    return jnp.where(lanes() == 127, 0.0, pltpu.roll(x, 127, 1))


def row_below(x, halo_row):
    return jnp.where(sublanes() == 0, jnp.broadcast_to(halo_row, (8, 128)), pltpu.roll(x, 1, 0))


def row_above(x, halo_row):
    return jnp.where(sublanes() == 7, jnp.broadcast_to(halo_row, (8, 128)), pltpu.roll(x, 7, 0))


def stepped(heat, fuel, neighbours):
    heat_sum = neighbours[0][0]
    fuel_sum = neighbours[0][1]
    product_sum = neighbours[0][0] * neighbours[0][1]
    square_sum = neighbours[0][0] * neighbours[0][0]
    for heat_n, fuel_n in neighbours[1:]:
        heat_sum = heat_sum + heat_n
        fuel_sum = fuel_sum + fuel_n
        product_sum = product_sum + heat_n * fuel_n
        square_sum = square_sum + heat_n * heat_n
    heat_flux = (heat_sum - 6.0 * heat) + 1.5 * (square_sum - 6.0 * (heat * heat))
    fuel_flux = 0.5 * (
        (1.0 + 1.5 * heat) * (fuel_sum - 6.0 * fuel) + 1.5 * (product_sum - fuel * heat_sum)
    )
    ratio = zeldovich / expansion
    reaction = fuel * jnp.exp(ratio - ratio / ((1.0 - expansion) + expansion * heat))
    return (
        heat + time_step * (heat_flux + heat_release * reaction),
        fuel + time_step * (fuel_flux - reaction),
    )


LEAD = 8


def block_step(field, at, count, edge_rows):
    heat = [field[0, at - 1 + j] for j in range(count + 2)]
    burn = [field[1, at - 1 + j] for j in range(count + 2)]
    results = []
    for j in range(1, count + 1):
        h, b = heat[j], burn[j]
        (h_low, b_low), (h_high, b_high) = edge_rows(j - 1)
        around = [
            (heat[j - 1], burn[j - 1]),
            (heat[j + 1], burn[j + 1]),
            (row_below(h, h_low), row_below(b, b_low)),
            (row_above(h, h_high), row_above(b, b_high)),
            (left_of(h), left_of(b)),
            (right_of(h), right_of(b)),
        ]
        results.append(stepped(h, b, around))
    return results


def rows_beside(edge, sides, place):
    return [tuple(edge[n, side, pl.ds(place, 1), :] for n in range(2)) for side in sides]


def step_edges(edge0, inner, side, at, inner_at, count):
    edge_row = 1 + side
    outer_row = 3 * side

    def rows(ref, row, place):
        found = tuple(ref(n)[row(n), pl.ds(place, count), :] for n in range(2))
        return tuple(jnp.broadcast_to(x, (8, 128)) for x in found)

    def edge(row, shift):
        return rows(lambda n: edge0.at[n], lambda n: row, at + shift)

    heat, burn = edge(edge_row, 0)
    around = [
        edge(edge_row, -1),
        edge(edge_row, 1),
        edge(outer_row, 0),
        rows(lambda n: inner, lambda n: 2 * side + n, inner_at),
        (left_of(heat), left_of(burn)),
        (right_of(heat), right_of(burn)),
    ]
    outside = lax.axis_index("lat") == (0 if side == 0 else lax.axis_size("lat") - 1)
    return [jnp.where(outside, 0.0, x) for x in stepped(heat, burn, around)]


def look_up(low_table, rise_table, value):
    bins = low_table.shape[2]
    position = jnp.clip(value, 0.0, 1.0) * (bins - 1)
    lower = jnp.minimum(position.astype(jnp.int32), bins - 2)
    fraction = position - lower.astype(F32)

    def at(entry):
        low = jnp.take_along_axis(low_table[entry], lower, axis=1)
        rise = jnp.take_along_axis(rise_table[entry], lower, axis=1)
        return low + fraction * rise

    return at


def add_layer(sums, number, at, alive):
    for f in range(2 * number, 2 * number + 2):
        gone, red, green, blue = sums[4 * f : 4 * f + 4]
        depth = jnp.where(alive, at(4 * f + 3), 0.0)
        gain = depth * (1.0 + depth * (0.5 + depth * (1.0 / 6.0)))
        gain = gain + gone * gain
        sums[4 * f] = gone + gain
        sums[4 * f + 1] = red + gain * at(4 * f)
        sums[4 * f + 2] = green + gain * at(4 * f + 1)
        sums[4 * f + 3] = blue + gain * at(4 * f + 2)


def inner_layers(
    first, count, unroll, depth_count, field1, edge1, tables, results, sums, after=None
):
    def body(block, carry):
        start = first + block * unroll

        def edge_rows(j):
            return rows_beside(edge1, (0, 1), start + j)

        carry = list(carry)
        for j, new in enumerate(block_step(field1, start + 1, unroll, edge_rows)):
            for number in range(2):
                value = jnp.where(start + j < depth_count, new[number], 0.0)
                results[number][start + j] = value
                add_layer(carry, number, look_up(*tables, value), start + j < depth_count - 2)
        if after is not None:
            after(start, unroll)
        return tuple(carry)

    return lax.fori_loop(0, count // unroll, body, tuple(sums))


def early_step(
    places,
    functions,
    all_layers,
    counts,
    choice,
    camera,
    field0,
    library,
    own_rows,
    rows_pair,
    rows_gap,
    field1,
    edge0,
    edge1,
    low_table,
    rise_table,
    theta_next,
    fuel_next,
    sums,
    tables,
):
    lat_even = is_even("lat")
    bins = library.shape[2]
    tables[...] = library[...].astype(F32)
    per_cell = 3.0 / all_layers
    for f in range(functions):
        sign = jnp.where(camera[f] == 0, -per_cell, per_cell)
        for c in range(4):
            low = jnp.broadcast_to(tables[choice[f], c : c + 1, :], (8, bins))
            rise = pltpu.roll(low, bins - 1, 1) - low
            if c == 3:
                low = low * sign
                rise = rise * sign
            low_table[4 * f + c] = low
            rise_table[4 * f + c] = rise

    for number in range(2):
        for row in range(2):
            pair, gap = rows_pair[2 * number + row], rows_gap[2 * number + row]
            edge0[number, row, LEAD : LEAD + places] = select(lat_even, gap, pair)
            edge0[number, 2 + row, LEAD : LEAD + places] = select(lat_even, pair, gap)

    for block in range(places // 8):
        for side in range(2):
            fresh = step_edges(edge0, own_rows, side, LEAD + 8 * block, 8 * block, 8)
            for number in range(2):
                edge1[number, side, 8 * block : 8 * block + 8] = fresh[number]

    def first_step(block, carry):
        start = block * UNROLL_1

        def edge_rows(j):
            return rows_beside(edge0, (1, 2), LEAD + start + j)

        for j, new in enumerate(block_step(field0, start + 2, UNROLL_1, edge_rows)):
            for number in range(2):
                field1[number, start + 1 + j] = new[number]
        return carry

    lax.fori_loop(0, places // UNROLL_1, first_step, 0)
    zero = jnp.zeros((8, 128), F32)
    for out in (theta_next, fuel_next):
        for place in (0, 1, places - 2, places - 1):
            out[place] = zero
    found = inner_layers(
        2,
        EARLY,
        UNROLL_EARLY,
        counts[0],
        field1,
        edge1,
        (low_table, rise_table),
        (theta_next, fuel_next),
        [zero] * (4 * functions),
    )
    for entry, value in enumerate(found):
        sums[entry] = value


def middle_step(
    places,
    counts,
    field1,
    edge1,
    low_table,
    rise_table,
    order,
    theta_in,
    fuel_in,
    sums_in,
    theta_out,
    fuel_out,
    theta_next,
    fuel_next,
    sums,
    copies,
):
    def leave(number, first, count):
        return pltpu.make_async_copy(
            (theta_next, fuel_next)[number].at[pl.ds(first, count)],
            (theta_out, fuel_out)[number].at[pl.ds(first, count)],
            copies.at[number],
        )

    def start_leaving(first, count):
        for number in range(2):
            leave(number, first, count).start()

    start_leaving(0, 2 + EARLY)
    start_leaving(places - 2, 2)
    found = inner_layers(
        2 + EARLY,
        places - 4 - EARLY,
        UNROLL_MIDDLE,
        counts[0],
        field1,
        edge1,
        (low_table, rise_table),
        (theta_next, fuel_next),
        [sums_in[entry] for entry in range(sums_in.shape[0])],
        start_leaving,
    )
    for entry, value in enumerate(found):
        sums[entry] = value
    for number in range(2):
        leave(number, 0, places).wait()


def late_step(
    functions,
    counts,
    camera,
    field0_in,
    field1_in,
    edge0_in,
    edge1_in,
    low_table,
    rise_table,
    sums,
    own_rows,
    rim_pair,
    rim_gap,
    next_pair,
    next_gap,
    image,
    ends,
    field0,
    field1,
    edge0,
    edge1,
):
    depth_count = counts[0]
    depth_even = is_even("depth")

    def from_below(pair, gap, *at):
        return select(depth_even, gap[at], pair[at])

    def from_above(pair, gap, *at):
        return select(depth_even, pair[at], gap[at])

    below_size = from_below(rim_pair, rim_gap, 0, 2)
    above_size = from_above(rim_pair, rim_gap, 0, 2)
    for number in range(2):
        field0[number, 0] = jnp.where(
            below_size == 1.0,
            from_below(next_pair, next_gap, number, 0),
            from_below(rim_pair, rim_gap, number, 1),
        )
        field0[number, 1] = from_below(rim_pair, rim_gap, number, 0)
        field0[number, depth_count + 2] = from_above(rim_pair, rim_gap, number, 0)
        field0[number, depth_count + 3] = jnp.where(
            above_size == 1.0,
            from_above(next_pair, next_gap, number, 0),
            from_above(rim_pair, rim_gap, number, 1),
        )
        below_rows = from_below(next_pair, next_gap, number, 1)
        above_rows = from_above(next_pair, next_gap, number, 1)
        for side in range(2):
            edge0[number, 1 + side, LEAD - 1 : LEAD] = below_rows[side : side + 1]
            edge0[number, 1 + side, pl.ds(LEAD + depth_count, 1)] = above_rows[side : side + 1]
    for place in (0, depth_count - 1):
        for side in range(2):
            fresh = step_edges(edge0, own_rows, side, LEAD + place, place, 1)
            for number in range(2):
                edge1[number, side, pl.ds(place, 1)] = fresh[number][0:1]
    for place, size in (
        (-1, below_size),
        (0, None),
        (depth_count - 1, None),
        (depth_count, above_size),
    ):

        def edge_rows(j, place=place):
            return rows_beside(edge0, (1, 2), LEAD + place)

        (fresh,) = block_step(field0, place + 2, 1, edge_rows)
        for number in range(2):
            value = fresh[number]
            field1[number, place + 1] = (
                value if size is None else jnp.where(size > 0.0, value, 0.0)
            )

    zero = jnp.zeros((8, 128), F32)
    pairs = ((0, 0), (2, jnp.maximum(depth_count - 2, 2)))
    stepped_ends = []
    for slot, start in pairs:

        def edge_rows(j, start=start):
            return rows_beside(edge1, (0, 1), start + j)

        fresh = block_step(field1, start + 1, 2, edge_rows)
        alive = [start + j < depth_count for j in range(2)]
        fresh = [[jnp.where(alive[j], value, 0.0) for value in fresh[j]] for j in range(2)]
        stepped_ends.append((alive, fresh))
        for number in range(2):
            for j in range(2):
                ends[number, slot + j] = fresh[j][number]
    segments = []
    for alive, fresh in stepped_ends:
        segment = [zero] * (4 * functions)
        for j in range(2):
            for number in range(2):
                at = look_up(low_table, rise_table, fresh[j][number])
                add_layer(segment, number, at, alive[j])
        segments.append(segment)

    head, tail = segments
    channels = []
    for f in range(functions):
        through_head = 1.0 + head[4 * f]
        through_body = 1.0 + sums[4 * f]
        gone, red, green, blue = [
            head[4 * f + c]
            + through_head * (sums[4 * f + c] + through_body * tail[4 * f + c])
            for c in range(4)
        ]
        scale = jnp.where(camera[f] == 0, -1.0, 1.0 / (1.0 + gone))
        channels += [red * scale, green * scale, blue * scale, gone * scale]

    group = lanes() // 16
    for half in range(2):
        regs = channels[8 * half : 8 * half + 8]
        for bit in (1, 2, 4):
            upper = (group & bit) != 0
            fresh = list(regs)
            for i in range(8):
                if i & bit:
                    continue
                a, b = regs[i], regs[i | bit]
                fresh[i] = jnp.where(upper, pltpu.roll(b, 16 * bit, 1), a)
                fresh[i | bit] = jnp.where(upper, b, pltpu.roll(a, 128 - 16 * bit, 1))
            regs = fresh
        for g in range(8):
            image[pl.ds(2 * g + half, 8, stride=16), :] = regs[g]


def composite(
    counts, camera, pieces, ends, theta_in, fuel_in, image_out, theta_next, fuel_next, image, copies
):
    sources = pieces.shape[0] // 2
    leave = [
        pltpu.make_async_copy(
            ends.at[number, pl.ds(slot, 2)],
            out.at[pl.ds(place, 2)],
            copies.at[slot + number],
        )
        for number, out in enumerate((theta_next, fuel_next))
        for slot, place in ((0, 0), (2, jnp.maximum(counts[0] - 2, 2)))
    ]
    for copy in leave:
        copy.start()
    leave.append(pltpu.make_async_copy(image, image_out, copies.at[4]))
    lane = lanes()
    row = sublanes()
    opacity_lane = lane // 64 * 64 + 48 + lane % 16
    for half in range(2):
        forward = jnp.where(
            lane < 64,
            (camera[2 * half] == 0).astype(jnp.int32),
            (camera[2 * half + 1] == 0).astype(jnp.int32),
        ) == 1
        values, clear, through = [], [], []
        carry = jnp.ones((8, 128), F32)
        for block in range(sources // 8):
            value = pieces[pl.ds(16 * block + half, 8, stride=2), :]
            passing = 1.0 - jnp.take_along_axis(value, opacity_lane, axis=1)
            product = passing
            for shift in (1, 2, 4):
                product = product * jnp.where(row >= shift, pltpu.roll(product, shift, 0), 1.0)
            product = product * carry
            carry = jnp.broadcast_to(product[7:8], (8, 128))
            values.append(value)
            clear.append(passing)
            through.append(product)
        total = jnp.zeros((8, 128), F32)
        for value, passing, product in zip(values, clear, through):
            top = jnp.where(forward, product, carry)
            bottom = jnp.where(forward, passing, product)
            total = total + value * (top / bottom)
        line = jnp.sum(total, axis=0, keepdims=True)
        for clo in range(8):
            channel = 8 * half + clo
            image[channel // 4, channel % 4] = line[:, 16 * clo : 16 * clo + 16]
    leave[-1].start()
    for copy in leave:
        copy.wait()


def swapped(array, axis, first):
    count = lax.axis_size(axis)
    pairs = []
    for i in range(first, count - 1, 2):
        pairs += [(i, i + 1), (i + 1, i)]
    return lax.ppermute(array, axis, pairs)


def held(array):
    return pltpu.with_memory_space_constraint(array, VMEM)


def in_hbm(array):
    return pltpu.with_memory_space_constraint(array, pltpu.HBM)


def params():
    return pltpu.CompilerParams(vmem_limit_bytes=16 * 1024 * 1024)


def anywhere():
    return pl.BlockSpec(memory_space=pl.ANY)


def in_scalars(array):
    return pltpu.with_memory_space_constraint(array, SMEM)


def first_kernel(counts, choice, camera, theta, fuel, library):
    places = theta.shape[0]
    rows = VMEM((4, places, 128), F32)
    rim = VMEM((2, 3, 8, 128), F32)
    return pl.pallas_call(
        pack_rows,
        out_shape=tuple(SMEM(x.shape, jnp.int32) for x in (counts, choice, camera))
        + (VMEM(library.shape, library.dtype), VMEM((2, places + 4, 8, 128), F32))
        + (rows, rows, rows, rim, rim),
        in_specs=[anywhere()] * 6,
        out_specs=(in_smem(),) * 3 + (in_vmem(),) * 7,
        scratch_shapes=[pltpu.SemaphoreType.DMA((6,))],
        compiler_params=params(),
        name="pack_rows",
    )(counts, *map(in_hbm, (choice, camera, theta, fuel, library)))


def rim_kernel(counts, *received):
    rim = VMEM((2, 2, 8, 128), F32)
    return pl.pallas_call(
        pack_rims,
        out_shape=(rim, rim),
        in_specs=[in_smem()] + [in_vmem()] * len(received),
        out_specs=(in_vmem(),) * 2,
        compiler_params=params(),
        name="pack_rims",
    )(in_scalars(counts), *map(held, received))


def cost(flops):
    return pl.CostEstimate(flops=flops, bytes_accessed=10**6, transcendentals=10**5)


def early_kernel(devices, counts, choice, camera, field0, library, *rows):
    places = field0.shape[1] - 4
    functions = choice.shape[0]
    bins = library.shape[2]
    table = VMEM((4 * functions, 8, bins), F32)
    field = VMEM((places, 8, 128), F32)
    return pl.pallas_call(
        functools.partial(early_step, places, functions, float(MEAN_DEPTH * devices)),
        out_shape=(
            VMEM((2, places + 2, 8, 128), F32),
            VMEM((2, 4, places + 16, 128), F32),
            VMEM((2, 2, places, 128), F32),
            table,
            table,
            field,
            field,
            VMEM((4 * functions, 8, 128), F32),
        ),
        in_specs=[in_smem()] * 3 + [in_vmem()] * 5,
        out_specs=(in_vmem(),) * 8,
        scratch_shapes=[VMEM(library.shape, F32)],
        compiler_params=params(),
        cost_estimate=cost(10**7),
        name="early_step",
    )(*map(in_scalars, (counts, choice, camera)), *map(held, (field0, library, *rows)))


def middle_kernel(counts, *arrays):
    theta_next, fuel_next, sums = arrays[-3:]
    field = jax.ShapeDtypeStruct(theta_next.shape, F32)
    return pl.pallas_call(
        functools.partial(middle_step, theta_next.shape[0]),
        out_shape=(field, field) + tuple(VMEM(x.shape, F32) for x in (theta_next, fuel_next, sums)),
        in_specs=[in_smem()] + [in_vmem()] * len(arrays),
        out_specs=(anywhere(),) * 2 + (in_vmem(),) * 3,
        scratch_shapes=[pltpu.SemaphoreType.DMA((2,))],
        input_output_aliases={len(arrays) - 2 + i: 2 + i for i in range(2)},
        compiler_params=params(),
        cost_estimate=cost(10**7),
        name="middle_step",
    )(in_scalars(counts), *map(held, arrays))


def late_kernel(devices, counts, camera, *arrays):
    functions = camera.shape[0]
    kept = arrays[:4]
    image, ends, *_ = pl.pallas_call(
        functools.partial(late_step, functions),
        out_shape=(VMEM((2 * devices, 128), F32), VMEM((2, 4, 8, 128), F32))
        + tuple(VMEM(x.shape, F32) for x in kept),
        in_specs=[in_smem()] * 2 + [in_vmem()] * len(arrays),
        out_specs=(in_vmem(),) * 6,
        input_output_aliases={2 + i: 2 + i for i in range(4)},
        compiler_params=params(),
        cost_estimate=cost(10**6),
        name="late_step",
    )(*map(in_scalars, (counts, camera)), *map(held, arrays))
    return image, ends


def last_kernel(functions, counts, camera, pieces, ends, *fields):
    field = jax.ShapeDtypeStruct(fields[0].shape, F32)
    image = (functions, 4, 1, 16)
    return pl.pallas_call(
        composite,
        out_shape=(jax.ShapeDtypeStruct(image, F32), field, field),
        in_specs=[in_smem()] * 2 + [in_vmem()] * 2 + [anywhere()] * 2,
        out_specs=(anywhere(),) * 3,
        scratch_shapes=[VMEM(image, F32), pltpu.SemaphoreType.DMA((5,))],
        input_output_aliases={4: 1, 5: 2},
        compiler_params=params(),
        name="composite",
    )(*map(in_scalars, (counts, camera)), *map(held, (pieces, ends)), *map(in_hbm, fields))


def on_device(
    thermal_values,
    reactant_fraction,
    active_sheet_number,
    colour_lookup_library,
    colour_lookup_choice,
    camera_direction,
):
    devices = lax.axis_size("depth")
    counts, choice, camera, library, field0, own_rows, *messages = first_kernel(
        active_sheet_number,
        colour_lookup_choice,
        camera_direction,
        thermal_values,
        reactant_fraction,
        colour_lookup_library,
    )
    rows_gap = swapped(messages[1], "lat", 1)
    rows_pair = swapped(messages[0], "lat", 0)
    rim_gap = swapped(messages[3], "depth", 1)
    rim_pair = swapped(messages[2], "depth", 0)
    field1, edge0, edge1, low_table, rise_table, theta_next, fuel_next, sums = early_kernel(
        devices, counts, choice, camera, field0, library, own_rows, rows_pair, rows_gap
    )
    next_pair, next_gap = rim_kernel(counts, rows_pair, rows_gap, rim_pair, rim_gap, sums)
    order = next_pair
    next_gap = swapped(next_gap, "depth", 1)
    next_pair = swapped(next_pair, "depth", 0)
    theta_next, fuel_next, _, _, sums = middle_kernel(
        counts, field1, edge1, low_table, rise_table, order, theta_next, fuel_next, sums
    )
    pieces, ends = late_kernel(
        devices,
        counts,
        camera,
        field0,
        field1,
        edge0,
        edge1,
        low_table,
        rise_table,
        sums,
        own_rows,
        rim_pair,
        rim_gap,
        next_pair,
        next_gap,
    )
    pieces = lax.all_to_all(pieces, "depth", 0, 0, tiled=True)
    image, theta_next, fuel_next = last_kernel(
        choice.shape[0], counts, camera, pieces, ends, theta_next, fuel_next
    )
    return (theta_next, fuel_next, image)


def solution(mesh):
    placed = (P("depth", "lat", None), P("depth", "lat", None), P("depth"), P(), P(), P())
    return jax.shard_map(
        on_device,
        mesh=mesh,
        in_specs=placed,
        out_specs=(P("depth", "lat", None), P("depth", "lat", None), P(None, None, "lat", "depth")),
        check_vma=False,
    )
```

```python
import functools

import jax
import jax.numpy as jnp
from jax import lax
from jax.experimental import pallas as pl
from jax.experimental.pallas import tpu as pltpu
from jax.sharding import PartitionSpec as P

MEAN_DEPTH = 32
STEPS = 2

time_step = 0.03
heat_release = 2.0
zeldovich = 8.0
expansion = 0.8

VMEM = pltpu.VMEM
SMEM = pltpu.SMEM
F32 = jnp.float32


def in_vmem():
    return pl.BlockSpec(memory_space=VMEM)


def in_smem():
    return pl.BlockSpec(memory_space=SMEM)


UNROLL_1 = 16
WINDOWS = ((12, 12), (24, 12), (24, 12))


def is_even(axis):
    return lax.rem(lax.axis_index(axis), 2) == 0


def select(which, first, second):
    return jnp.where(which, first, second)


def pack_rows(
    counts_in,
    choice_in,
    camera_in,
    theta,
    fuel,
    library_in,
    counts,
    choice,
    camera,
    library,
    field0,
    own_rows,
    rows_pair,
    rows_gap,
    rim_pair,
    copies,
):
    places = theta.shape[0]
    moves = [
        (counts_in, counts),
        (theta, field0.at[0, pl.ds(2, places)]),
        (fuel, field0.at[1, pl.ds(2, places)]),
        (choice_in, choice),
        (camera_in, camera),
        (library_in, library),
    ]
    fetch = [
        pltpu.make_async_copy(source, target, copies.at[number])
        for number, (source, target) in enumerate(moves)
    ]
    for copy in fetch:
        copy.start()
    lat_even, depth_even = is_even("lat"), is_even("depth")
    for number in range(2):
        fetch[1 + number].wait()
        for row in range(2):
            low = field0[number, 2 : places + 2, row, :]
            high = field0[number, 2 : places + 2, 6 + row, :]
            rows_pair[2 * number + row] = select(lat_even, high, low)
            rows_gap[2 * number + row] = select(lat_even, low, high)
            own_rows[2 * row + number] = (low, high)[row]
    fetch[0].wait()
    depth_count = counts[0]
    last = depth_count + 1
    second_last = jnp.maximum(depth_count, 2)
    second = jnp.minimum(3, last)
    size = jnp.broadcast_to(depth_count.astype(F32), (8, 128))
    for number in range(2):
        up = (field0[number, last], field0[number, second_last], size)
        down = (field0[number, 2], field0[number, second], size)
        for layer in range(3):
            rim_pair[number, layer] = select(depth_even, up[layer], down[layer])
    for copy in fetch[3:]:
        copy.wait()


def beside(rows_pair, rows_gap, number, place):
    lat_even = is_even("lat")
    below = [ref[2 * number + 1, pl.ds(place, 1), :] for ref in (rows_gap, rows_pair)]
    above = [ref[2 * number, pl.ds(place, 1), :] for ref in (rows_pair, rows_gap)]
    rows = (select(lat_even, *below), select(lat_even, *above))
    return tuple(jnp.broadcast_to(x, (8, 128)) for x in rows)


def pack_gap(counts, field0, rows_pair, rows_gap, rim_pair, order, rim_gap):
    depth_count = counts[0]
    depth_even = is_even("depth")
    end = jnp.where(depth_even, 0, depth_count - 1)
    inward = jnp.where(depth_even, 1, jnp.maximum(depth_count - 2, 0))
    size = depth_count.astype(F32)
    row = sublanes()
    for number in range(2):
        rim_gap[number, 0] = field0[number, 2 + end]
        rim_gap[number, 1] = select(
            depth_count == 1, rim_pair[number, 0], field0[number, 2 + inward]
        )
        below, above = beside(rows_pair, rows_gap, number, end)
        rim_gap[number, 2] = jnp.where(row == 0, below, jnp.where(row == 1, above, size))


def pack_next(counts, rows_pair, rows_gap, rim_gap, order, next_pair):
    end = jnp.where(is_even("depth"), counts[0] - 1, 0)
    for number in range(2):
        next_pair[number, 0] = rim_gap[number, 0]
        below, above = beside(rows_pair, rows_gap, number, end)
        next_pair[number, 1] = jnp.where(sublanes() == 0, below, above)


def lanes():
    return lax.broadcasted_iota(jnp.int32, (8, 128), 1)


def sublanes():
    return lax.broadcasted_iota(jnp.int32, (8, 128), 0)


def left_of(x):
    return jnp.where(lanes() == 0, 0.0, pltpu.roll(x, 1, 1))


def right_of(x):
    return jnp.where(lanes() == 127, 0.0, pltpu.roll(x, 127, 1))


def row_below(x, halo_row):
    return jnp.where(sublanes() == 0, jnp.broadcast_to(halo_row, (8, 128)), pltpu.roll(x, 1, 0))


def row_above(x, halo_row):
    return jnp.where(sublanes() == 7, jnp.broadcast_to(halo_row, (8, 128)), pltpu.roll(x, 7, 0))


def stepped(heat, fuel, neighbours):
    heat_sum = neighbours[0][0]
    fuel_sum = neighbours[0][1]
    product_sum = neighbours[0][0] * neighbours[0][1]
    square_sum = neighbours[0][0] * neighbours[0][0]
    for heat_n, fuel_n in neighbours[1:]:
        heat_sum = heat_sum + heat_n
        fuel_sum = fuel_sum + fuel_n
        product_sum = product_sum + heat_n * fuel_n
        square_sum = square_sum + heat_n * heat_n
    heat_flux = (heat_sum - 6.0 * heat) + 1.5 * (square_sum - 6.0 * (heat * heat))
    fuel_flux = 0.5 * (
        (1.0 + 1.5 * heat) * (fuel_sum - 6.0 * fuel) + 1.5 * (product_sum - fuel * heat_sum)
    )
    ratio = zeldovich / expansion
    reaction = fuel * jnp.exp(ratio - ratio / ((1.0 - expansion) + expansion * heat))
    return (
        heat + time_step * (heat_flux + heat_release * reaction),
        fuel + time_step * (fuel_flux - reaction),
    )


LEAD = 8


def block_step(field, at, count, edge_rows):
    heat = [field[0, at - 1 + j] for j in range(count + 2)]
    burn = [field[1, at - 1 + j] for j in range(count + 2)]
    results = []
    for j in range(1, count + 1):
        h, b = heat[j], burn[j]
        (h_low, b_low), (h_high, b_high) = edge_rows(j - 1)
        around = [
            (heat[j - 1], burn[j - 1]),
            (heat[j + 1], burn[j + 1]),
            (row_below(h, h_low), row_below(b, b_low)),
            (row_above(h, h_high), row_above(b, b_high)),
            (left_of(h), left_of(b)),
            (right_of(h), right_of(b)),
        ]
        results.append(stepped(h, b, around))
    return results


def rows_beside(edge, sides, place):
    return [tuple(edge[n, side, pl.ds(place, 1), :] for n in range(2)) for side in sides]


def step_edges(edge0, inner, side, at, inner_at, count):
    edge_row = 1 + side
    outer_row = 3 * side

    def rows(ref, row, place):
        found = tuple(ref(n)[row(n), pl.ds(place, count), :] for n in range(2))
        return tuple(jnp.broadcast_to(x, (8, 128)) for x in found)

    def edge(row, shift):
        return rows(lambda n: edge0.at[n], lambda n: row, at + shift)

    heat, burn = edge(edge_row, 0)
    around = [
        edge(edge_row, -1),
        edge(edge_row, 1),
        edge(outer_row, 0),
        rows(lambda n: inner, lambda n: 2 * side + n, inner_at),
        (left_of(heat), left_of(burn)),
        (right_of(heat), right_of(burn)),
    ]
    outside = lax.axis_index("lat") == (0 if side == 0 else lax.axis_size("lat") - 1)
    return [jnp.where(outside, 0.0, x) for x in stepped(heat, burn, around)]


def look_up(low_table, rise_table, value):
    bins = low_table.shape[2]
    position = jnp.clip(value, 0.0, 1.0) * (bins - 1)
    lower = jnp.minimum(position.astype(jnp.int32), bins - 2)
    fraction = position - lower.astype(F32)

    def at(entry):
        low = jnp.take_along_axis(low_table[entry], lower, axis=1)
        rise = jnp.take_along_axis(rise_table[entry], lower, axis=1)
        return low + fraction * rise

    return at


def add_layer(sums, number, at, alive):
    for f in range(2 * number, 2 * number + 2):
        gone, red, green, blue = sums[4 * f : 4 * f + 4]
        depth = jnp.where(alive, at(4 * f + 3), 0.0)
        gain = depth * (1.0 + depth * (0.5 + depth * (1.0 / 6.0)))
        gain = gain + gone * gain
        sums[4 * f] = gone + gain
        sums[4 * f + 1] = red + gain * at(4 * f)
        sums[4 * f + 2] = green + gain * at(4 * f + 1)
        sums[4 * f + 3] = blue + gain * at(4 * f + 2)


def inner_layers(
    first, count, unroll, depth_count, field1, edge1, tables, results, sums, after=None
):
    def body(block, carry):
        start = first + block * unroll

        def edge_rows(j):
            return rows_beside(edge1, (0, 1), start + j)

        carry = list(carry)
        for j, new in enumerate(block_step(field1, start + 1, unroll, edge_rows)):
            for number in range(2):
                value = jnp.where(start + j < depth_count, new[number], 0.0)
                results[number][start + j] = value
                add_layer(carry, number, look_up(*tables, value), start + j < depth_count - 2)
        if after is not None:
            after(start, unroll)
        return tuple(carry)

    return lax.fori_loop(0, count // unroll, body, tuple(sums))


def early_step(
    places,
    functions,
    all_layers,
    counts,
    choice,
    camera,
    field0,
    library,
    own_rows,
    rows_pair,
    rows_gap,
    field1,
    edge0,
    edge1,
    low_table,
    rise_table,
    theta_next,
    fuel_next,
    sums,
    tables,
):
    lat_even = is_even("lat")
    bins = library.shape[2]
    tables[...] = library[...].astype(F32)
    per_cell = 3.0 / all_layers
    for f in range(functions):
        sign = jnp.where(camera[f] == 0, -per_cell, per_cell)
        for c in range(4):
            low = jnp.broadcast_to(tables[choice[f], c : c + 1, :], (8, bins))
            rise = pltpu.roll(low, bins - 1, 1) - low
            if c == 3:
                low = low * sign
                rise = rise * sign
            low_table[4 * f + c] = low
            rise_table[4 * f + c] = rise

    for number in range(2):
        for row in range(2):
            pair, gap = rows_pair[2 * number + row], rows_gap[2 * number + row]
            edge0[number, row, LEAD : LEAD + places] = select(lat_even, gap, pair)
            edge0[number, 2 + row, LEAD : LEAD + places] = select(lat_even, pair, gap)

    for block in range(places // 8):
        for side in range(2):
            fresh = step_edges(edge0, own_rows, side, LEAD + 8 * block, 8 * block, 8)
            for number in range(2):
                edge1[number, side, 8 * block : 8 * block + 8] = fresh[number]

    def first_step(block, carry):
        start = block * UNROLL_1

        def edge_rows(j):
            return rows_beside(edge0, (1, 2), LEAD + start + j)

        for j, new in enumerate(block_step(field0, start + 2, UNROLL_1, edge_rows)):
            for number in range(2):
                field1[number, start + 1 + j] = new[number]
        return carry

    lax.fori_loop(0, places // UNROLL_1, first_step, 0)
    zero = jnp.zeros((8, 128), F32)
    for out in (theta_next, fuel_next):
        for place in (0, 1, places - 2, places - 1):
            out[place] = zero
    found = inner_layers(
        2,
        *WINDOWS[0],
        counts[0],
        field1,
        edge1,
        (low_table, rise_table),
        (theta_next, fuel_next),
        [zero] * (4 * functions),
    )
    for entry, value in enumerate(found):
        sums[entry] = value


def middle_step(
    places,
    window,
    counts,
    field1,
    edge1,
    low_table,
    rise_table,
    order,
    theta_in,
    fuel_in,
    sums_in,
    *outs,
):
    last = window == len(WINDOWS) - 1
    if last:
        theta_out, fuel_out, theta_next, fuel_next, sums, copies = outs
    else:
        theta_next, fuel_next, sums = outs

    def leave(number, first, count):
        return pltpu.make_async_copy(
            (theta_next, fuel_next)[number].at[pl.ds(first, count)],
            (theta_out, fuel_out)[number].at[pl.ds(first, count)],
            copies.at[number],
        )

    def start_leaving(first, count):
        for number in range(2):
            leave(number, first, count).start()

    first = 2 + sum(layers for layers, unroll in WINDOWS[:window])
    if last:
        start_leaving(0, first)
        start_leaving(places - 2, 2)
    found = inner_layers(
        first,
        *WINDOWS[window],
        counts[0],
        field1,
        edge1,
        (low_table, rise_table),
        (theta_next, fuel_next),
        [sums_in[entry] for entry in range(sums_in.shape[0])],
        start_leaving if last else None,
    )
    for entry, value in enumerate(found):
        sums[entry] = value
    if last:
        for number in range(2):
            leave(number, 0, places).wait()


def late_step(
    functions,
    counts,
    camera,
    field0_in,
    field1_in,
    edge0_in,
    edge1_in,
    low_table,
    rise_table,
    sums,
    own_rows,
    rim_pair,
    rim_gap,
    next_pair,
    image,
    ends,
    field0,
    field1,
    edge0,
    edge1,
):
    depth_count = counts[0]
    depth_even = is_even("depth")

    def sides(pair, gap):
        return select(depth_even, gap, pair), select(depth_even, pair, gap)

    pair_size = rim_pair[0, 2]
    gap_size = jnp.broadcast_to(rim_gap[0, 2, 2:3], (8, 128))
    below_size, above_size = sides(pair_size, gap_size)
    for number in range(2):
        nearest = sides(rim_pair[number, 0], rim_gap[number, 0])
        second = jnp.where(pair_size == 1.0, next_pair[number, 0], rim_pair[number, 1])
        second = sides(second, rim_gap[number, 1])
        rows = sides(next_pair[number, 1], rim_gap[number, 2])
        field0[number, 0] = second[0]
        field0[number, 1] = nearest[0]
        field0[number, depth_count + 2] = nearest[1]
        field0[number, depth_count + 3] = second[1]
        for side in range(2):
            edge0[number, 1 + side, LEAD - 1 : LEAD] = rows[0][side : side + 1]
            edge0[number, 1 + side, pl.ds(LEAD + depth_count, 1)] = rows[1][side : side + 1]
    for place in (0, depth_count - 1):
        for side in range(2):
            fresh = step_edges(edge0, own_rows, side, LEAD + place, place, 1)
            for number in range(2):
                edge1[number, side, pl.ds(place, 1)] = fresh[number][0:1]
    for place, size in (
        (-1, below_size),
        (0, None),
        (depth_count - 1, None),
        (depth_count, above_size),
    ):

        def edge_rows(j, place=place):
            return rows_beside(edge0, (1, 2), LEAD + place)

        (fresh,) = block_step(field0, place + 2, 1, edge_rows)
        for number in range(2):
            value = fresh[number]
            field1[number, place + 1] = (
                value if size is None else jnp.where(size > 0.0, value, 0.0)
            )

    zero = jnp.zeros((8, 128), F32)
    pairs = ((0, 0), (2, jnp.maximum(depth_count - 2, 2)))
    stepped_ends = []
    for slot, start in pairs:

        def edge_rows(j, start=start):
            return rows_beside(edge1, (0, 1), start + j)

        fresh = block_step(field1, start + 1, 2, edge_rows)
        alive = [start + j < depth_count for j in range(2)]
        fresh = [[jnp.where(alive[j], value, 0.0) for value in fresh[j]] for j in range(2)]
        stepped_ends.append((alive, fresh))
        for number in range(2):
            for j in range(2):
                ends[number, slot + j] = fresh[j][number]
    segments = []
    for alive, fresh in stepped_ends:
        segment = [zero] * (4 * functions)
        for j in range(2):
            for number in range(2):
                at = look_up(low_table, rise_table, fresh[j][number])
                add_layer(segment, number, at, alive[j])
        segments.append(segment)

    head, tail = segments
    channels = []
    for f in range(functions):
        through_head = 1.0 + head[4 * f]
        through_body = 1.0 + sums[4 * f]
        gone, red, green, blue = [
            head[4 * f + c]
            + through_head * (sums[4 * f + c] + through_body * tail[4 * f + c])
            for c in range(4)
        ]
        scale = jnp.where(camera[f] == 0, -1.0, 1.0 / (1.0 + gone))
        channels += [red * scale, green * scale, blue * scale, gone * scale]

    group = lanes() // 16
    for half in range(2):
        regs = channels[8 * half : 8 * half + 8]
        for bit in (1, 2, 4):
            upper = (group & bit) != 0
            fresh = list(regs)
            for i in range(8):
                if i & bit:
                    continue
                a, b = regs[i], regs[i | bit]
                fresh[i] = jnp.where(upper, pltpu.roll(b, 16 * bit, 1), a)
                fresh[i | bit] = jnp.where(upper, b, pltpu.roll(a, 128 - 16 * bit, 1))
            regs = fresh
        for g in range(8):
            image[pl.ds(2 * g + half, 8, stride=16), :] = regs[g]


def composite(
    counts, camera, pieces, ends, theta_in, fuel_in, image_out, theta_next, fuel_next, image, copies
):
    sources = pieces.shape[0] // 2
    leave = [
        pltpu.make_async_copy(
            ends.at[number, pl.ds(slot, 2)],
            out.at[pl.ds(place, 2)],
            copies.at[slot + number],
        )
        for number, out in enumerate((theta_next, fuel_next))
        for slot, place in ((0, 0), (2, jnp.maximum(counts[0] - 2, 2)))
    ]
    for copy in leave:
        copy.start()
    leave.append(pltpu.make_async_copy(image, image_out, copies.at[4]))
    lane = lanes()
    row = sublanes()
    opacity_lane = lane // 64 * 64 + 48 + lane % 16
    for half in range(2):
        forward = jnp.where(
            lane < 64,
            (camera[2 * half] == 0).astype(jnp.int32),
            (camera[2 * half + 1] == 0).astype(jnp.int32),
        ) == 1
        values, clear, through = [], [], []
        carry = jnp.ones((8, 128), F32)
        for block in range(sources // 8):
            value = pieces[pl.ds(16 * block + half, 8, stride=2), :]
            passing = 1.0 - jnp.take_along_axis(value, opacity_lane, axis=1)
            product = passing
            for shift in (1, 2, 4):
                product = product * jnp.where(row >= shift, pltpu.roll(product, shift, 0), 1.0)
            product = product * carry
            carry = jnp.broadcast_to(product[7:8], (8, 128))
            values.append(value)
            clear.append(passing)
            through.append(product)
        total = jnp.zeros((8, 128), F32)
        for value, passing, product in zip(values, clear, through):
            top = jnp.where(forward, product, carry)
            bottom = jnp.where(forward, passing, product)
            total = total + value * (top / bottom)
        line = jnp.sum(total, axis=0, keepdims=True)
        for clo in range(8):
            channel = 8 * half + clo
            image[channel // 4, channel % 4] = line[:, 16 * clo : 16 * clo + 16]
    leave[-1].start()
    for copy in leave:
        copy.wait()


def swapped(array, axis, first):
    count = lax.axis_size(axis)
    pairs = []
    for i in range(first, count - 1, 2):
        pairs += [(i, i + 1), (i + 1, i)]
    return lax.ppermute(array, axis, pairs)


def held(array):
    return pltpu.with_memory_space_constraint(array, VMEM)


def in_hbm(array):
    return pltpu.with_memory_space_constraint(array, pltpu.HBM)


def params():
    return pltpu.CompilerParams(vmem_limit_bytes=16 * 1024 * 1024)


def anywhere():
    return pl.BlockSpec(memory_space=pl.ANY)


def in_scalars(array):
    return pltpu.with_memory_space_constraint(array, SMEM)


def first_kernel(counts, choice, camera, theta, fuel, library):
    places = theta.shape[0]
    rows = VMEM((4, places, 128), F32)
    rim = VMEM((2, 3, 8, 128), F32)
    return pl.pallas_call(
        pack_rows,
        out_shape=tuple(SMEM(x.shape, jnp.int32) for x in (counts, choice, camera))
        + (VMEM(library.shape, library.dtype), VMEM((2, places + 4, 8, 128), F32))
        + (rows, rows, rows, rim),
        in_specs=[anywhere()] * 6,
        out_specs=(in_smem(),) * 3 + (in_vmem(),) * 6,
        scratch_shapes=[pltpu.SemaphoreType.DMA((6,))],
        compiler_params=params(),
        name="pack_rows",
    )(counts, *map(in_hbm, (choice, camera, theta, fuel, library)))


def rim_kernel(body, layers, counts, *arrays):
    return pl.pallas_call(
        body,
        out_shape=VMEM((2, layers, 8, 128), F32),
        in_specs=[in_smem()] + [in_vmem()] * len(arrays),
        out_specs=in_vmem(),
        compiler_params=params(),
        name=body.__name__,
    )(in_scalars(counts), *map(held, arrays))


def cost(flops):
    return pl.CostEstimate(flops=flops, bytes_accessed=10**6, transcendentals=10**5)


def early_kernel(devices, counts, choice, camera, field0, library, *rows):
    places = field0.shape[1] - 4
    functions = choice.shape[0]
    bins = library.shape[2]
    table = VMEM((4 * functions, 8, bins), F32)
    field = VMEM((places, 8, 128), F32)
    return pl.pallas_call(
        functools.partial(early_step, places, functions, float(MEAN_DEPTH * devices)),
        out_shape=(
            VMEM((2, places + 2, 8, 128), F32),
            VMEM((2, 4, places + 16, 128), F32),
            VMEM((2, 2, places, 128), F32),
            table,
            table,
            field,
            field,
            VMEM((4 * functions, 8, 128), F32),
        ),
        in_specs=[in_smem()] * 3 + [in_vmem()] * 5,
        out_specs=(in_vmem(),) * 8,
        scratch_shapes=[VMEM(library.shape, F32)],
        compiler_params=params(),
        cost_estimate=cost(10**7),
        name="early_step",
    )(*map(in_scalars, (counts, choice, camera)), *map(held, (field0, library, *rows)))


def middle_kernel(window, counts, *arrays):
    theta_next, fuel_next, sums = arrays[-3:]
    field = jax.ShapeDtypeStruct(theta_next.shape, F32)
    last = window == len(WINDOWS) - 1
    lead = 2 if last else 0
    return pl.pallas_call(
        functools.partial(middle_step, theta_next.shape[0], window),
        out_shape=(field,) * lead + tuple(VMEM(x.shape, F32) for x in (theta_next, fuel_next, sums)),
        in_specs=[in_smem()] + [in_vmem()] * len(arrays),
        out_specs=(anywhere(),) * lead + (in_vmem(),) * 3,
        scratch_shapes=[pltpu.SemaphoreType.DMA((2,))] if last else [],
        input_output_aliases={len(arrays) - 2 + i: lead + i for i in range(2)},
        compiler_params=params(),
        cost_estimate=cost(10**7),
        name="middle_step",
    )(in_scalars(counts), *map(held, arrays))


def late_kernel(devices, counts, camera, *arrays):
    functions = camera.shape[0]
    kept = arrays[:4]
    image, ends, *_ = pl.pallas_call(
        functools.partial(late_step, functions),
        out_shape=(VMEM((2 * devices, 128), F32), VMEM((2, 4, 8, 128), F32))
        + tuple(VMEM(x.shape, F32) for x in kept),
        in_specs=[in_smem()] * 2 + [in_vmem()] * len(arrays),
        out_specs=(in_vmem(),) * 6,
        input_output_aliases={2 + i: 2 + i for i in range(4)},
        compiler_params=params(),
        cost_estimate=cost(10**6),
        name="late_step",
    )(*map(in_scalars, (counts, camera)), *map(held, arrays))
    return image, ends


def last_kernel(functions, counts, camera, pieces, ends, *fields):
    field = jax.ShapeDtypeStruct(fields[0].shape, F32)
    image = (functions, 4, 1, 16)
    return pl.pallas_call(
        composite,
        out_shape=(jax.ShapeDtypeStruct(image, F32), field, field),
        in_specs=[in_smem()] * 2 + [in_vmem()] * 2 + [anywhere()] * 2,
        out_specs=(anywhere(),) * 3,
        scratch_shapes=[VMEM(image, F32), pltpu.SemaphoreType.DMA((5,))],
        input_output_aliases={4: 1, 5: 2},
        compiler_params=params(),
        name="composite",
    )(*map(in_scalars, (counts, camera)), *map(held, (pieces, ends)), *map(in_hbm, fields))


def on_device(
    thermal_values,
    reactant_fraction,
    active_sheet_number,
    colour_lookup_library,
    colour_lookup_choice,
    camera_direction,
):
    devices = lax.axis_size("depth")
    counts, choice, camera, library, field0, own_rows, *messages = first_kernel(
        active_sheet_number,
        colour_lookup_choice,
        camera_direction,
        thermal_values,
        reactant_fraction,
        colour_lookup_library,
    )
    rows_pair = swapped(messages[0], "lat", 0)
    rows_gap = swapped(messages[1], "lat", 1)
    rim_pair = swapped(messages[2], "depth", 0)
    field1, edge0, edge1, low_table, rise_table, theta_next, fuel_next, sums = early_kernel(
        devices, counts, choice, camera, field0, library, own_rows, rows_pair, rows_gap
    )
    order = rim_kernel(pack_gap, 3, counts, field0, rows_pair, rows_gap, rim_pair, sums)
    rim_gap = swapped(order, "depth", 1)
    theta_next, fuel_next, sums = middle_kernel(
        1, counts, field1, edge1, low_table, rise_table, order, theta_next, fuel_next, sums
    )
    order = rim_kernel(pack_next, 2, counts, rows_pair, rows_gap, rim_gap, sums)
    next_pair = swapped(order, "depth", 0)
    theta_next, fuel_next, _, _, sums = middle_kernel(
        2, counts, field1, edge1, low_table, rise_table, order, theta_next, fuel_next, sums
    )
    pieces, ends = late_kernel(
        devices,
        counts,
        camera,
        field0,
        field1,
        edge0,
        edge1,
        low_table,
        rise_table,
        sums,
        own_rows,
        rim_pair,
        rim_gap,
        next_pair,
    )
    pieces = lax.all_to_all(pieces, "depth", 0, 0, tiled=True)
    image, theta_next, fuel_next = last_kernel(
        choice.shape[0], counts, camera, pieces, ends, theta_next, fuel_next
    )
    return (theta_next, fuel_next, image)


def solution(mesh):
    placed = (P("depth", "lat", None), P("depth", "lat", None), P("depth"), P(), P(), P())
    return jax.shard_map(
        on_device,
        mesh=mesh,
        in_specs=placed,
        out_specs=(P("depth", "lat", None), P("depth", "lat", None), P(None, None, "lat", "depth")),
        check_vma=False,
    )
```

```python
import functools

import jax
import jax.numpy as jnp
from jax import lax
from jax.experimental import pallas as pl
from jax.experimental.pallas import tpu as pltpu
from jax.sharding import PartitionSpec as P

MEAN_DEPTH = 32
STEPS = 2

time_step = 0.03
heat_release = 2.0
zeldovich = 8.0
expansion = 0.8

VMEM = pltpu.VMEM
SMEM = pltpu.SMEM
F32 = jnp.float32


def in_vmem():
    return pl.BlockSpec(memory_space=VMEM)


def in_smem():
    return pl.BlockSpec(memory_space=SMEM)


UNROLL_1 = 16
WINDOWS = ((12, 12), (24, 12), (24, 12))


def is_even(axis):
    return lax.rem(lax.axis_index(axis), 2) == 0


def select(which, first, second):
    return jnp.where(which, first, second)


def pack_rows(
    counts_in,
    choice_in,
    camera_in,
    theta,
    fuel,
    library_in,
    counts,
    choice,
    camera,
    library,
    field0,
    own_rows,
    rows_gap,
    rows_pair,
    rim_pair,
    copies,
):
    places = theta.shape[0]
    moves = [
        (counts_in, counts),
        (theta, field0.at[0, pl.ds(2, places)]),
        (fuel, field0.at[1, pl.ds(2, places)]),
        (choice_in, choice),
        (camera_in, camera),
        (library_in, library),
    ]
    fetch = [
        pltpu.make_async_copy(source, target, copies.at[number])
        for number, (source, target) in enumerate(moves)
    ]
    for copy in fetch:
        copy.start()
    lat_even, depth_even = is_even("lat"), is_even("depth")
    for number in range(2):
        fetch[1 + number].wait()
        for row in range(2):
            low = field0[number, 2 : places + 2, row, :]
            high = field0[number, 2 : places + 2, 6 + row, :]
            rows_pair[2 * number + row] = select(lat_even, high, low)
            rows_gap[2 * number + row] = select(lat_even, low, high)
            own_rows[2 * row + number] = (low, high)[row]
    fetch[0].wait()
    depth_count = counts[0]
    last = depth_count + 1
    second_last = jnp.maximum(depth_count, 2)
    second = jnp.minimum(3, last)
    size = jnp.broadcast_to(depth_count.astype(F32), (8, 128))
    for number in range(2):
        up = (field0[number, last], field0[number, second_last], size)
        down = (field0[number, 2], field0[number, second], size)
        for layer in range(3):
            rim_pair[number, layer] = select(depth_even, up[layer], down[layer])
    for copy in fetch[3:]:
        copy.wait()


def beside(rows_gap, rows_pair, number, place):
    lat_even = is_even("lat")
    below = [ref[2 * number + 1, pl.ds(place, 1), :] for ref in (rows_gap, rows_pair)]
    above = [ref[2 * number, pl.ds(place, 1), :] for ref in (rows_pair, rows_gap)]
    rows = (select(lat_even, *below), select(lat_even, *above))
    return tuple(jnp.broadcast_to(x, (8, 128)) for x in rows)


def pack_gap(counts, field0, rows_gap, rows_pair, rim_pair, order, rim_gap):
    depth_count = counts[0]
    depth_even = is_even("depth")
    end = jnp.where(depth_even, 0, depth_count - 1)
    inward = jnp.where(depth_even, 1, jnp.maximum(depth_count - 2, 0))
    size = depth_count.astype(F32)
    row = sublanes()
    for number in range(2):
        rim_gap[number, 0] = field0[number, 2 + end]
        rim_gap[number, 1] = select(
            depth_count == 1, rim_pair[number, 0], field0[number, 2 + inward]
        )
        below, above = beside(rows_gap, rows_pair, number, end)
        rim_gap[number, 2] = jnp.where(row == 0, below, jnp.where(row == 1, above, size))


def pack_next(counts, rows_gap, rows_pair, rim_gap, order, next_pair):
    end = jnp.where(is_even("depth"), counts[0] - 1, 0)
    for number in range(2):
        next_pair[number, 0] = rim_gap[number, 0]
        below, above = beside(rows_gap, rows_pair, number, end)
        next_pair[number, 1] = jnp.where(sublanes() == 0, below, above)


def lanes():
    return lax.broadcasted_iota(jnp.int32, (8, 128), 1)


def sublanes():
    return lax.broadcasted_iota(jnp.int32, (8, 128), 0)


def left_of(x):
    return jnp.where(lanes() == 0, 0.0, pltpu.roll(x, 1, 1))


def right_of(x):
    return jnp.where(lanes() == 127, 0.0, pltpu.roll(x, 127, 1))


def row_below(x, halo_row):
    return jnp.where(sublanes() == 0, jnp.broadcast_to(halo_row, (8, 128)), pltpu.roll(x, 1, 0))


def row_above(x, halo_row):
    return jnp.where(sublanes() == 7, jnp.broadcast_to(halo_row, (8, 128)), pltpu.roll(x, 7, 0))


def stepped(heat, fuel, neighbours):
    heat_sum = neighbours[0][0]
    fuel_sum = neighbours[0][1]
    product_sum = neighbours[0][0] * neighbours[0][1]
    square_sum = neighbours[0][0] * neighbours[0][0]
    for heat_n, fuel_n in neighbours[1:]:
        heat_sum = heat_sum + heat_n
        fuel_sum = fuel_sum + fuel_n
        product_sum = product_sum + heat_n * fuel_n
        square_sum = square_sum + heat_n * heat_n
    heat_flux = (heat_sum - 6.0 * heat) + 1.5 * (square_sum - 6.0 * (heat * heat))
    fuel_flux = 0.5 * (
        (1.0 + 1.5 * heat) * (fuel_sum - 6.0 * fuel) + 1.5 * (product_sum - fuel * heat_sum)
    )
    ratio = zeldovich / expansion
    reaction = fuel * jnp.exp(ratio - ratio / ((1.0 - expansion) + expansion * heat))
    return (
        heat + time_step * (heat_flux + heat_release * reaction),
        fuel + time_step * (fuel_flux - reaction),
    )


LEAD = 8


def block_step(field, at, count, edge_rows):
    heat = [field[0, at - 1 + j] for j in range(count + 2)]
    burn = [field[1, at - 1 + j] for j in range(count + 2)]
    results = []
    for j in range(1, count + 1):
        h, b = heat[j], burn[j]
        (h_low, b_low), (h_high, b_high) = edge_rows(j - 1)
        around = [
            (heat[j - 1], burn[j - 1]),
            (heat[j + 1], burn[j + 1]),
            (row_below(h, h_low), row_below(b, b_low)),
            (row_above(h, h_high), row_above(b, b_high)),
            (left_of(h), left_of(b)),
            (right_of(h), right_of(b)),
        ]
        results.append(stepped(h, b, around))
    return results


def rows_beside(edge, sides, place):
    return [tuple(edge[n, side, pl.ds(place, 1), :] for n in range(2)) for side in sides]


def step_edges(edge0, inner, side, at, inner_at, count):
    edge_row = 1 + side
    outer_row = 3 * side

    def rows(ref, row, place):
        found = tuple(ref(n)[row(n), pl.ds(place, count), :] for n in range(2))
        return tuple(jnp.broadcast_to(x, (8, 128)) for x in found)

    def edge(row, shift):
        return rows(lambda n: edge0.at[n], lambda n: row, at + shift)

    heat, burn = edge(edge_row, 0)
    around = [
        edge(edge_row, -1),
        edge(edge_row, 1),
        edge(outer_row, 0),
        rows(lambda n: inner, lambda n: 2 * side + n, inner_at),
        (left_of(heat), left_of(burn)),
        (right_of(heat), right_of(burn)),
    ]
    outside = lax.axis_index("lat") == (0 if side == 0 else lax.axis_size("lat") - 1)
    return [jnp.where(outside, 0.0, x) for x in stepped(heat, burn, around)]


def look_up(low_table, rise_table, value):
    bins = low_table.shape[2]
    position = jnp.clip(value, 0.0, 1.0) * (bins - 1)
    lower = jnp.minimum(position.astype(jnp.int32), bins - 2)
    fraction = position - lower.astype(F32)

    def at(entry):
        low = jnp.take_along_axis(low_table[entry], lower, axis=1)
        rise = jnp.take_along_axis(rise_table[entry], lower, axis=1)
        return low + fraction * rise

    return at


def add_layer(sums, number, at, alive):
    for f in range(2 * number, 2 * number + 2):
        gone, red, green, blue = sums[4 * f : 4 * f + 4]
        depth = jnp.where(alive, at(4 * f + 3), 0.0)
        gain = depth * (1.0 + depth * (0.5 + depth * (1.0 / 6.0)))
        gain = gain + gone * gain
        sums[4 * f] = gone + gain
        sums[4 * f + 1] = red + gain * at(4 * f)
        sums[4 * f + 2] = green + gain * at(4 * f + 1)
        sums[4 * f + 3] = blue + gain * at(4 * f + 2)


def inner_layers(
    first, count, unroll, depth_count, field1, edge1, tables, results, sums, after=None
):
    def body(block, carry):
        start = first + block * unroll

        def edge_rows(j):
            return rows_beside(edge1, (0, 1), start + j)

        carry = list(carry)
        for j, new in enumerate(block_step(field1, start + 1, unroll, edge_rows)):
            for number in range(2):
                value = jnp.where(start + j < depth_count, new[number], 0.0)
                results[number][start + j] = value
                add_layer(carry, number, look_up(*tables, value), start + j < depth_count - 2)
        if after is not None:
            after(start, unroll)
        return tuple(carry)

    return lax.fori_loop(0, count // unroll, body, tuple(sums))


def early_step(
    places,
    functions,
    all_layers,
    counts,
    choice,
    camera,
    field0,
    library,
    own_rows,
    rows_gap,
    rows_pair,
    field1,
    edge0,
    edge1,
    low_table,
    rise_table,
    theta_next,
    fuel_next,
    sums,
    tables,
):
    lat_even = is_even("lat")
    bins = library.shape[2]
    tables[...] = library[...].astype(F32)
    per_cell = 3.0 / all_layers
    for f in range(functions):
        sign = jnp.where(camera[f] == 0, -per_cell, per_cell)
        for c in range(4):
            low = jnp.broadcast_to(tables[choice[f], c : c + 1, :], (8, bins))
            rise = pltpu.roll(low, bins - 1, 1) - low
            if c == 3:
                low = low * sign
                rise = rise * sign
            low_table[4 * f + c] = low
            rise_table[4 * f + c] = rise

    for number in range(2):
        for row in range(2):
            pair, gap = rows_pair[2 * number + row], rows_gap[2 * number + row]
            edge0[number, row, LEAD : LEAD + places] = select(lat_even, gap, pair)
            edge0[number, 2 + row, LEAD : LEAD + places] = select(lat_even, pair, gap)

    for block in range(places // 8):
        for side in range(2):
            fresh = step_edges(edge0, own_rows, side, LEAD + 8 * block, 8 * block, 8)
            for number in range(2):
                edge1[number, side, 8 * block : 8 * block + 8] = fresh[number]

    def first_step(block, carry):
        start = block * UNROLL_1

        def edge_rows(j):
            return rows_beside(edge0, (1, 2), LEAD + start + j)

        for j, new in enumerate(block_step(field0, start + 2, UNROLL_1, edge_rows)):
            for number in range(2):
                field1[number, start + 1 + j] = new[number]
        return carry

    lax.fori_loop(0, places // UNROLL_1, first_step, 0)
    zero = jnp.zeros((8, 128), F32)
    for out in (theta_next, fuel_next):
        for place in (0, 1, places - 2, places - 1):
            out[place] = zero
    found = inner_layers(
        2,
        *WINDOWS[0],
        counts[0],
        field1,
        edge1,
        (low_table, rise_table),
        (theta_next, fuel_next),
        [zero] * (4 * functions),
    )
    for entry, value in enumerate(found):
        sums[entry] = value


def middle_step(
    places,
    window,
    counts,
    field1,
    edge1,
    low_table,
    rise_table,
    order,
    theta_in,
    fuel_in,
    sums_in,
    *outs,
):
    last = window == len(WINDOWS) - 1
    if last:
        theta_out, fuel_out, theta_next, fuel_next, sums, copies = outs
    else:
        theta_next, fuel_next, sums = outs

    def leave(number, first, count):
        return pltpu.make_async_copy(
            (theta_next, fuel_next)[number].at[pl.ds(first, count)],
            (theta_out, fuel_out)[number].at[pl.ds(first, count)],
            copies.at[number],
        )

    def start_leaving(first, count):
        for number in range(2):
            leave(number, first, count).start()

    first = 2 + sum(layers for layers, unroll in WINDOWS[:window])
    if last:
        start_leaving(0, first)
        start_leaving(places - 2, 2)
    found = inner_layers(
        first,
        *WINDOWS[window],
        counts[0],
        field1,
        edge1,
        (low_table, rise_table),
        (theta_next, fuel_next),
        [sums_in[entry] for entry in range(sums_in.shape[0])],
        start_leaving if last else None,
    )
    for entry, value in enumerate(found):
        sums[entry] = value
    if last:
        for number in range(2):
            leave(number, 0, places).wait()


def late_step(
    functions,
    counts,
    camera,
    field0_in,
    field1_in,
    edge0_in,
    edge1_in,
    low_table,
    rise_table,
    sums,
    own_rows,
    rim_pair,
    rim_gap,
    next_pair,
    image,
    ends,
    field0,
    field1,
    edge0,
    edge1,
):
    depth_count = counts[0]
    depth_even = is_even("depth")

    def sides(pair, gap):
        return select(depth_even, gap, pair), select(depth_even, pair, gap)

    pair_size = rim_pair[0, 2]
    gap_size = jnp.broadcast_to(rim_gap[0, 2, 2:3], (8, 128))
    below_size, above_size = sides(pair_size, gap_size)
    for number in range(2):
        nearest = sides(rim_pair[number, 0], rim_gap[number, 0])
        second = jnp.where(pair_size == 1.0, next_pair[number, 0], rim_pair[number, 1])
        second = sides(second, rim_gap[number, 1])
        rows = sides(next_pair[number, 1], rim_gap[number, 2])
        field0[number, 0] = second[0]
        field0[number, 1] = nearest[0]
        field0[number, depth_count + 2] = nearest[1]
        field0[number, depth_count + 3] = second[1]
        for side in range(2):
            edge0[number, 1 + side, LEAD - 1 : LEAD] = rows[0][side : side + 1]
            edge0[number, 1 + side, pl.ds(LEAD + depth_count, 1)] = rows[1][side : side + 1]
    for place in (0, depth_count - 1):
        for side in range(2):
            fresh = step_edges(edge0, own_rows, side, LEAD + place, place, 1)
            for number in range(2):
                edge1[number, side, pl.ds(place, 1)] = fresh[number][0:1]
    for place, size in (
        (-1, below_size),
        (0, None),
        (depth_count - 1, None),
        (depth_count, above_size),
    ):

        def edge_rows(j, place=place):
            return rows_beside(edge0, (1, 2), LEAD + place)

        (fresh,) = block_step(field0, place + 2, 1, edge_rows)
        for number in range(2):
            value = fresh[number]
            field1[number, place + 1] = (
                value if size is None else jnp.where(size > 0.0, value, 0.0)
            )

    zero = jnp.zeros((8, 128), F32)
    pairs = ((0, 0), (2, jnp.maximum(depth_count - 2, 2)))
    stepped_ends = []
    for slot, start in pairs:

        def edge_rows(j, start=start):
            return rows_beside(edge1, (0, 1), start + j)

        fresh = block_step(field1, start + 1, 2, edge_rows)
        alive = [start + j < depth_count for j in range(2)]
        fresh = [[jnp.where(alive[j], value, 0.0) for value in fresh[j]] for j in range(2)]
        stepped_ends.append((alive, fresh))
        for number in range(2):
            for j in range(2):
                ends[number, slot + j] = fresh[j][number]
    segments = []
    for alive, fresh in stepped_ends:
        segment = [zero] * (4 * functions)
        for j in range(2):
            for number in range(2):
                at = look_up(low_table, rise_table, fresh[j][number])
                add_layer(segment, number, at, alive[j])
        segments.append(segment)

    head, tail = segments
    channels = []
    for f in range(functions):
        through_head = 1.0 + head[4 * f]
        through_body = 1.0 + sums[4 * f]
        gone, red, green, blue = [
            head[4 * f + c]
            + through_head * (sums[4 * f + c] + through_body * tail[4 * f + c])
            for c in range(4)
        ]
        scale = jnp.where(camera[f] == 0, -1.0, 1.0 / (1.0 + gone))
        channels += [red * scale, green * scale, blue * scale, gone * scale]

    group = lanes() // 16
    for half in range(2):
        regs = channels[8 * half : 8 * half + 8]
        for bit in (1, 2, 4):
            upper = (group & bit) != 0
            fresh = list(regs)
            for i in range(8):
                if i & bit:
                    continue
                a, b = regs[i], regs[i | bit]
                fresh[i] = jnp.where(upper, pltpu.roll(b, 16 * bit, 1), a)
                fresh[i | bit] = jnp.where(upper, b, pltpu.roll(a, 128 - 16 * bit, 1))
            regs = fresh
        for g in range(8):
            image[pl.ds(2 * g + half, 8, stride=16), :] = regs[g]


def composite(
    counts, camera, pieces, ends, theta_in, fuel_in, image_out, theta_next, fuel_next, image, copies
):
    sources = pieces.shape[0] // 2
    leave = [
        pltpu.make_async_copy(
            ends.at[number, pl.ds(slot, 2)],
            out.at[pl.ds(place, 2)],
            copies.at[slot + number],
        )
        for number, out in enumerate((theta_next, fuel_next))
        for slot, place in ((0, 0), (2, jnp.maximum(counts[0] - 2, 2)))
    ]
    for copy in leave:
        copy.start()
    leave.append(pltpu.make_async_copy(image, image_out, copies.at[4]))
    lane = lanes()
    row = sublanes()
    opacity_lane = lane // 64 * 64 + 48 + lane % 16
    for half in range(2):
        forward = jnp.where(
            lane < 64,
            (camera[2 * half] == 0).astype(jnp.int32),
            (camera[2 * half + 1] == 0).astype(jnp.int32),
        ) == 1
        values, clear, through = [], [], []
        carry = jnp.ones((8, 128), F32)
        for block in range(sources // 8):
            value = pieces[pl.ds(16 * block + half, 8, stride=2), :]
            passing = 1.0 - jnp.take_along_axis(value, opacity_lane, axis=1)
            product = passing
            for shift in (1, 2, 4):
                product = product * jnp.where(row >= shift, pltpu.roll(product, shift, 0), 1.0)
            product = product * carry
            carry = jnp.broadcast_to(product[7:8], (8, 128))
            values.append(value)
            clear.append(passing)
            through.append(product)
        total = jnp.zeros((8, 128), F32)
        for value, passing, product in zip(values, clear, through):
            top = jnp.where(forward, product, carry)
            bottom = jnp.where(forward, passing, product)
            total = total + value * (top / bottom)
        line = jnp.sum(total, axis=0, keepdims=True)
        for clo in range(8):
            channel = 8 * half + clo
            image[channel // 4, channel % 4] = line[:, 16 * clo : 16 * clo + 16]
    leave[-1].start()
    for copy in leave:
        copy.wait()


def swapped(array, axis, first):
    count = lax.axis_size(axis)
    pairs = []
    for i in range(first, count - 1, 2):
        pairs += [(i, i + 1), (i + 1, i)]
    return lax.ppermute(array, axis, pairs)


def held(array):
    return pltpu.with_memory_space_constraint(array, VMEM)


def in_hbm(array):
    return pltpu.with_memory_space_constraint(array, pltpu.HBM)


def params():
    return pltpu.CompilerParams(vmem_limit_bytes=16 * 1024 * 1024)


def anywhere():
    return pl.BlockSpec(memory_space=pl.ANY)


def in_scalars(array):
    return pltpu.with_memory_space_constraint(array, SMEM)


def first_kernel(counts, choice, camera, theta, fuel, library):
    places = theta.shape[0]
    rows = VMEM((4, places, 128), F32)
    rim = VMEM((2, 3, 8, 128), F32)
    return pl.pallas_call(
        pack_rows,
        out_shape=tuple(SMEM(x.shape, jnp.int32) for x in (counts, choice, camera))
        + (VMEM(library.shape, library.dtype), VMEM((2, places + 4, 8, 128), F32))
        + (rows, rows, rows, rim),
        in_specs=[anywhere()] * 6,
        out_specs=(in_smem(),) * 3 + (in_vmem(),) * 6,
        scratch_shapes=[pltpu.SemaphoreType.DMA((6,))],
        compiler_params=params(),
        name="pack_rows",
    )(counts, *map(in_hbm, (choice, camera, theta, fuel, library)))


def rim_kernel(body, layers, counts, *arrays):
    return pl.pallas_call(
        body,
        out_shape=VMEM((2, layers, 8, 128), F32),
        in_specs=[in_smem()] + [in_vmem()] * len(arrays),
        out_specs=in_vmem(),
        compiler_params=params(),
        name=body.__name__,
    )(in_scalars(counts), *map(held, arrays))


def cost(flops):
    return pl.CostEstimate(flops=flops, bytes_accessed=10**6, transcendentals=10**5)


def early_kernel(devices, counts, choice, camera, field0, library, *rows):
    places = field0.shape[1] - 4
    functions = choice.shape[0]
    bins = library.shape[2]
    table = VMEM((4 * functions, 8, bins), F32)
    field = VMEM((places, 8, 128), F32)
    return pl.pallas_call(
        functools.partial(early_step, places, functions, float(MEAN_DEPTH * devices)),
        out_shape=(
            VMEM((2, places + 2, 8, 128), F32),
            VMEM((2, 4, places + 16, 128), F32),
            VMEM((2, 2, places, 128), F32),
            table,
            table,
            field,
            field,
            VMEM((4 * functions, 8, 128), F32),
        ),
        in_specs=[in_smem()] * 3 + [in_vmem()] * 5,
        out_specs=(in_vmem(),) * 8,
        scratch_shapes=[VMEM(library.shape, F32)],
        compiler_params=params(),
        cost_estimate=cost(10**7),
        name="early_step",
    )(*map(in_scalars, (counts, choice, camera)), *map(held, (field0, library, *rows)))


def middle_kernel(window, counts, *arrays):
    theta_next, fuel_next, sums = arrays[-3:]
    field = jax.ShapeDtypeStruct(theta_next.shape, F32)
    last = window == len(WINDOWS) - 1
    lead = 2 if last else 0
    return pl.pallas_call(
        functools.partial(middle_step, theta_next.shape[0], window),
        out_shape=(field,) * lead + tuple(VMEM(x.shape, F32) for x in (theta_next, fuel_next, sums)),
        in_specs=[in_smem()] + [in_vmem()] * len(arrays),
        out_specs=(anywhere(),) * lead + (in_vmem(),) * 3,
        scratch_shapes=[pltpu.SemaphoreType.DMA((2,))] if last else [],
        input_output_aliases={len(arrays) - 2 + i: lead + i for i in range(2)},
        compiler_params=params(),
        cost_estimate=cost(10**7),
        name="middle_step",
    )(in_scalars(counts), *map(held, arrays))


def late_kernel(devices, counts, camera, *arrays):
    functions = camera.shape[0]
    kept = arrays[:4]
    image, ends, *_ = pl.pallas_call(
        functools.partial(late_step, functions),
        out_shape=(VMEM((2 * devices, 128), F32), VMEM((2, 4, 8, 128), F32))
        + tuple(VMEM(x.shape, F32) for x in kept),
        in_specs=[in_smem()] * 2 + [in_vmem()] * len(arrays),
        out_specs=(in_vmem(),) * 6,
        input_output_aliases={2 + i: 2 + i for i in range(4)},
        compiler_params=params(),
        cost_estimate=cost(10**6),
        name="late_step",
    )(*map(in_scalars, (counts, camera)), *map(held, arrays))
    return image, ends


def last_kernel(functions, counts, camera, pieces, ends, *fields):
    field = jax.ShapeDtypeStruct(fields[0].shape, F32)
    image = (functions, 4, 1, 16)
    return pl.pallas_call(
        composite,
        out_shape=(jax.ShapeDtypeStruct(image, F32), field, field),
        in_specs=[in_smem()] * 2 + [in_vmem()] * 2 + [anywhere()] * 2,
        out_specs=(anywhere(),) * 3,
        scratch_shapes=[VMEM(image, F32), pltpu.SemaphoreType.DMA((5,))],
        input_output_aliases={4: 1, 5: 2},
        compiler_params=params(),
        name="composite",
    )(*map(in_scalars, (counts, camera)), *map(held, (pieces, ends)), *map(in_hbm, fields))


def on_device(
    thermal_values,
    reactant_fraction,
    active_sheet_number,
    colour_lookup_library,
    colour_lookup_choice,
    camera_direction,
):
    devices = lax.axis_size("depth")
    counts, choice, camera, library, field0, own_rows, *messages = first_kernel(
        active_sheet_number,
        colour_lookup_choice,
        camera_direction,
        thermal_values,
        reactant_fraction,
        colour_lookup_library,
    )
    rows_gap = swapped(messages[0], "lat", 1)
    rows_pair = swapped(messages[1], "lat", 0)
    rim_pair = swapped(messages[2], "depth", 0)
    field1, edge0, edge1, low_table, rise_table, theta_next, fuel_next, sums = early_kernel(
        devices, counts, choice, camera, field0, library, own_rows, rows_gap, rows_pair
    )
    order = rim_kernel(pack_gap, 3, counts, field0, rows_gap, rows_pair, rim_pair, sums)
    rim_gap = swapped(order, "depth", 1)
    theta_next, fuel_next, sums = middle_kernel(
        1, counts, field1, edge1, low_table, rise_table, order, theta_next, fuel_next, sums
    )
    order = rim_kernel(pack_next, 2, counts, rows_gap, rows_pair, rim_gap, sums)
    next_pair = swapped(order, "depth", 0)
    theta_next, fuel_next, _, _, sums = middle_kernel(
        2, counts, field1, edge1, low_table, rise_table, order, theta_next, fuel_next, sums
    )
    pieces, ends = late_kernel(
        devices,
        counts,
        camera,
        field0,
        field1,
        edge0,
        edge1,
        low_table,
        rise_table,
        sums,
        own_rows,
        rim_pair,
        rim_gap,
        next_pair,
    )
    pieces = lax.all_to_all(pieces, "depth", 0, 0, tiled=True)
    image, theta_next, fuel_next = last_kernel(
        choice.shape[0], counts, camera, pieces, ends, theta_next, fuel_next
    )
    return (theta_next, fuel_next, image)


def solution(mesh):
    placed = (P("depth", "lat", None), P("depth", "lat", None), P("depth"), P(), P(), P())
    return jax.shard_map(
        on_device,
        mesh=mesh,
        in_specs=placed,
        out_specs=(P("depth", "lat", None), P("depth", "lat", None), P(None, None, "lat", "depth")),
        check_vma=False,
    )
```

```python
import functools

import jax
import jax.numpy as jnp
from jax import lax
from jax.experimental import pallas as pl
from jax.experimental.pallas import tpu as pltpu
from jax.sharding import PartitionSpec as P

MEAN_DEPTH = 32
STEPS = 2

time_step = 0.03
heat_release = 2.0
zeldovich = 8.0
expansion = 0.8

VMEM = pltpu.VMEM
SMEM = pltpu.SMEM
F32 = jnp.float32


def in_vmem():
    return pl.BlockSpec(memory_space=VMEM)


def in_smem():
    return pl.BlockSpec(memory_space=SMEM)


UNROLL_1 = 16
WINDOWS = ((36, 12), (24, 12))


def is_even(axis):
    return lax.rem(lax.axis_index(axis), 2) == 0


def select(which, first, second):
    return jnp.where(which, first, second)


def pack_rows(
    counts_in,
    choice_in,
    camera_in,
    theta,
    fuel,
    library_in,
    counts,
    choice,
    camera,
    library,
    field0,
    own_rows,
    rows_pair,
    rows_gap,
    rim_pair,
    copies,
):
    places = theta.shape[0]
    moves = [
        (counts_in, counts),
        (theta, field0.at[0, pl.ds(2, places)]),
        (fuel, field0.at[1, pl.ds(2, places)]),
        (choice_in, choice),
        (camera_in, camera),
        (library_in, library),
    ]
    fetch = [
        pltpu.make_async_copy(source, target, copies.at[number])
        for number, (source, target) in enumerate(moves)
    ]
    for copy in fetch:
        copy.start()
    lat_even, depth_even = is_even("lat"), is_even("depth")
    for number in range(2):
        fetch[1 + number].wait()
        for row in range(2):
            low = field0[number, 2 : places + 2, row, :]
            high = field0[number, 2 : places + 2, 6 + row, :]
            rows_pair[2 * number + row] = select(lat_even, high, low)
            rows_gap[2 * number + row] = select(lat_even, low, high)
            own_rows[2 * row + number] = (low, high)[row]
    fetch[0].wait()
    depth_count = counts[0]
    last = depth_count + 1
    second_last = jnp.maximum(depth_count, 2)
    second = jnp.minimum(3, last)
    size = jnp.broadcast_to(depth_count.astype(F32), (8, 128))
    for number in range(2):
        up = (field0[number, last], field0[number, second_last], size)
        down = (field0[number, 2], field0[number, second], size)
        for layer in range(3):
            rim_pair[number, layer] = select(depth_even, up[layer], down[layer])
    for copy in fetch[3:]:
        copy.wait()


def beside(rows_pair, rows_gap, number, place):
    lat_even = is_even("lat")
    below = [ref[2 * number + 1, pl.ds(place, 1), :] for ref in (rows_gap, rows_pair)]
    above = [ref[2 * number, pl.ds(place, 1), :] for ref in (rows_pair, rows_gap)]
    rows = (select(lat_even, *below), select(lat_even, *above))
    return tuple(jnp.broadcast_to(x, (8, 128)) for x in rows)


def pack_gap(counts, field0, rows_pair, rows_gap, rim_pair, rim_gap):
    depth_count = counts[0]
    depth_even = is_even("depth")
    end = jnp.where(depth_even, 0, depth_count - 1)
    inward = jnp.where(depth_even, 1, jnp.maximum(depth_count - 2, 0))
    size = depth_count.astype(F32)
    row = sublanes()
    for number in range(2):
        rim_gap[number, 0] = field0[number, 2 + end]
        rim_gap[number, 1] = select(
            depth_count == 1, rim_pair[number, 0], field0[number, 2 + inward]
        )
        below, above = beside(rows_pair, rows_gap, number, end)
        rim_gap[number, 2] = jnp.where(row == 0, below, jnp.where(row == 1, above, size))


def pack_next(counts, rows_pair, rows_gap, rim_gap, order, next_pair):
    end = jnp.where(is_even("depth"), counts[0] - 1, 0)
    for number in range(2):
        next_pair[number, 0] = rim_gap[number, 0]
        below, above = beside(rows_pair, rows_gap, number, end)
        next_pair[number, 1] = jnp.where(sublanes() == 0, below, above)


def lanes():
    return lax.broadcasted_iota(jnp.int32, (8, 128), 1)


def sublanes():
    return lax.broadcasted_iota(jnp.int32, (8, 128), 0)


def left_of(x):
    return jnp.where(lanes() == 0, 0.0, pltpu.roll(x, 1, 1))


def right_of(x):
    return jnp.where(lanes() == 127, 0.0, pltpu.roll(x, 127, 1))


def row_below(x, halo_row):
    return jnp.where(sublanes() == 0, jnp.broadcast_to(halo_row, (8, 128)), pltpu.roll(x, 1, 0))


def row_above(x, halo_row):
    return jnp.where(sublanes() == 7, jnp.broadcast_to(halo_row, (8, 128)), pltpu.roll(x, 7, 0))


def stepped(heat, fuel, neighbours):
    heat_sum = neighbours[0][0]
    fuel_sum = neighbours[0][1]
    product_sum = neighbours[0][0] * neighbours[0][1]
    square_sum = neighbours[0][0] * neighbours[0][0]
    for heat_n, fuel_n in neighbours[1:]:
        heat_sum = heat_sum + heat_n
        fuel_sum = fuel_sum + fuel_n
        product_sum = product_sum + heat_n * fuel_n
        square_sum = square_sum + heat_n * heat_n
    heat_flux = (heat_sum - 6.0 * heat) + 1.5 * (square_sum - 6.0 * (heat * heat))
    fuel_flux = 0.5 * (
        (1.0 + 1.5 * heat) * (fuel_sum - 6.0 * fuel) + 1.5 * (product_sum - fuel * heat_sum)
    )
    ratio = zeldovich / expansion
    reaction = fuel * jnp.exp(ratio - ratio / ((1.0 - expansion) + expansion * heat))
    return (
        heat + time_step * (heat_flux + heat_release * reaction),
        fuel + time_step * (fuel_flux - reaction),
    )


LEAD = 8


def block_step(field, at, count, edge_rows):
    heat = [field[0, at - 1 + j] for j in range(count + 2)]
    burn = [field[1, at - 1 + j] for j in range(count + 2)]
    results = []
    for j in range(1, count + 1):
        h, b = heat[j], burn[j]
        (h_low, b_low), (h_high, b_high) = edge_rows(j - 1)
        around = [
            (heat[j - 1], burn[j - 1]),
            (heat[j + 1], burn[j + 1]),
            (row_below(h, h_low), row_below(b, b_low)),
            (row_above(h, h_high), row_above(b, b_high)),
            (left_of(h), left_of(b)),
            (right_of(h), right_of(b)),
        ]
        results.append(stepped(h, b, around))
    return results


def rows_beside(edge, sides, place):
    return [tuple(edge[n, side, pl.ds(place, 1), :] for n in range(2)) for side in sides]


def step_edges(edge0, inner, side, at, inner_at, count):
    edge_row = 1 + side
    outer_row = 3 * side

    def rows(ref, row, place):
        found = tuple(ref(n)[row(n), pl.ds(place, count), :] for n in range(2))
        return tuple(jnp.broadcast_to(x, (8, 128)) for x in found)

    def edge(row, shift):
        return rows(lambda n: edge0.at[n], lambda n: row, at + shift)

    heat, burn = edge(edge_row, 0)
    around = [
        edge(edge_row, -1),
        edge(edge_row, 1),
        edge(outer_row, 0),
        rows(lambda n: inner, lambda n: 2 * side + n, inner_at),
        (left_of(heat), left_of(burn)),
        (right_of(heat), right_of(burn)),
    ]
    outside = lax.axis_index("lat") == (0 if side == 0 else lax.axis_size("lat") - 1)
    return [jnp.where(outside, 0.0, x) for x in stepped(heat, burn, around)]


def look_up(low_table, rise_table, value):
    bins = low_table.shape[2]
    position = jnp.clip(value, 0.0, 1.0) * (bins - 1)
    lower = jnp.minimum(position.astype(jnp.int32), bins - 2)
    fraction = position - lower.astype(F32)

    def at(entry):
        low = jnp.take_along_axis(low_table[entry], lower, axis=1)
        rise = jnp.take_along_axis(rise_table[entry], lower, axis=1)
        return low + fraction * rise

    return at


def add_layer(sums, number, at, alive):
    for f in range(2 * number, 2 * number + 2):
        gone, red, green, blue = sums[4 * f : 4 * f + 4]
        depth = jnp.where(alive, at(4 * f + 3), 0.0)
        gain = depth * (1.0 + depth * (0.5 + depth * (1.0 / 6.0)))
        gain = gain + gone * gain
        sums[4 * f] = gone + gain
        sums[4 * f + 1] = red + gain * at(4 * f)
        sums[4 * f + 2] = green + gain * at(4 * f + 1)
        sums[4 * f + 3] = blue + gain * at(4 * f + 2)


def inner_layers(
    first, count, unroll, depth_count, field1, edge1, tables, results, sums, after=None
):
    def body(block, carry):
        start = first + block * unroll

        def edge_rows(j):
            return rows_beside(edge1, (0, 1), start + j)

        carry = list(carry)
        for j, new in enumerate(block_step(field1, start + 1, unroll, edge_rows)):
            for number in range(2):
                value = jnp.where(start + j < depth_count, new[number], 0.0)
                results[number][start + j] = value
                add_layer(carry, number, look_up(*tables, value), start + j < depth_count - 2)
        if after is not None:
            after(start, unroll)
        return tuple(carry)

    return lax.fori_loop(0, count // unroll, body, tuple(sums))


def early_step(
    places,
    functions,
    all_layers,
    counts,
    choice,
    camera,
    field0,
    library,
    own_rows,
    rows_pair,
    rows_gap,
    order,
    field1,
    edge0,
    edge1,
    low_table,
    rise_table,
    theta_next,
    fuel_next,
    sums,
    tables,
):
    lat_even = is_even("lat")
    bins = library.shape[2]
    tables[...] = library[...].astype(F32)
    per_cell = 3.0 / all_layers
    for f in range(functions):
        sign = jnp.where(camera[f] == 0, -per_cell, per_cell)
        for c in range(4):
            low = jnp.broadcast_to(tables[choice[f], c : c + 1, :], (8, bins))
            rise = pltpu.roll(low, bins - 1, 1) - low
            if c == 3:
                low = low * sign
                rise = rise * sign
            low_table[4 * f + c] = low
            rise_table[4 * f + c] = rise

    for number in range(2):
        for row in range(2):
            pair, gap = rows_pair[2 * number + row], rows_gap[2 * number + row]
            edge0[number, row, LEAD : LEAD + places] = select(lat_even, gap, pair)
            edge0[number, 2 + row, LEAD : LEAD + places] = select(lat_even, pair, gap)

    for block in range(places // 8):
        for side in range(2):
            fresh = step_edges(edge0, own_rows, side, LEAD + 8 * block, 8 * block, 8)
            for number in range(2):
                edge1[number, side, 8 * block : 8 * block + 8] = fresh[number]

    def first_step(block, carry):
        start = block * UNROLL_1

        def edge_rows(j):
            return rows_beside(edge0, (1, 2), LEAD + start + j)

        for j, new in enumerate(block_step(field0, start + 2, UNROLL_1, edge_rows)):
            for number in range(2):
                field1[number, start + 1 + j] = new[number]
        return carry

    lax.fori_loop(0, places // UNROLL_1, first_step, 0)
    zero = jnp.zeros((8, 128), F32)
    for out in (theta_next, fuel_next):
        for place in (0, 1, places - 2, places - 1):
            out[place] = zero
    found = inner_layers(
        2,
        *WINDOWS[0],
        counts[0],
        field1,
        edge1,
        (low_table, rise_table),
        (theta_next, fuel_next),
        [zero] * (4 * functions),
    )
    for entry, value in enumerate(found):
        sums[entry] = value


def middle_step(
    places,
    counts,
    field1,
    edge1,
    low_table,
    rise_table,
    order,
    theta_in,
    fuel_in,
    sums_in,
    theta_out,
    fuel_out,
    theta_next,
    fuel_next,
    sums,
    copies,
):
    def leave(number, first, count):
        return pltpu.make_async_copy(
            (theta_next, fuel_next)[number].at[pl.ds(first, count)],
            (theta_out, fuel_out)[number].at[pl.ds(first, count)],
            copies.at[number],
        )

    def start_leaving(first, count):
        for number in range(2):
            leave(number, first, count).start()

    first = 2 + WINDOWS[0][0]
    start_leaving(0, first)
    start_leaving(places - 2, 2)
    found = inner_layers(
        first,
        *WINDOWS[1],
        counts[0],
        field1,
        edge1,
        (low_table, rise_table),
        (theta_next, fuel_next),
        [sums_in[entry] for entry in range(sums_in.shape[0])],
        start_leaving,
    )
    for entry, value in enumerate(found):
        sums[entry] = value
    for number in range(2):
        leave(number, 0, places).wait()


def late_step(
    functions,
    counts,
    camera,
    field0_in,
    field1_in,
    edge0_in,
    edge1_in,
    low_table,
    rise_table,
    sums,
    own_rows,
    rim_pair,
    rim_gap,
    next_pair,
    image,
    ends,
    field0,
    field1,
    edge0,
    edge1,
):
    depth_count = counts[0]
    depth_even = is_even("depth")

    def sides(pair, gap):
        return select(depth_even, gap, pair), select(depth_even, pair, gap)

    pair_size = rim_pair[0, 2]
    gap_size = jnp.broadcast_to(rim_gap[0, 2, 2:3], (8, 128))
    below_size, above_size = sides(pair_size, gap_size)
    for number in range(2):
        nearest = sides(rim_pair[number, 0], rim_gap[number, 0])
        second = jnp.where(pair_size == 1.0, next_pair[number, 0], rim_pair[number, 1])
        second = sides(second, rim_gap[number, 1])
        rows = sides(next_pair[number, 1], rim_gap[number, 2])
        field0[number, 0] = second[0]
        field0[number, 1] = nearest[0]
        field0[number, depth_count + 2] = nearest[1]
        field0[number, depth_count + 3] = second[1]
        for side in range(2):
            edge0[number, 1 + side, LEAD - 1 : LEAD] = rows[0][side : side + 1]
            edge0[number, 1 + side, pl.ds(LEAD + depth_count, 1)] = rows[1][side : side + 1]
    for place in (0, depth_count - 1):
        for side in range(2):
            fresh = step_edges(edge0, own_rows, side, LEAD + place, place, 1)
            for number in range(2):
                edge1[number, side, pl.ds(place, 1)] = fresh[number][0:1]
    for place, size in (
        (-1, below_size),
        (0, None),
        (depth_count - 1, None),
        (depth_count, above_size),
    ):

        def edge_rows(j, place=place):
            return rows_beside(edge0, (1, 2), LEAD + place)

        (fresh,) = block_step(field0, place + 2, 1, edge_rows)
        for number in range(2):
            value = fresh[number]
            field1[number, place + 1] = (
                value if size is None else jnp.where(size > 0.0, value, 0.0)
            )

    zero = jnp.zeros((8, 128), F32)
    pairs = ((0, 0), (2, jnp.maximum(depth_count - 2, 2)))
    stepped_ends = []
    for slot, start in pairs:

        def edge_rows(j, start=start):
            return rows_beside(edge1, (0, 1), start + j)

        fresh = block_step(field1, start + 1, 2, edge_rows)
        alive = [start + j < depth_count for j in range(2)]
        fresh = [[jnp.where(alive[j], value, 0.0) for value in fresh[j]] for j in range(2)]
        stepped_ends.append((alive, fresh))
        for number in range(2):
            for j in range(2):
                ends[number, slot + j] = fresh[j][number]
    segments = []
    for alive, fresh in stepped_ends:
        segment = [zero] * (4 * functions)
        for j in range(2):
            for number in range(2):
                at = look_up(low_table, rise_table, fresh[j][number])
                add_layer(segment, number, at, alive[j])
        segments.append(segment)

    head, tail = segments
    channels = []
    for f in range(functions):
        through_head = 1.0 + head[4 * f]
        through_body = 1.0 + sums[4 * f]
        gone, red, green, blue = [
            head[4 * f + c]
            + through_head * (sums[4 * f + c] + through_body * tail[4 * f + c])
            for c in range(4)
        ]
        scale = jnp.where(camera[f] == 0, -1.0, 1.0 / (1.0 + gone))
        channels += [red * scale, green * scale, blue * scale, gone * scale]

    group = lanes() // 16
    for half in range(2):
        regs = channels[8 * half : 8 * half + 8]
        for bit in (1, 2, 4):
            upper = (group & bit) != 0
            fresh = list(regs)
            for i in range(8):
                if i & bit:
                    continue
                a, b = regs[i], regs[i | bit]
                fresh[i] = jnp.where(upper, pltpu.roll(b, 16 * bit, 1), a)
                fresh[i | bit] = jnp.where(upper, b, pltpu.roll(a, 128 - 16 * bit, 1))
            regs = fresh
        for g in range(8):
            image[pl.ds(2 * g + half, 8, stride=16), :] = regs[g]


def composite(
    counts, camera, pieces, ends, theta_in, fuel_in, image_out, theta_next, fuel_next, image, copies
):
    sources = pieces.shape[0] // 2
    leave = [
        pltpu.make_async_copy(
            ends.at[number, pl.ds(slot, 2)],
            out.at[pl.ds(place, 2)],
            copies.at[slot + number],
        )
        for number, out in enumerate((theta_next, fuel_next))
        for slot, place in ((0, 0), (2, jnp.maximum(counts[0] - 2, 2)))
    ]
    for copy in leave:
        copy.start()
    leave.append(pltpu.make_async_copy(image, image_out, copies.at[4]))
    lane = lanes()
    row = sublanes()
    opacity_lane = lane // 64 * 64 + 48 + lane % 16
    for half in range(2):
        forward = jnp.where(
            lane < 64,
            (camera[2 * half] == 0).astype(jnp.int32),
            (camera[2 * half + 1] == 0).astype(jnp.int32),
        ) == 1
        values, clear, through = [], [], []
        carry = jnp.ones((8, 128), F32)
        for block in range(sources // 8):
            value = pieces[pl.ds(16 * block + half, 8, stride=2), :]
            passing = 1.0 - jnp.take_along_axis(value, opacity_lane, axis=1)
            product = passing
            for shift in (1, 2, 4):
                product = product * jnp.where(row >= shift, pltpu.roll(product, shift, 0), 1.0)
            product = product * carry
            carry = jnp.broadcast_to(product[7:8], (8, 128))
            values.append(value)
            clear.append(passing)
            through.append(product)
        total = jnp.zeros((8, 128), F32)
        for value, passing, product in zip(values, clear, through):
            top = jnp.where(forward, product, carry)
            bottom = jnp.where(forward, passing, product)
            total = total + value * (top / bottom)
        line = jnp.sum(total, axis=0, keepdims=True)
        for clo in range(8):
            channel = 8 * half + clo
            image[channel // 4, channel % 4] = line[:, 16 * clo : 16 * clo + 16]
    leave[-1].start()
    for copy in leave:
        copy.wait()


def swapped(array, axis, first):
    count = lax.axis_size(axis)
    pairs = []
    for i in range(first, count - 1, 2):
        pairs += [(i, i + 1), (i + 1, i)]
    return lax.ppermute(array, axis, pairs)


def held(array):
    return pltpu.with_memory_space_constraint(array, VMEM)


def in_hbm(array):
    return pltpu.with_memory_space_constraint(array, pltpu.HBM)


def params():
    return pltpu.CompilerParams(vmem_limit_bytes=16 * 1024 * 1024)


def anywhere():
    return pl.BlockSpec(memory_space=pl.ANY)


def in_scalars(array):
    return pltpu.with_memory_space_constraint(array, SMEM)


def first_kernel(counts, choice, camera, theta, fuel, library):
    places = theta.shape[0]
    rows = VMEM((4, places, 128), F32)
    rim = VMEM((2, 3, 8, 128), F32)
    return pl.pallas_call(
        pack_rows,
        out_shape=tuple(SMEM(x.shape, jnp.int32) for x in (counts, choice, camera))
        + (VMEM(library.shape, library.dtype), VMEM((2, places + 4, 8, 128), F32))
        + (rows, rows, rows, rim),
        in_specs=[anywhere()] * 6,
        out_specs=(in_smem(),) * 3 + (in_vmem(),) * 6,
        scratch_shapes=[pltpu.SemaphoreType.DMA((6,))],
        compiler_params=params(),
        name="pack_rows",
    )(counts, *map(in_hbm, (choice, camera, theta, fuel, library)))


def rim_kernel(body, layers, counts, *arrays):
    return pl.pallas_call(
        body,
        out_shape=VMEM((2, layers, 8, 128), F32),
        in_specs=[in_smem()] + [in_vmem()] * len(arrays),
        out_specs=in_vmem(),
        compiler_params=params(),
        name=body.__name__,
    )(in_scalars(counts), *map(held, arrays))


def cost(flops):
    return pl.CostEstimate(flops=flops, bytes_accessed=10**6, transcendentals=10**5)


def early_kernel(devices, counts, choice, camera, field0, library, *rows):
    places = field0.shape[1] - 4
    functions = choice.shape[0]
    bins = library.shape[2]
    table = VMEM((4 * functions, 8, bins), F32)
    field = VMEM((places, 8, 128), F32)
    return pl.pallas_call(
        functools.partial(early_step, places, functions, float(MEAN_DEPTH * devices)),
        out_shape=(
            VMEM((2, places + 2, 8, 128), F32),
            VMEM((2, 4, places + 16, 128), F32),
            VMEM((2, 2, places, 128), F32),
            table,
            table,
            field,
            field,
            VMEM((4 * functions, 8, 128), F32),
        ),
        in_specs=[in_smem()] * 3 + [in_vmem()] * 6,
        out_specs=(in_vmem(),) * 8,
        scratch_shapes=[VMEM(library.shape, F32)],
        compiler_params=params(),
        cost_estimate=cost(10**7),
        name="early_step",
    )(*map(in_scalars, (counts, choice, camera)), *map(held, (field0, library, *rows)))


def middle_kernel(counts, *arrays):
    theta_next, fuel_next, sums = arrays[-3:]
    field = jax.ShapeDtypeStruct(theta_next.shape, F32)
    return pl.pallas_call(
        functools.partial(middle_step, theta_next.shape[0]),
        out_shape=(field, field) + tuple(VMEM(x.shape, F32) for x in (theta_next, fuel_next, sums)),
        in_specs=[in_smem()] + [in_vmem()] * len(arrays),
        out_specs=(anywhere(),) * 2 + (in_vmem(),) * 3,
        scratch_shapes=[pltpu.SemaphoreType.DMA((2,))],
        input_output_aliases={len(arrays) - 2 + i: 2 + i for i in range(2)},
        compiler_params=params(),
        cost_estimate=cost(10**7),
        name="middle_step",
    )(in_scalars(counts), *map(held, arrays))


def late_kernel(devices, counts, camera, *arrays):
    functions = camera.shape[0]
    kept = arrays[:4]
    image, ends, *_ = pl.pallas_call(
        functools.partial(late_step, functions),
        out_shape=(VMEM((2 * devices, 128), F32), VMEM((2, 4, 8, 128), F32))
        + tuple(VMEM(x.shape, F32) for x in kept),
        in_specs=[in_smem()] * 2 + [in_vmem()] * len(arrays),
        out_specs=(in_vmem(),) * 6,
        input_output_aliases={2 + i: 2 + i for i in range(4)},
        compiler_params=params(),
        cost_estimate=cost(10**6),
        name="late_step",
    )(*map(in_scalars, (counts, camera)), *map(held, arrays))
    return image, ends


def last_kernel(functions, counts, camera, pieces, ends, *fields):
    field = jax.ShapeDtypeStruct(fields[0].shape, F32)
    image = (functions, 4, 1, 16)
    return pl.pallas_call(
        composite,
        out_shape=(jax.ShapeDtypeStruct(image, F32), field, field),
        in_specs=[in_smem()] * 2 + [in_vmem()] * 2 + [anywhere()] * 2,
        out_specs=(anywhere(),) * 3,
        scratch_shapes=[VMEM(image, F32), pltpu.SemaphoreType.DMA((5,))],
        input_output_aliases={4: 1, 5: 2},
        compiler_params=params(),
        name="composite",
    )(*map(in_scalars, (counts, camera)), *map(held, (pieces, ends)), *map(in_hbm, fields))


def on_device(
    thermal_values,
    reactant_fraction,
    active_sheet_number,
    colour_lookup_library,
    colour_lookup_choice,
    camera_direction,
):
    devices = lax.axis_size("depth")
    counts, choice, camera, library, field0, own_rows, *messages = first_kernel(
        active_sheet_number,
        colour_lookup_choice,
        camera_direction,
        thermal_values,
        reactant_fraction,
        colour_lookup_library,
    )
    rows_pair = swapped(messages[0], "lat", 0)
    rows_gap = swapped(messages[1], "lat", 1)
    rim_pair = swapped(messages[2], "depth", 0)
    order = rim_kernel(pack_gap, 3, counts, field0, rows_pair, rows_gap, rim_pair)
    rim_gap = swapped(order, "depth", 1)
    field1, edge0, edge1, low_table, rise_table, theta_next, fuel_next, sums = early_kernel(
        devices, counts, choice, camera, field0, library, own_rows, rows_pair, rows_gap, order
    )
    order = rim_kernel(pack_next, 2, counts, rows_pair, rows_gap, rim_gap, sums)
    next_pair = swapped(order, "depth", 0)
    theta_next, fuel_next, _, _, sums = middle_kernel(
        counts, field1, edge1, low_table, rise_table, order, theta_next, fuel_next, sums
    )
    pieces, ends = late_kernel(
        devices,
        counts,
        camera,
        field0,
        field1,
        edge0,
        edge1,
        low_table,
        rise_table,
        sums,
        own_rows,
        rim_pair,
        rim_gap,
        next_pair,
    )
    pieces = lax.all_to_all(pieces, "depth", 0, 0, tiled=True)
    image, theta_next, fuel_next = last_kernel(
        choice.shape[0], counts, camera, pieces, ends, theta_next, fuel_next
    )
    return (theta_next, fuel_next, image)


def solution(mesh):
    placed = (P("depth", "lat", None), P("depth", "lat", None), P("depth"), P(), P(), P())
    return jax.shard_map(
        on_device,
        mesh=mesh,
        in_specs=placed,
        out_specs=(P("depth", "lat", None), P("depth", "lat", None), P(None, None, "lat", "depth")),
        check_vma=False,
    )
```

```python
import functools

import jax
import jax.numpy as jnp
from jax import lax
from jax.experimental import pallas as pl
from jax.experimental.pallas import tpu as pltpu
from jax.sharding import PartitionSpec as P

MEAN_DEPTH = 32
STEPS = 2

time_step = 0.03
heat_release = 2.0
zeldovich = 8.0
expansion = 0.8

VMEM = pltpu.VMEM
SMEM = pltpu.SMEM
F32 = jnp.float32


def in_vmem():
    return pl.BlockSpec(memory_space=VMEM)


def in_smem():
    return pl.BlockSpec(memory_space=SMEM)


UNROLL_1 = 16
WINDOWS = ((20, 20), (40, 20))


def is_even(axis):
    return lax.rem(lax.axis_index(axis), 2) == 0


def select(which, first, second):
    return jnp.where(which, first, second)


def pack_rows(
    counts_in,
    choice_in,
    camera_in,
    theta,
    fuel,
    library_in,
    counts,
    choice,
    camera,
    library,
    field0,
    own_rows,
    rows_pair,
    rows_gap,
    rim_pair,
    copies,
):
    places = theta.shape[0]
    moves = [
        (counts_in, counts),
        (theta, field0.at[0, pl.ds(2, places)]),
        (fuel, field0.at[1, pl.ds(2, places)]),
        (choice_in, choice),
        (camera_in, camera),
        (library_in, library),
    ]
    fetch = [
        pltpu.make_async_copy(source, target, copies.at[number])
        for number, (source, target) in enumerate(moves)
    ]
    for copy in fetch:
        copy.start()
    lat_even, depth_even = is_even("lat"), is_even("depth")
    for number in range(2):
        fetch[1 + number].wait()
        for row in range(2):
            low = field0[number, 2 : places + 2, row, :]
            high = field0[number, 2 : places + 2, 6 + row, :]
            rows_pair[2 * number + row] = select(lat_even, high, low)
            rows_gap[2 * number + row] = select(lat_even, low, high)
            own_rows[2 * row + number] = (low, high)[row]
    fetch[0].wait()
    depth_count = counts[0]
    for number in range(2):
        rim_pair[number] = select(
            depth_even, field0[number, depth_count + 1], field0[number, 2]
        )
    for copy in fetch[3:]:
        copy.wait()


def beside(rows_pair, rows_gap, place, rest):
    lat_even = is_even("lat")
    row = sublanes()
    out = jnp.broadcast_to(rest, (8, 128))
    for number in range(2):
        below = [ref[2 * number + 1, pl.ds(place, 1), :] for ref in (rows_gap, rows_pair)]
        above = [ref[2 * number, pl.ds(place, 1), :] for ref in (rows_pair, rows_gap)]
        for side, rows in enumerate((below, above)):
            line = jnp.broadcast_to(select(lat_even, *rows), (8, 128))
            out = jnp.where(row == 2 * number + side, line, out)
    return out


def end_places(upward, depth_count):
    return (
        jnp.where(upward, depth_count + 1, 2),
        jnp.where(upward, jnp.maximum(depth_count, 2), 3),
    )


def pack_gap(counts, field0, rows_pair, rows_gap, rim_pair, rim_gap):
    depth_count = counts[0]
    end, inward = end_places(jnp.logical_not(is_even("depth")), depth_count)
    for number in range(2):
        rim_gap[number] = field0[number, end]
        rim_gap[2 + number] = select(depth_count == 1, rim_pair[number], field0[number, inward])
    rim_gap[4] = beside(rows_pair, rows_gap, end - 2, depth_count.astype(F32))


def pack_next(counts, field0, rows_pair, rows_gap, rim_gap, order, next_pair):
    depth_count = counts[0]
    end, inward = end_places(is_even("depth"), depth_count)
    for number in range(2):
        next_pair[number] = select(depth_count == 1, rim_gap[number], field0[number, inward])
    next_pair[2] = beside(rows_pair, rows_gap, end - 2, 0.0)


def lanes():
    return lax.broadcasted_iota(jnp.int32, (8, 128), 1)


def sublanes():
    return lax.broadcasted_iota(jnp.int32, (8, 128), 0)


def left_of(x):
    return jnp.where(lanes() == 0, 0.0, pltpu.roll(x, 1, 1))


def right_of(x):
    return jnp.where(lanes() == 127, 0.0, pltpu.roll(x, 127, 1))


def row_below(x, halo_row):
    return jnp.where(sublanes() == 0, jnp.broadcast_to(halo_row, (8, 128)), pltpu.roll(x, 1, 0))


def row_above(x, halo_row):
    return jnp.where(sublanes() == 7, jnp.broadcast_to(halo_row, (8, 128)), pltpu.roll(x, 7, 0))


def stepped(heat, fuel, neighbours):
    heat_sum = neighbours[0][0]
    fuel_sum = neighbours[0][1]
    product_sum = neighbours[0][0] * neighbours[0][1]
    square_sum = neighbours[0][0] * neighbours[0][0]
    for heat_n, fuel_n in neighbours[1:]:
        heat_sum = heat_sum + heat_n
        fuel_sum = fuel_sum + fuel_n
        product_sum = product_sum + heat_n * fuel_n
        square_sum = square_sum + heat_n * heat_n
    heat_flux = (heat_sum - 6.0 * heat) + 1.5 * (square_sum - 6.0 * (heat * heat))
    fuel_flux = 0.5 * (
        (1.0 + 1.5 * heat) * (fuel_sum - 6.0 * fuel) + 1.5 * (product_sum - fuel * heat_sum)
    )
    ratio = zeldovich / expansion
    reaction = fuel * jnp.exp(ratio - ratio / ((1.0 - expansion) + expansion * heat))
    return (
        heat + time_step * (heat_flux + heat_release * reaction),
        fuel + time_step * (fuel_flux - reaction),
    )


LEAD = 8


def block_step(field, at, count, edge_rows):
    heat = [field[0, at - 1 + j] for j in range(count + 2)]
    burn = [field[1, at - 1 + j] for j in range(count + 2)]
    results = []
    for j in range(1, count + 1):
        h, b = heat[j], burn[j]
        (h_low, b_low), (h_high, b_high) = edge_rows(j - 1)
        around = [
            (heat[j - 1], burn[j - 1]),
            (heat[j + 1], burn[j + 1]),
            (row_below(h, h_low), row_below(b, b_low)),
            (row_above(h, h_high), row_above(b, b_high)),
            (left_of(h), left_of(b)),
            (right_of(h), right_of(b)),
        ]
        results.append(stepped(h, b, around))
    return results


def rows_beside(edge, sides, place):
    return [tuple(edge[n, side, pl.ds(place, 1), :] for n in range(2)) for side in sides]


def step_edges(edge0, inner, side, at, inner_at, count):
    edge_row = 1 + side
    outer_row = 3 * side

    def rows(ref, row, place):
        found = tuple(ref(n)[row(n), pl.ds(place, count), :] for n in range(2))
        return tuple(jnp.broadcast_to(x, (8, 128)) for x in found)

    def edge(row, shift):
        return rows(lambda n: edge0.at[n], lambda n: row, at + shift)

    heat, burn = edge(edge_row, 0)
    around = [
        edge(edge_row, -1),
        edge(edge_row, 1),
        edge(outer_row, 0),
        rows(lambda n: inner, lambda n: 2 * side + n, inner_at),
        (left_of(heat), left_of(burn)),
        (right_of(heat), right_of(burn)),
    ]
    outside = lax.axis_index("lat") == (0 if side == 0 else lax.axis_size("lat") - 1)
    return [jnp.where(outside, 0.0, x) for x in stepped(heat, burn, around)]


def look_up(low_table, rise_table, value):
    bins = low_table.shape[2]
    position = jnp.clip(value, 0.0, 1.0) * (bins - 1)
    lower = jnp.minimum(position.astype(jnp.int32), bins - 2)
    fraction = position - lower.astype(F32)

    def at(entry):
        low = jnp.take_along_axis(low_table[entry], lower, axis=1)
        rise = jnp.take_along_axis(rise_table[entry], lower, axis=1)
        return low + fraction * rise

    return at


def add_layer(sums, number, at, alive):
    for f in range(2 * number, 2 * number + 2):
        gone, red, green, blue = sums[4 * f : 4 * f + 4]
        depth = jnp.where(alive, at(4 * f + 3), 0.0)
        gain = depth * (1.0 + depth * (0.5 + depth * (1.0 / 6.0)))
        gain = gain + gone * gain
        sums[4 * f] = gone + gain
        sums[4 * f + 1] = red + gain * at(4 * f)
        sums[4 * f + 2] = green + gain * at(4 * f + 1)
        sums[4 * f + 3] = blue + gain * at(4 * f + 2)


def inner_layers(
    first, count, unroll, depth_count, field1, edge1, tables, results, sums, after=None
):
    def body(block, carry):
        start = first + block * unroll

        def edge_rows(j):
            return rows_beside(edge1, (0, 1), start + j)

        carry = list(carry)
        for j, new in enumerate(block_step(field1, start + 1, unroll, edge_rows)):
            for number in range(2):
                value = jnp.where(start + j < depth_count, new[number], 0.0)
                results[number][start + j] = value
                add_layer(carry, number, look_up(*tables, value), start + j < depth_count - 2)
        if after is not None:
            after(start, unroll)
        return tuple(carry)

    return lax.fori_loop(0, count // unroll, body, tuple(sums))


def early_step(
    places,
    functions,
    all_layers,
    counts,
    choice,
    camera,
    field0,
    library,
    own_rows,
    rows_pair,
    rows_gap,
    order,
    field1,
    edge0,
    edge1,
    low_table,
    rise_table,
    theta_next,
    fuel_next,
    sums,
    tables,
):
    lat_even = is_even("lat")
    bins = library.shape[2]
    tables[...] = library[...].astype(F32)
    per_cell = 3.0 / all_layers
    for f in range(functions):
        sign = jnp.where(camera[f] == 0, -per_cell, per_cell)
        for c in range(4):
            low = jnp.broadcast_to(tables[choice[f], c : c + 1, :], (8, bins))
            rise = pltpu.roll(low, bins - 1, 1) - low
            if c == 3:
                low = low * sign
                rise = rise * sign
            low_table[4 * f + c] = low
            rise_table[4 * f + c] = rise

    for number in range(2):
        for row in range(2):
            pair, gap = rows_pair[2 * number + row], rows_gap[2 * number + row]
            edge0[number, row, LEAD : LEAD + places] = select(lat_even, gap, pair)
            edge0[number, 2 + row, LEAD : LEAD + places] = select(lat_even, pair, gap)

    for block in range(places // 8):
        for side in range(2):
            fresh = step_edges(edge0, own_rows, side, LEAD + 8 * block, 8 * block, 8)
            for number in range(2):
                edge1[number, side, 8 * block : 8 * block + 8] = fresh[number]

    def first_step(block, carry):
        start = block * UNROLL_1

        def edge_rows(j):
            return rows_beside(edge0, (1, 2), LEAD + start + j)

        for j, new in enumerate(block_step(field0, start + 2, UNROLL_1, edge_rows)):
            for number in range(2):
                field1[number, start + 1 + j] = new[number]
        return carry

    lax.fori_loop(0, places // UNROLL_1, first_step, 0)
    zero = jnp.zeros((8, 128), F32)
    for out in (theta_next, fuel_next):
        for place in (0, 1, places - 2, places - 1):
            out[place] = zero
    found = inner_layers(
        2,
        *WINDOWS[0],
        counts[0],
        field1,
        edge1,
        (low_table, rise_table),
        (theta_next, fuel_next),
        [zero] * (4 * functions),
    )
    for entry, value in enumerate(found):
        sums[entry] = value


def middle_step(
    places,
    counts,
    field1,
    edge1,
    low_table,
    rise_table,
    order,
    theta_in,
    fuel_in,
    sums_in,
    theta_out,
    fuel_out,
    theta_next,
    fuel_next,
    sums,
    copies,
):
    def leave(number, first, count):
        return pltpu.make_async_copy(
            (theta_next, fuel_next)[number].at[pl.ds(first, count)],
            (theta_out, fuel_out)[number].at[pl.ds(first, count)],
            copies.at[number],
        )

    def start_leaving(first, count):
        for number in range(2):
            leave(number, first, count).start()

    first = 2 + WINDOWS[0][0]
    start_leaving(0, first)
    start_leaving(places - 2, 2)
    found = inner_layers(
        first,
        *WINDOWS[1],
        counts[0],
        field1,
        edge1,
        (low_table, rise_table),
        (theta_next, fuel_next),
        [sums_in[entry] for entry in range(sums_in.shape[0])],
        start_leaving,
    )
    for entry, value in enumerate(found):
        sums[entry] = value
    for number in range(2):
        leave(number, 0, places).wait()


def late_step(
    functions,
    counts,
    camera,
    field0_in,
    field1_in,
    edge0_in,
    edge1_in,
    low_table,
    rise_table,
    sums,
    own_rows,
    rim_pair,
    rim_gap,
    next_pair,
    image,
    ends,
    field0,
    field1,
    edge0,
    edge1,
):
    depth_count = counts[0]
    depth_even = is_even("depth")

    def sides(pair, gap):
        return select(depth_even, gap, pair), select(depth_even, pair, gap)

    gap_size = jnp.broadcast_to(rim_gap[4, 4:5], (8, 128))
    below_size, above_size = sides(jnp.ones((8, 128), F32), gap_size)
    for number in range(2):
        nearest = sides(rim_pair[number], rim_gap[number])
        second = sides(next_pair[number], rim_gap[2 + number])
        rows = sides(
            next_pair[2, 2 * number : 2 * number + 2], rim_gap[4, 2 * number : 2 * number + 2]
        )
        field0[number, 0] = second[0]
        field0[number, 1] = nearest[0]
        field0[number, depth_count + 2] = nearest[1]
        field0[number, depth_count + 3] = second[1]
        for side in range(2):
            edge0[number, 1 + side, LEAD - 1 : LEAD] = rows[0][side : side + 1]
            edge0[number, 1 + side, pl.ds(LEAD + depth_count, 1)] = rows[1][side : side + 1]
    for place in (0, depth_count - 1):
        for side in range(2):
            fresh = step_edges(edge0, own_rows, side, LEAD + place, place, 1)
            for number in range(2):
                edge1[number, side, pl.ds(place, 1)] = fresh[number][0:1]
    for place, size in (
        (-1, below_size),
        (0, None),
        (depth_count - 1, None),
        (depth_count, above_size),
    ):

        def edge_rows(j, place=place):
            return rows_beside(edge0, (1, 2), LEAD + place)

        (fresh,) = block_step(field0, place + 2, 1, edge_rows)
        for number in range(2):
            value = fresh[number]
            field1[number, place + 1] = (
                value if size is None else jnp.where(size > 0.0, value, 0.0)
            )

    zero = jnp.zeros((8, 128), F32)
    pairs = ((0, 0), (2, jnp.maximum(depth_count - 2, 2)))
    stepped_ends = []
    for slot, start in pairs:

        def edge_rows(j, start=start):
            return rows_beside(edge1, (0, 1), start + j)

        fresh = block_step(field1, start + 1, 2, edge_rows)
        alive = [start + j < depth_count for j in range(2)]
        fresh = [[jnp.where(alive[j], value, 0.0) for value in fresh[j]] for j in range(2)]
        stepped_ends.append((alive, fresh))
        for number in range(2):
            for j in range(2):
                ends[number, slot + j] = fresh[j][number]
    segments = []
    for alive, fresh in stepped_ends:
        segment = [zero] * (4 * functions)
        for j in range(2):
            for number in range(2):
                at = look_up(low_table, rise_table, fresh[j][number])
                add_layer(segment, number, at, alive[j])
        segments.append(segment)

    head, tail = segments
    channels = []
    for f in range(functions):
        through_head = 1.0 + head[4 * f]
        through_body = 1.0 + sums[4 * f]
        gone, red, green, blue = [
            head[4 * f + c]
            + through_head * (sums[4 * f + c] + through_body * tail[4 * f + c])
            for c in range(4)
        ]
        scale = jnp.where(camera[f] == 0, -1.0, 1.0 / (1.0 + gone))
        channels += [red * scale, green * scale, blue * scale, gone * scale]

    group = lanes() // 16
    for half in range(2):
        regs = channels[8 * half : 8 * half + 8]
        for bit in (1, 2, 4):
            upper = (group & bit) != 0
            fresh = list(regs)
            for i in range(8):
                if i & bit:
                    continue
                a, b = regs[i], regs[i | bit]
                fresh[i] = jnp.where(upper, pltpu.roll(b, 16 * bit, 1), a)
                fresh[i | bit] = jnp.where(upper, b, pltpu.roll(a, 128 - 16 * bit, 1))
            regs = fresh
        for g in range(8):
            image[pl.ds(2 * g + half, 8, stride=16), :] = regs[g]


def composite(
    counts, camera, pieces, ends, theta_in, fuel_in, image_out, theta_next, fuel_next, image, copies
):
    sources = pieces.shape[0] // 2
    leave = [
        pltpu.make_async_copy(
            ends.at[number, pl.ds(slot, 2)],
            out.at[pl.ds(place, 2)],
            copies.at[slot + number],
        )
        for number, out in enumerate((theta_next, fuel_next))
        for slot, place in ((0, 0), (2, jnp.maximum(counts[0] - 2, 2)))
    ]
    for copy in leave:
        copy.start()
    leave.append(pltpu.make_async_copy(image, image_out, copies.at[4]))
    lane = lanes()
    row = sublanes()
    opacity_lane = lane // 64 * 64 + 48 + lane % 16
    for half in range(2):
        forward = jnp.where(
            lane < 64,
            (camera[2 * half] == 0).astype(jnp.int32),
            (camera[2 * half + 1] == 0).astype(jnp.int32),
        ) == 1
        values, clear, through = [], [], []
        carry = jnp.ones((8, 128), F32)
        for block in range(sources // 8):
            value = pieces[pl.ds(16 * block + half, 8, stride=2), :]
            passing = 1.0 - jnp.take_along_axis(value, opacity_lane, axis=1)
            product = passing
            for shift in (1, 2, 4):
                product = product * jnp.where(row >= shift, pltpu.roll(product, shift, 0), 1.0)
            product = product * carry
            carry = jnp.broadcast_to(product[7:8], (8, 128))
            values.append(value)
            clear.append(passing)
            through.append(product)
        total = jnp.zeros((8, 128), F32)
        for value, passing, product in zip(values, clear, through):
            top = jnp.where(forward, product, carry)
            bottom = jnp.where(forward, passing, product)
            total = total + value * (top / bottom)
        line = jnp.sum(total, axis=0, keepdims=True)
        for clo in range(8):
            channel = 8 * half + clo
            image[channel // 4, channel % 4] = line[:, 16 * clo : 16 * clo + 16]
    leave[-1].start()
    for copy in leave:
        copy.wait()


def swapped(array, axis, first):
    count = lax.axis_size(axis)
    pairs = []
    for i in range(first, count - 1, 2):
        pairs += [(i, i + 1), (i + 1, i)]
    return lax.ppermute(array, axis, pairs)


def held(array):
    return pltpu.with_memory_space_constraint(array, VMEM)


def in_hbm(array):
    return pltpu.with_memory_space_constraint(array, pltpu.HBM)


def params():
    return pltpu.CompilerParams(vmem_limit_bytes=16 * 1024 * 1024)


def anywhere():
    return pl.BlockSpec(memory_space=pl.ANY)


def in_scalars(array):
    return pltpu.with_memory_space_constraint(array, SMEM)


def first_kernel(counts, choice, camera, theta, fuel, library):
    places = theta.shape[0]
    rows = VMEM((4, places, 128), F32)
    rim = VMEM((2, 8, 128), F32)
    return pl.pallas_call(
        pack_rows,
        out_shape=tuple(SMEM(x.shape, jnp.int32) for x in (counts, choice, camera))
        + (VMEM(library.shape, library.dtype), VMEM((2, places + 4, 8, 128), F32))
        + (rows, rows, rows, rim),
        in_specs=[anywhere()] * 6,
        out_specs=(in_smem(),) * 3 + (in_vmem(),) * 6,
        scratch_shapes=[pltpu.SemaphoreType.DMA((6,))],
        compiler_params=params(),
        name="pack_rows",
    )(counts, *map(in_hbm, (choice, camera, theta, fuel, library)))


def rim_kernel(body, layers, counts, *arrays):
    return pl.pallas_call(
        body,
        out_shape=VMEM((layers, 8, 128), F32),
        in_specs=[in_smem()] + [in_vmem()] * len(arrays),
        out_specs=in_vmem(),
        compiler_params=params(),
        name=body.__name__,
    )(in_scalars(counts), *map(held, arrays))


def cost(flops):
    return pl.CostEstimate(flops=flops, bytes_accessed=10**6, transcendentals=10**5)


def early_kernel(devices, counts, choice, camera, field0, library, *rows):
    places = field0.shape[1] - 4
    functions = choice.shape[0]
    bins = library.shape[2]
    table = VMEM((4 * functions, 8, bins), F32)
    field = VMEM((places, 8, 128), F32)
    return pl.pallas_call(
        functools.partial(early_step, places, functions, float(MEAN_DEPTH * devices)),
        out_shape=(
            VMEM((2, places + 2, 8, 128), F32),
            VMEM((2, 4, places + 16, 128), F32),
            VMEM((2, 2, places, 128), F32),
            table,
            table,
            field,
            field,
            VMEM((4 * functions, 8, 128), F32),
        ),
        in_specs=[in_smem()] * 3 + [in_vmem()] * 6,
        out_specs=(in_vmem(),) * 8,
        scratch_shapes=[VMEM(library.shape, F32)],
        compiler_params=params(),
        cost_estimate=cost(10**7),
        name="early_step",
    )(*map(in_scalars, (counts, choice, camera)), *map(held, (field0, library, *rows)))


def middle_kernel(counts, *arrays):
    theta_next, fuel_next, sums = arrays[-3:]
    field = jax.ShapeDtypeStruct(theta_next.shape, F32)
    return pl.pallas_call(
        functools.partial(middle_step, theta_next.shape[0]),
        out_shape=(field, field) + tuple(VMEM(x.shape, F32) for x in (theta_next, fuel_next, sums)),
        in_specs=[in_smem()] + [in_vmem()] * len(arrays),
        out_specs=(anywhere(),) * 2 + (in_vmem(),) * 3,
        scratch_shapes=[pltpu.SemaphoreType.DMA((2,))],
        input_output_aliases={len(arrays) - 2 + i: 2 + i for i in range(2)},
        compiler_params=params(),
        cost_estimate=cost(10**7),
        name="middle_step",
    )(in_scalars(counts), *map(held, arrays))


def late_kernel(devices, counts, camera, *arrays):
    functions = camera.shape[0]
    kept = arrays[:4]
    image, ends, *_ = pl.pallas_call(
        functools.partial(late_step, functions),
        out_shape=(VMEM((2 * devices, 128), F32), VMEM((2, 4, 8, 128), F32))
        + tuple(VMEM(x.shape, F32) for x in kept),
        in_specs=[in_smem()] * 2 + [in_vmem()] * len(arrays),
        out_specs=(in_vmem(),) * 6,
        input_output_aliases={2 + i: 2 + i for i in range(4)},
        compiler_params=params(),
        cost_estimate=cost(10**6),
        name="late_step",
    )(*map(in_scalars, (counts, camera)), *map(held, arrays))
    return image, ends


def last_kernel(functions, counts, camera, pieces, ends, *fields):
    field = jax.ShapeDtypeStruct(fields[0].shape, F32)
    image = (functions, 4, 1, 16)
    return pl.pallas_call(
        composite,
        out_shape=(jax.ShapeDtypeStruct(image, F32), field, field),
        in_specs=[in_smem()] * 2 + [in_vmem()] * 2 + [anywhere()] * 2,
        out_specs=(anywhere(),) * 3,
        scratch_shapes=[VMEM(image, F32), pltpu.SemaphoreType.DMA((5,))],
        input_output_aliases={4: 1, 5: 2},
        compiler_params=params(),
        name="composite",
    )(*map(in_scalars, (counts, camera)), *map(held, (pieces, ends)), *map(in_hbm, fields))


def on_device(
    thermal_values,
    reactant_fraction,
    active_sheet_number,
    colour_lookup_library,
    colour_lookup_choice,
    camera_direction,
):
    devices = lax.axis_size("depth")
    counts, choice, camera, library, field0, own_rows, *messages = first_kernel(
        active_sheet_number,
        colour_lookup_choice,
        camera_direction,
        thermal_values,
        reactant_fraction,
        colour_lookup_library,
    )
    rows_pair = swapped(messages[0], "lat", 0)
    rows_gap = swapped(messages[1], "lat", 1)
    rim_pair = swapped(messages[2], "depth", 0)
    order = rim_kernel(pack_gap, 5, counts, field0, rows_pair, rows_gap, rim_pair)
    rim_gap = swapped(order, "depth", 1)
    field1, edge0, edge1, low_table, rise_table, theta_next, fuel_next, sums = early_kernel(
        devices, counts, choice, camera, field0, library, own_rows, rows_pair, rows_gap, order
    )
    order = rim_kernel(pack_next, 3, counts, field0, rows_pair, rows_gap, rim_gap, sums)
    next_pair = swapped(order, "depth", 0)
    theta_next, fuel_next, _, _, sums = middle_kernel(
        counts, field1, edge1, low_table, rise_table, order, theta_next, fuel_next, sums
    )
    pieces, ends = late_kernel(
        devices,
        counts,
        camera,
        field0,
        field1,
        edge0,
        edge1,
        low_table,
        rise_table,
        sums,
        own_rows,
        rim_pair,
        rim_gap,
        next_pair,
    )
    pieces = lax.all_to_all(pieces, "depth", 0, 0, tiled=True)
    image, theta_next, fuel_next = last_kernel(
        choice.shape[0], counts, camera, pieces, ends, theta_next, fuel_next
    )
    return (theta_next, fuel_next, image)


def solution(mesh):
    placed = (P("depth", "lat", None), P("depth", "lat", None), P("depth"), P(), P(), P())
    return jax.shard_map(
        on_device,
        mesh=mesh,
        in_specs=placed,
        out_specs=(P("depth", "lat", None), P("depth", "lat", None), P(None, None, "lat", "depth")),
        check_vma=False,
    )
```

```python
import functools

import jax
import jax.numpy as jnp
from jax import lax
from jax.experimental import pallas as pl
from jax.experimental.pallas import tpu as pltpu
from jax.sharding import PartitionSpec as P

MEAN_DEPTH = 32
STEPS = 2

time_step = 0.03
heat_release = 2.0
zeldovich = 8.0
expansion = 0.8

VMEM = pltpu.VMEM
SMEM = pltpu.SMEM
F32 = jnp.float32


def in_vmem():
    return pl.BlockSpec(memory_space=VMEM)


def in_smem():
    return pl.BlockSpec(memory_space=SMEM)


UNROLL_1 = 16
WINDOWS = ((0, 12), (24, 12), (36, 12))


def is_even(axis):
    return lax.rem(lax.axis_index(axis), 2) == 0


def select(which, first, second):
    return jnp.where(which, first, second)


def pack_rows(
    counts_in,
    choice_in,
    camera_in,
    theta,
    fuel,
    library_in,
    counts,
    choice,
    camera,
    library,
    field0,
    own_rows,
    rows_pair,
    rows_gap,
    rim_pair,
    copies,
):
    places = theta.shape[0]
    moves = [
        (counts_in, counts),
        (theta, field0.at[0, pl.ds(2, places)]),
        (fuel, field0.at[1, pl.ds(2, places)]),
        (choice_in, choice),
        (camera_in, camera),
        (library_in, library),
    ]
    fetch = [
        pltpu.make_async_copy(source, target, copies.at[number])
        for number, (source, target) in enumerate(moves)
    ]
    for copy in fetch:
        copy.start()
    lat_even, depth_even = is_even("lat"), is_even("depth")
    for number in range(2):
        fetch[1 + number].wait()
        for row in range(2):
            low = field0[number, 2 : places + 2, row, :]
            high = field0[number, 2 : places + 2, 6 + row, :]
            rows_pair[2 * number + row] = select(lat_even, high, low)
            rows_gap[2 * number + row] = select(lat_even, low, high)
            own_rows[2 * row + number] = (low, high)[row]
    fetch[0].wait()
    depth_count = counts[0]
    last = depth_count + 1
    second_last = jnp.maximum(depth_count, 2)
    second = jnp.minimum(3, last)
    size = jnp.broadcast_to(depth_count.astype(F32), (8, 128))
    for number in range(2):
        up = (field0[number, last], field0[number, second_last], size)
        down = (field0[number, 2], field0[number, second], size)
        for layer in range(3):
            rim_pair[number, layer] = select(depth_even, up[layer], down[layer])
    for copy in fetch[3:]:
        copy.wait()


def beside(rows_pair, rows_gap, number, place):
    lat_even = is_even("lat")
    below = [ref[2 * number + 1, pl.ds(place, 1), :] for ref in (rows_gap, rows_pair)]
    above = [ref[2 * number, pl.ds(place, 1), :] for ref in (rows_pair, rows_gap)]
    rows = (select(lat_even, *below), select(lat_even, *above))
    return tuple(jnp.broadcast_to(x, (8, 128)) for x in rows)


def pack_gap(counts, field0, rows_pair, rows_gap, rim_pair, order, rim_gap):
    depth_count = counts[0]
    depth_even = is_even("depth")
    end = jnp.where(depth_even, 0, depth_count - 1)
    inward = jnp.where(depth_even, 1, jnp.maximum(depth_count - 2, 0))
    size = depth_count.astype(F32)
    row = sublanes()
    for number in range(2):
        rim_gap[number, 0] = field0[number, 2 + end]
        rim_gap[number, 1] = select(
            depth_count == 1, rim_pair[number, 0], field0[number, 2 + inward]
        )
        below, above = beside(rows_pair, rows_gap, number, end)
        rim_gap[number, 2] = jnp.where(row == 0, below, jnp.where(row == 1, above, size))


def pack_next(counts, rows_pair, rows_gap, rim_gap, order, next_pair):
    end = jnp.where(is_even("depth"), counts[0] - 1, 0)
    for number in range(2):
        next_pair[number, 0] = rim_gap[number, 0]
        below, above = beside(rows_pair, rows_gap, number, end)
        next_pair[number, 1] = jnp.where(sublanes() == 0, below, above)


def lanes():
    return lax.broadcasted_iota(jnp.int32, (8, 128), 1)


def sublanes():
    return lax.broadcasted_iota(jnp.int32, (8, 128), 0)


def left_of(x):
    return jnp.where(lanes() == 0, 0.0, pltpu.roll(x, 1, 1))


def right_of(x):
    return jnp.where(lanes() == 127, 0.0, pltpu.roll(x, 127, 1))


def row_below(x, halo_row):
    return jnp.where(sublanes() == 0, jnp.broadcast_to(halo_row, (8, 128)), pltpu.roll(x, 1, 0))


def row_above(x, halo_row):
    return jnp.where(sublanes() == 7, jnp.broadcast_to(halo_row, (8, 128)), pltpu.roll(x, 7, 0))


def stepped(heat, fuel, neighbours):
    heat_sum = neighbours[0][0]
    fuel_sum = neighbours[0][1]
    product_sum = neighbours[0][0] * neighbours[0][1]
    square_sum = neighbours[0][0] * neighbours[0][0]
    for heat_n, fuel_n in neighbours[1:]:
        heat_sum = heat_sum + heat_n
        fuel_sum = fuel_sum + fuel_n
        product_sum = product_sum + heat_n * fuel_n
        square_sum = square_sum + heat_n * heat_n
    heat_flux = (heat_sum - 6.0 * heat) + 1.5 * (square_sum - 6.0 * (heat * heat))
    fuel_flux = 0.5 * (
        (1.0 + 1.5 * heat) * (fuel_sum - 6.0 * fuel) + 1.5 * (product_sum - fuel * heat_sum)
    )
    ratio = zeldovich / expansion
    reaction = fuel * jnp.exp(ratio - ratio / ((1.0 - expansion) + expansion * heat))
    return (
        heat + time_step * (heat_flux + heat_release * reaction),
        fuel + time_step * (fuel_flux - reaction),
    )


LEAD = 8


def block_step(field, at, count, edge_rows):
    heat = [field[0, at - 1 + j] for j in range(count + 2)]
    burn = [field[1, at - 1 + j] for j in range(count + 2)]
    results = []
    for j in range(1, count + 1):
        h, b = heat[j], burn[j]
        (h_low, b_low), (h_high, b_high) = edge_rows(j - 1)
        around = [
            (heat[j - 1], burn[j - 1]),
            (heat[j + 1], burn[j + 1]),
            (row_below(h, h_low), row_below(b, b_low)),
            (row_above(h, h_high), row_above(b, b_high)),
            (left_of(h), left_of(b)),
            (right_of(h), right_of(b)),
        ]
        results.append(stepped(h, b, around))
    return results


def rows_beside(edge, sides, place):
    return [tuple(edge[n, side, pl.ds(place, 1), :] for n in range(2)) for side in sides]


def step_edges(edge0, inner, side, at, inner_at, count):
    edge_row = 1 + side
    outer_row = 3 * side

    def rows(ref, row, place):
        found = tuple(ref(n)[row(n), pl.ds(place, count), :] for n in range(2))
        return tuple(jnp.broadcast_to(x, (8, 128)) for x in found)

    def edge(row, shift):
        return rows(lambda n: edge0.at[n], lambda n: row, at + shift)

    heat, burn = edge(edge_row, 0)
    around = [
        edge(edge_row, -1),
        edge(edge_row, 1),
        edge(outer_row, 0),
        rows(lambda n: inner, lambda n: 2 * side + n, inner_at),
        (left_of(heat), left_of(burn)),
        (right_of(heat), right_of(burn)),
    ]
    outside = lax.axis_index("lat") == (0 if side == 0 else lax.axis_size("lat") - 1)
    return [jnp.where(outside, 0.0, x) for x in stepped(heat, burn, around)]


def look_up(low_table, rise_table, value):
    bins = low_table.shape[2]
    position = jnp.clip(value, 0.0, 1.0) * (bins - 1)
    lower = jnp.minimum(position.astype(jnp.int32), bins - 2)
    fraction = position - lower.astype(F32)

    def at(entry):
        low = jnp.take_along_axis(low_table[entry], lower, axis=1)
        rise = jnp.take_along_axis(rise_table[entry], lower, axis=1)
        return low + fraction * rise

    return at


def add_layer(sums, number, at, alive):
    for f in range(2 * number, 2 * number + 2):
        gone, red, green, blue = sums[4 * f : 4 * f + 4]
        depth = jnp.where(alive, at(4 * f + 3), 0.0)
        gain = depth * (1.0 + depth * (0.5 + depth * (1.0 / 6.0)))
        gain = gain + gone * gain
        sums[4 * f] = gone + gain
        sums[4 * f + 1] = red + gain * at(4 * f)
        sums[4 * f + 2] = green + gain * at(4 * f + 1)
        sums[4 * f + 3] = blue + gain * at(4 * f + 2)


def inner_layers(
    first, count, unroll, depth_count, field1, edge1, tables, results, sums, after=None
):
    def body(block, carry):
        start = first + block * unroll

        def edge_rows(j):
            return rows_beside(edge1, (0, 1), start + j)

        carry = list(carry)
        for j, new in enumerate(block_step(field1, start + 1, unroll, edge_rows)):
            for number in range(2):
                value = jnp.where(start + j < depth_count, new[number], 0.0)
                results[number][start + j] = value
                add_layer(carry, number, look_up(*tables, value), start + j < depth_count - 2)
        if after is not None:
            after(start, unroll)
        return tuple(carry)

    return lax.fori_loop(0, count // unroll, body, tuple(sums))


def early_step(
    places,
    functions,
    all_layers,
    counts,
    choice,
    camera,
    field0,
    library,
    own_rows,
    rows_pair,
    rows_gap,
    field1,
    edge0,
    edge1,
    low_table,
    rise_table,
    theta_next,
    fuel_next,
    sums,
    tables,
):
    lat_even = is_even("lat")
    bins = library.shape[2]
    tables[...] = library[...].astype(F32)
    per_cell = 3.0 / all_layers
    for f in range(functions):
        sign = jnp.where(camera[f] == 0, -per_cell, per_cell)
        for c in range(4):
            low = jnp.broadcast_to(tables[choice[f], c : c + 1, :], (8, bins))
            rise = pltpu.roll(low, bins - 1, 1) - low
            if c == 3:
                low = low * sign
                rise = rise * sign
            low_table[4 * f + c] = low
            rise_table[4 * f + c] = rise

    for number in range(2):
        for row in range(2):
            pair, gap = rows_pair[2 * number + row], rows_gap[2 * number + row]
            edge0[number, row, LEAD : LEAD + places] = select(lat_even, gap, pair)
            edge0[number, 2 + row, LEAD : LEAD + places] = select(lat_even, pair, gap)

    for block in range(places // 8):
        for side in range(2):
            fresh = step_edges(edge0, own_rows, side, LEAD + 8 * block, 8 * block, 8)
            for number in range(2):
                edge1[number, side, 8 * block : 8 * block + 8] = fresh[number]

    def first_step(block, carry):
        start = block * UNROLL_1

        def edge_rows(j):
            return rows_beside(edge0, (1, 2), LEAD + start + j)

        for j, new in enumerate(block_step(field0, start + 2, UNROLL_1, edge_rows)):
            for number in range(2):
                field1[number, start + 1 + j] = new[number]
        return carry

    lax.fori_loop(0, places // UNROLL_1, first_step, 0)
    zero = jnp.zeros((8, 128), F32)
    for out in (theta_next, fuel_next):
        for place in (0, 1, places - 2, places - 1):
            out[place] = zero
    found = inner_layers(
        2,
        *WINDOWS[0],
        counts[0],
        field1,
        edge1,
        (low_table, rise_table),
        (theta_next, fuel_next),
        [zero] * (4 * functions),
    )
    for entry, value in enumerate(found):
        sums[entry] = value


def middle_step(
    places,
    window,
    counts,
    field1,
    edge1,
    low_table,
    rise_table,
    order,
    theta_in,
    fuel_in,
    sums_in,
    *outs,
):
    last = window == len(WINDOWS) - 1
    if last:
        theta_out, fuel_out, theta_next, fuel_next, sums, copies = outs
    else:
        theta_next, fuel_next, sums = outs

    def leave(number, first, count):
        return pltpu.make_async_copy(
            (theta_next, fuel_next)[number].at[pl.ds(first, count)],
            (theta_out, fuel_out)[number].at[pl.ds(first, count)],
            copies.at[number],
        )

    def start_leaving(first, count):
        for number in range(2):
            leave(number, first, count).start()

    first = 2 + sum(layers for layers, unroll in WINDOWS[:window])
    if last:
        start_leaving(0, first)
        start_leaving(places - 2, 2)
    found = inner_layers(
        first,
        *WINDOWS[window],
        counts[0],
        field1,
        edge1,
        (low_table, rise_table),
        (theta_next, fuel_next),
        [sums_in[entry] for entry in range(sums_in.shape[0])],
        start_leaving if last else None,
    )
    for entry, value in enumerate(found):
        sums[entry] = value
    if last:
        for number in range(2):
            leave(number, 0, places).wait()


def late_step(
    functions,
    counts,
    camera,
    field0_in,
    field1_in,
    edge0_in,
    edge1_in,
    low_table,
    rise_table,
    sums,
    own_rows,
    rim_pair,
    rim_gap,
    next_pair,
    image,
    ends,
    field0,
    field1,
    edge0,
    edge1,
):
    depth_count = counts[0]
    depth_even = is_even("depth")

    def sides(pair, gap):
        return select(depth_even, gap, pair), select(depth_even, pair, gap)

    pair_size = rim_pair[0, 2]
    gap_size = jnp.broadcast_to(rim_gap[0, 2, 2:3], (8, 128))
    below_size, above_size = sides(pair_size, gap_size)
    for number in range(2):
        nearest = sides(rim_pair[number, 0], rim_gap[number, 0])
        second = jnp.where(pair_size == 1.0, next_pair[number, 0], rim_pair[number, 1])
        second = sides(second, rim_gap[number, 1])
        rows = sides(next_pair[number, 1], rim_gap[number, 2])
        field0[number, 0] = second[0]
        field0[number, 1] = nearest[0]
        field0[number, depth_count + 2] = nearest[1]
        field0[number, depth_count + 3] = second[1]
        for side in range(2):
            edge0[number, 1 + side, LEAD - 1 : LEAD] = rows[0][side : side + 1]
            edge0[number, 1 + side, pl.ds(LEAD + depth_count, 1)] = rows[1][side : side + 1]
    for place in (0, depth_count - 1):
        for side in range(2):
            fresh = step_edges(edge0, own_rows, side, LEAD + place, place, 1)
            for number in range(2):
                edge1[number, side, pl.ds(place, 1)] = fresh[number][0:1]
    for place, size in (
        (-1, below_size),
        (0, None),
        (depth_count - 1, None),
        (depth_count, above_size),
    ):

        def edge_rows(j, place=place):
            return rows_beside(edge0, (1, 2), LEAD + place)

        (fresh,) = block_step(field0, place + 2, 1, edge_rows)
        for number in range(2):
            value = fresh[number]
            field1[number, place + 1] = (
                value if size is None else jnp.where(size > 0.0, value, 0.0)
            )

    zero = jnp.zeros((8, 128), F32)
    pairs = ((0, 0), (2, jnp.maximum(depth_count - 2, 2)))
    stepped_ends = []
    for slot, start in pairs:

        def edge_rows(j, start=start):
            return rows_beside(edge1, (0, 1), start + j)

        fresh = block_step(field1, start + 1, 2, edge_rows)
        alive = [start + j < depth_count for j in range(2)]
        fresh = [[jnp.where(alive[j], value, 0.0) for value in fresh[j]] for j in range(2)]
        stepped_ends.append((alive, fresh))
        for number in range(2):
            for j in range(2):
                ends[number, slot + j] = fresh[j][number]
    segments = []
    for alive, fresh in stepped_ends:
        segment = [zero] * (4 * functions)
        for j in range(2):
            for number in range(2):
                at = look_up(low_table, rise_table, fresh[j][number])
                add_layer(segment, number, at, alive[j])
        segments.append(segment)

    head, tail = segments
    channels = []
    for f in range(functions):
        through_head = 1.0 + head[4 * f]
        through_body = 1.0 + sums[4 * f]
        gone, red, green, blue = [
            head[4 * f + c]
            + through_head * (sums[4 * f + c] + through_body * tail[4 * f + c])
            for c in range(4)
        ]
        scale = jnp.where(camera[f] == 0, -1.0, 1.0 / (1.0 + gone))
        channels += [red * scale, green * scale, blue * scale, gone * scale]

    group = lanes() // 16
    for half in range(2):
        regs = channels[8 * half : 8 * half + 8]
        for bit in (1, 2, 4):
            upper = (group & bit) != 0
            fresh = list(regs)
            for i in range(8):
                if i & bit:
                    continue
                a, b = regs[i], regs[i | bit]
                fresh[i] = jnp.where(upper, pltpu.roll(b, 16 * bit, 1), a)
                fresh[i | bit] = jnp.where(upper, b, pltpu.roll(a, 128 - 16 * bit, 1))
            regs = fresh
        for g in range(8):
            image[pl.ds(2 * g + half, 8, stride=16), :] = regs[g]


def composite(
    counts, camera, pieces, ends, theta_in, fuel_in, image_out, theta_next, fuel_next, image, copies
):
    sources = pieces.shape[0] // 2
    leave = [
        pltpu.make_async_copy(
            ends.at[number, pl.ds(slot, 2)],
            out.at[pl.ds(place, 2)],
            copies.at[slot + number],
        )
        for number, out in enumerate((theta_next, fuel_next))
        for slot, place in ((0, 0), (2, jnp.maximum(counts[0] - 2, 2)))
    ]
    for copy in leave:
        copy.start()
    leave.append(pltpu.make_async_copy(image, image_out, copies.at[4]))
    lane = lanes()
    row = sublanes()
    opacity_lane = lane // 64 * 64 + 48 + lane % 16
    for half in range(2):
        forward = jnp.where(
            lane < 64,
            (camera[2 * half] == 0).astype(jnp.int32),
            (camera[2 * half + 1] == 0).astype(jnp.int32),
        ) == 1
        values, clear, through = [], [], []
        carry = jnp.ones((8, 128), F32)
        for block in range(sources // 8):
            value = pieces[pl.ds(16 * block + half, 8, stride=2), :]
            passing = 1.0 - jnp.take_along_axis(value, opacity_lane, axis=1)
            product = passing
            for shift in (1, 2, 4):
                product = product * jnp.where(row >= shift, pltpu.roll(product, shift, 0), 1.0)
            product = product * carry
            carry = jnp.broadcast_to(product[7:8], (8, 128))
            values.append(value)
            clear.append(passing)
            through.append(product)
        total = jnp.zeros((8, 128), F32)
        for value, passing, product in zip(values, clear, through):
            top = jnp.where(forward, product, carry)
            bottom = jnp.where(forward, passing, product)
            total = total + value * (top / bottom)
        line = jnp.sum(total, axis=0, keepdims=True)
        for clo in range(8):
            channel = 8 * half + clo
            image[channel // 4, channel % 4] = line[:, 16 * clo : 16 * clo + 16]
    leave[-1].start()
    for copy in leave:
        copy.wait()


def swapped(array, axis, first):
    count = lax.axis_size(axis)
    pairs = []
    for i in range(first, count - 1, 2):
        pairs += [(i, i + 1), (i + 1, i)]
    return lax.ppermute(array, axis, pairs)


def held(array):
    return pltpu.with_memory_space_constraint(array, VMEM)


def in_hbm(array):
    return pltpu.with_memory_space_constraint(array, pltpu.HBM)


def params():
    return pltpu.CompilerParams(vmem_limit_bytes=16 * 1024 * 1024)


def anywhere():
    return pl.BlockSpec(memory_space=pl.ANY)


def in_scalars(array):
    return pltpu.with_memory_space_constraint(array, SMEM)


def first_kernel(counts, choice, camera, theta, fuel, library):
    places = theta.shape[0]
    rows = VMEM((4, places, 128), F32)
    rim = VMEM((2, 3, 8, 128), F32)
    return pl.pallas_call(
        pack_rows,
        out_shape=tuple(SMEM(x.shape, jnp.int32) for x in (counts, choice, camera))
        + (VMEM(library.shape, library.dtype), VMEM((2, places + 4, 8, 128), F32))
        + (rows, rows, rows, rim),
        in_specs=[anywhere()] * 6,
        out_specs=(in_smem(),) * 3 + (in_vmem(),) * 6,
        scratch_shapes=[pltpu.SemaphoreType.DMA((6,))],
        compiler_params=params(),
        name="pack_rows",
    )(counts, *map(in_hbm, (choice, camera, theta, fuel, library)))


def rim_kernel(body, layers, counts, *arrays):
    return pl.pallas_call(
        body,
        out_shape=VMEM((2, layers, 8, 128), F32),
        in_specs=[in_smem()] + [in_vmem()] * len(arrays),
        out_specs=in_vmem(),
        compiler_params=params(),
        name=body.__name__,
    )(in_scalars(counts), *map(held, arrays))


def cost(flops):
    return pl.CostEstimate(flops=flops, bytes_accessed=10**6, transcendentals=10**5)


def early_kernel(devices, counts, choice, camera, field0, library, *rows):
    places = field0.shape[1] - 4
    functions = choice.shape[0]
    bins = library.shape[2]
    table = VMEM((4 * functions, 8, bins), F32)
    field = VMEM((places, 8, 128), F32)
    return pl.pallas_call(
        functools.partial(early_step, places, functions, float(MEAN_DEPTH * devices)),
        out_shape=(
            VMEM((2, places + 2, 8, 128), F32),
            VMEM((2, 4, places + 16, 128), F32),
            VMEM((2, 2, places, 128), F32),
            table,
            table,
            field,
            field,
            VMEM((4 * functions, 8, 128), F32),
        ),
        in_specs=[in_smem()] * 3 + [in_vmem()] * 5,
        out_specs=(in_vmem(),) * 8,
        scratch_shapes=[VMEM(library.shape, F32)],
        compiler_params=params(),
        cost_estimate=cost(10**7),
        name="early_step",
    )(*map(in_scalars, (counts, choice, camera)), *map(held, (field0, library, *rows)))


def middle_kernel(window, counts, *arrays):
    theta_next, fuel_next, sums = arrays[-3:]
    field = jax.ShapeDtypeStruct(theta_next.shape, F32)
    last = window == len(WINDOWS) - 1
    lead = 2 if last else 0
    return pl.pallas_call(
        functools.partial(middle_step, theta_next.shape[0], window),
        out_shape=(field,) * lead + tuple(VMEM(x.shape, F32) for x in (theta_next, fuel_next, sums)),
        in_specs=[in_smem()] + [in_vmem()] * len(arrays),
        out_specs=(anywhere(),) * lead + (in_vmem(),) * 3,
        scratch_shapes=[pltpu.SemaphoreType.DMA((2,))] if last else [],
        input_output_aliases={len(arrays) - 2 + i: lead + i for i in range(2)},
        compiler_params=params(),
        cost_estimate=cost(10**7),
        name="middle_step",
    )(in_scalars(counts), *map(held, arrays))


def late_kernel(devices, counts, camera, *arrays):
    functions = camera.shape[0]
    kept = arrays[:4]
    image, ends, *_ = pl.pallas_call(
        functools.partial(late_step, functions),
        out_shape=(VMEM((2 * devices, 128), F32), VMEM((2, 4, 8, 128), F32))
        + tuple(VMEM(x.shape, F32) for x in kept),
        in_specs=[in_smem()] * 2 + [in_vmem()] * len(arrays),
        out_specs=(in_vmem(),) * 6,
        input_output_aliases={2 + i: 2 + i for i in range(4)},
        compiler_params=params(),
        cost_estimate=cost(10**6),
        name="late_step",
    )(*map(in_scalars, (counts, camera)), *map(held, arrays))
    return image, ends


def last_kernel(functions, counts, camera, pieces, ends, *fields):
    field = jax.ShapeDtypeStruct(fields[0].shape, F32)
    image = (functions, 4, 1, 16)
    return pl.pallas_call(
        composite,
        out_shape=(jax.ShapeDtypeStruct(image, F32), field, field),
        in_specs=[in_smem()] * 2 + [in_vmem()] * 2 + [anywhere()] * 2,
        out_specs=(anywhere(),) * 3,
        scratch_shapes=[VMEM(image, F32), pltpu.SemaphoreType.DMA((5,))],
        input_output_aliases={4: 1, 5: 2},
        compiler_params=params(),
        name="composite",
    )(*map(in_scalars, (counts, camera)), *map(held, (pieces, ends)), *map(in_hbm, fields))


def on_device(
    thermal_values,
    reactant_fraction,
    active_sheet_number,
    colour_lookup_library,
    colour_lookup_choice,
    camera_direction,
):
    devices = lax.axis_size("depth")
    counts, choice, camera, library, field0, own_rows, *messages = first_kernel(
        active_sheet_number,
        colour_lookup_choice,
        camera_direction,
        thermal_values,
        reactant_fraction,
        colour_lookup_library,
    )
    rows_pair = swapped(messages[0], "lat", 0)
    rows_gap = swapped(messages[1], "lat", 1)
    rim_pair = swapped(messages[2], "depth", 0)
    field1, edge0, edge1, low_table, rise_table, theta_next, fuel_next, sums = early_kernel(
        devices, counts, choice, camera, field0, library, own_rows, rows_pair, rows_gap
    )
    order = rim_kernel(pack_gap, 3, counts, field0, rows_pair, rows_gap, rim_pair, sums)
    rim_gap = swapped(order, "depth", 1)
    theta_next, fuel_next, sums = middle_kernel(
        1, counts, field1, edge1, low_table, rise_table, order, theta_next, fuel_next, sums
    )
    order = rim_kernel(pack_next, 2, counts, rows_pair, rows_gap, rim_gap, sums)
    next_pair = swapped(order, "depth", 0)
    theta_next, fuel_next, _, _, sums = middle_kernel(
        2, counts, field1, edge1, low_table, rise_table, order, theta_next, fuel_next, sums
    )
    pieces, ends = late_kernel(
        devices,
        counts,
        camera,
        field0,
        field1,
        edge0,
        edge1,
        low_table,
        rise_table,
        sums,
        own_rows,
        rim_pair,
        rim_gap,
        next_pair,
    )
    pieces = lax.all_to_all(pieces, "depth", 0, 0, tiled=True)
    image, theta_next, fuel_next = last_kernel(
        choice.shape[0], counts, camera, pieces, ends, theta_next, fuel_next
    )
    return (theta_next, fuel_next, image)


def solution(mesh):
    placed = (P("depth", "lat", None), P("depth", "lat", None), P("depth"), P(), P(), P())
    return jax.shard_map(
        on_device,
        mesh=mesh,
        in_specs=placed,
        out_specs=(P("depth", "lat", None), P("depth", "lat", None), P(None, None, "lat", "depth")),
        check_vma=False,
    )
```
